128 devices in a mesh: gx: 8 (over x, y_lo), gy: 16 (over y_hi, z, core).
Axes of the slice: x: 4, y: 4 (y_hi: 2, y_lo: 2; y = y_hi * 2 + y_lo), z: 4, core: 2. Of those that a mesh axis runs over, the one named last changes fastest.
Arguments:
- hidden: bfloat16 [16384, 2048], P('gx', 'gy'), may hold values from -6 to 6
- attn_gain: float32 [2048], P('gy'), may hold values from 0.5 to 1.5
- query_weight: bfloat16 [2048, 2048], P('gx', 'gy'), may hold values from -0.4375 to 0.4375
- key_matrix: bfloat16 [2048, 512], P('gx', 'gy'), may hold values from -0.4375 to 0.4375
- value_matrix: bfloat16 [2048, 512], P('gx', 'gy'), may hold values from -0.125 to 0.125
- output_weight: bfloat16 [2048, 2048], P('gy', 'gx'), may hold values from -3 to 3
- ffn_gain: float32 [2048], P('gy'), may hold values from 0.5 to 1.5
- gate_weight: bfloat16 [2048, 8192], P('gx', 'gy'), may hold values from -0.125 to 0.125
- up_weight: bfloat16 [2048, 8192], P('gx', 'gy'), may hold values from -0.125 to 0.125
- down_weight: bfloat16 [8192, 2048], P('gy', 'gx'), may hold values from -0.5 to 0.5
- segments: int32 [16, 1024], P('gx'), may hold values from 0 to 3, never falling along the last dimension, each value on 1 to 512 neighbouring positions
- cotangent: bfloat16 [16384, 2048], P('gx', 'gy'), may hold values from -6 to 6
Outputs:
- output: float32 [16384, 2048], P('gx', 'gy')
- grad_hidden: float32 [16384, 2048], P('gx', 'gy')
- grad_attngain: float32 [2048], P('gy')
- grad_query: float32 [2048, 2048], P('gx', 'gy')
- grad_key: float32 [2048, 512], P('gx', 'gy')
- grad_value: float32 [2048, 512], P('gx', 'gy')
- grad_outproj: float32 [2048, 2048], P('gy', 'gx')
- grad_ffngain: float32 [2048], P('gy')
- grad_gate: float32 [2048, 8192], P('gx', 'gy')
- grad_up: float32 [2048, 8192], P('gx', 'gy')
- grad_down: float32 [8192, 2048], P('gy', 'gx')
The draws below stay inside these ranges and needn't reach their ends.
Inputs may be any that keep to these rules, and one draw needn't show every extreme that they name: `segments`: within each packed sequence the document numbers never fall from one token to the next; a document has 1 to 512 tokens, and one document in each sequence has exactly 512.
All inputs are finite; a program needn't handle non-finite values.
Results may differ from the reference program's by a relative error of at most 0.02.
Values may be sent and summed in bfloat16 or wider, within the bound.
A program may use at most 192 MiB of HBM per device.

```python
import math
import jax
import jax.numpy as jnp
import numpy as np
from jax import lax

MODEL_DIM = 2048
QUERY_HEADS = 32
KEY_VALUE_HEADS = 8
HEAD_SIZE = 64
FF = 8192
PACKED_LENGTH = 1024
NSEQ = 16
TOKENS = 16384


def block_scale(rng, extent, shards, low, largest):
    gain = 1.0
    for dim, blocks in shards:
        heights = jax.random.uniform(jax.random.fold_in(jax.random.fold_in(rng, 6), dim), (blocks,), jnp.float32, low / len(shards), largest / len(shards))
        gain = gain * jnp.repeat(jnp.exp(heights), extent[dim] // blocks).reshape((-1,) + (1,) * (len(extent) - 1 - dim))
    return gain


def length_profile(number_of, total, bound, slope):
    weights = [(1 << 20) // math.isqrt(rank ** slope) + 1 for rank in range(2, number_of + 1)]
    surplus, holding = total - bound - (number_of - 1), [1] * (number_of - 1)
    while surplus > 0:
        candidates = [i for i in range(number_of - 1) if holding[i] < bound]
        mass, remaining = sum([weights[i] for i in candidates]), surplus
        for i in candidates:
            more = min(bound - holding[i], max(1, remaining * weights[i] // mass), surplus)
            holding[i] = holding[i] + more
            surplus = surplus - more
    return np.array([bound] + holding)


def uneven(stream_key, amount, total, limit, skew):
    if amount == 2:
        one = jax.random.randint(stream_key, (), max(1, total - limit), min(limit, total - 1) + 1)
        return jnp.stack([one, total - one])
    lengths = jnp.asarray(length_profile(amount, total, limit, skew), jnp.int32)
    couples = (amount - 1) // 2
    donor, receiver = lengths[1:1 + 2 * couples:2], lengths[2:2 + 2 * couples:2]
    room = jnp.minimum(donor - 1, limit - receiver)
    shifted = jax.random.randint(jax.random.fold_in(stream_key, 1), (couples,), 0, 1 << 20) % (room + 1)
    lengths = lengths.at[1:1 + 2 * couples:2].set(donor - shifted).at[2:2 + 2 * couples:2].set(receiver + shifted)
    return lengths[jax.random.permutation(jax.random.fold_in(stream_key, 2), amount)]


def noise(key, dims, scale, bound, shards=(), kind=jnp.bfloat16):
    values = scale * jax.random.normal(key, dims, jnp.float32)
    if shards:
        values = values * block_scale(key, dims, shards, -0.22, 0.18)
    return jnp.clip(values, -bound, bound).astype(kind)


def setup_inputs(seed: int = 0) -> dict:
    key_list = jax.random.split(jax.random.key(seed), 13)
    return {
        "hidden": noise(key_list[0], (TOKENS, MODEL_DIM), 1.0, 6.0, ((0, 8), (1, 16))),
        "attn_gain": jnp.clip(1.0 + 0.1 * jax.random.normal(key_list[1], (MODEL_DIM,), jnp.float32), 0.5, 1.5),
        "query_weight": noise(key_list[2], (MODEL_DIM, QUERY_HEADS * HEAD_SIZE), (MODEL_DIM // 12) ** -0.5, 0.4375, ((0, 8), (1, 16))),
        "key_matrix": noise(key_list[3], (MODEL_DIM, KEY_VALUE_HEADS * HEAD_SIZE), (MODEL_DIM // 12) ** -0.5, 0.4375, ((0, 8), (1, 16))),
        "value_matrix": noise(key_list[4], (MODEL_DIM, KEY_VALUE_HEADS * HEAD_SIZE), MODEL_DIM ** -0.5, 0.125, ((0, 8), (1, 16))),
        "output_weight": noise(key_list[5], (QUERY_HEADS * HEAD_SIZE, MODEL_DIM), (max(1, QUERY_HEADS * HEAD_SIZE // 512)) ** -0.5, 3.0, ((0, 16), (1, 8))),
        "ffn_gain": jnp.clip(1.0 + 0.1 * jax.random.normal(key_list[6], (MODEL_DIM,), jnp.float32), 0.5, 1.5),
        "gate_weight": noise(key_list[7], (MODEL_DIM, FF), MODEL_DIM ** -0.5, 0.125, ((0, 8), (1, 16))),
        "up_weight": noise(key_list[8], (MODEL_DIM, FF), MODEL_DIM ** -0.5, 0.125, ((0, 8), (1, 16))),
        "down_weight": noise(key_list[9], (FF, MODEL_DIM), (FF // 64) ** -0.5, 0.5, ((0, 16), (1, 8))),
        "segments": jax.vmap(lambda own: jnp.searchsorted(jnp.cumsum(uneven(own, 4, PACKED_LENGTH, PACKED_LENGTH // 2, 0)), jnp.arange(PACKED_LENGTH), side="right"))(jax.random.split(key_list[10], NSEQ)).reshape((NSEQ, PACKED_LENGTH)).astype(jnp.int32),
        "cotangent": noise(key_list[11], (TOKENS, MODEL_DIM), 1.0, 6.0, ((0, 8), (1, 16))),
    }


epsilon = 1e-06
rope_base = 10000000.0
attn_scale = 1.0 / 64.0
res_scale = 0.22
highest = lax.Precision.HIGHEST

@jax.custom_vjp
def lower_half(v):
    return lax.optimization_barrier(v.astype(jnp.bfloat16)).astype(jnp.float32)

@jax.custom_vjp
def low_back(v):
    return v

def low_keep(v):
    return (lower_half(v), None)

def low_pass(kept, grad):
    return (grad,)

def back_keep(v):
    return (v, None)

def back_low(kept, grad):
    return (lower_half(grad),)
lower_half.defvjp(low_keep, low_pass)
low_back.defvjp(back_keep, back_low)

def matmul_high(left_side, right_side):
    return jnp.dot(left_side, right_side, precision=highest, preferred_element_type=jnp.float32)

def rms_norm(stream, gain_vector):
    inverse = lax.rsqrt(lax.optimization_barrier(jnp.mean(stream * stream, axis=-1, keepdims=True)) + epsilon)
    return stream * inverse * gain_vector

def rope_tables(segment_rows, head_dim):
    token_index = jnp.broadcast_to(jnp.arange(segment_rows.shape[1], dtype=jnp.int32), segment_rows.shape)
    boundary = jnp.concatenate([jnp.ones((segment_rows.shape[0], 1), jnp.bool_), segment_rows[:, 1:] != segment_rows[:, :-1]], axis=1)
    starts = lax.cummax(jnp.where(boundary, token_index, 0), axis=1)
    places = (token_index - starts).astype(jnp.float32)
    frequency = rope_base ** (-jnp.arange(0, head_dim, 2, dtype=jnp.float32) / head_dim)
    turned = places[..., None] * frequency
    return (jnp.cos(turned), jnp.sin(turned))

def apply_rotary(vectors, cosine_table, sine_table):
    half_dim = vectors.shape[-1] // 2
    front_half = vectors[..., :half_dim]
    back_half = vectors[..., half_dim:]
    return jnp.concatenate([front_half * cosine_table - back_half * sine_table, back_half * cosine_table + front_half * sine_table], axis=-1)

def attend(queries, key_head_rows, value_head_rows, segment):
    heads_per_group = QUERY_HEADS // KEY_VALUE_HEADS
    keys_all = jnp.repeat(key_head_rows, heads_per_group, axis=1)
    values_all = jnp.repeat(value_head_rows, heads_per_group, axis=1)
    length = queries.shape[0]
    block_span = min(512, length)
    positions_all = jnp.arange(length, dtype=jnp.int32)

    def one_block(block_index):
        row_start = (block_index * block_span).astype(jnp.int32)
        block_query = lax.dynamic_slice_in_dim(queries, row_start, block_span, 0)
        block_segment = lax.dynamic_slice_in_dim(segment, row_start, block_span, 0)
        block_positions = row_start + jnp.arange(block_span, dtype=jnp.int32)
        raw_scores = jnp.einsum('qhd,khd->hqk', block_query, keys_all, precision=highest)
        scores = low_back(raw_scores * attn_scale)
        visible_keys = (block_segment[:, None] == segment[None, :]) & (block_positions[:, None] >= positions_all[None, :])
        scores = jnp.where(visible_keys[None], scores, -1e+30)
        probabilities = jax.nn.softmax(scores, axis=-1)
        return jnp.einsum('hqk,khd->qhd', lower_half(probabilities), values_all, precision=highest)
    blocks = lax.map(jax.checkpoint(one_block), jnp.arange(length // block_span, dtype=jnp.int32))
    return blocks.reshape(length, QUERY_HEADS, HEAD_SIZE)

def decoder_layer(stream, segment_groups, attn_gain, query_weight, key_matrix, value_matrix, output_weight, ffn_gain, gate_weight, up_weight, down_weight):
    groups_number = segment_groups.shape[0]
    normed_one = lower_half(rms_norm(stream, attn_gain))
    query_lin = low_back(matmul_high(normed_one, query_weight))
    key_linear = low_back(matmul_high(normed_one, key_matrix))
    value_linear = low_back(matmul_high(normed_one, value_matrix))
    cosine_table, sine_table = rope_tables(segment_groups, HEAD_SIZE)
    cosine_table = cosine_table[:, :, None, :]
    sine_table = sine_table[:, :, None, :]
    queries = lower_half(apply_rotary(query_lin.reshape(groups_number, PACKED_LENGTH, QUERY_HEADS, HEAD_SIZE), cosine_table, sine_table))
    key_head_rows = lower_half(apply_rotary(key_linear.reshape(groups_number, PACKED_LENGTH, KEY_VALUE_HEADS, HEAD_SIZE), cosine_table, sine_table))
    value_head_rows = lower_half(value_linear.reshape(groups_number, PACKED_LENGTH, KEY_VALUE_HEADS, HEAD_SIZE))
    attended = lax.map(lambda packed: attend(packed[0], packed[1], packed[2], packed[3]), (queries, key_head_rows, value_head_rows, segment_groups))
    heads_out = low_back(lower_half(attended.reshape(stream.shape[0], QUERY_HEADS * HEAD_SIZE)))
    attn_out = low_back(matmul_high(heads_out, output_weight))
    after_attn = stream + res_scale * attn_out
    normed_two = lower_half(rms_norm(after_attn, ffn_gain))
    gate_pre = low_back(matmul_high(normed_two, gate_weight))
    up_pre = low_back(matmul_high(normed_two, up_weight))
    hidden_act = low_back(lower_half(jax.nn.silu(gate_pre) * up_pre))
    ffn_out = low_back(matmul_high(hidden_act, down_weight))
    return after_attn + res_scale * ffn_out

def forward_all(stream, attn_gain, query_weight, key_matrix, value_matrix, output_weight, ffn_gain, gate_weight, up_weight, down_weight, segments):
    token_count = stream.shape[0]
    group_seqs = math.gcd(segments.shape[0], max(1, 4096 // PACKED_LENGTH))
    groups = segments.shape[0] // group_seqs
    stream_groups = stream.reshape(groups, group_seqs * PACKED_LENGTH, stream.shape[1])
    segment_groups = segments.reshape(groups, group_seqs, PACKED_LENGTH)

    def group_step(carried, group_item):
        result = decoder_layer(group_item[0], group_item[1], attn_gain, query_weight, key_matrix, value_matrix, output_weight, ffn_gain, gate_weight, up_weight, down_weight)
        return (carried, result)
    _, results = lax.scan(jax.checkpoint(group_step), jnp.zeros((), jnp.float32), (stream_groups, segment_groups))
    return results.reshape(token_count, stream.shape[1])

def reference(hidden, attn_gain, query_weight, key_matrix, value_matrix, output_weight, ffn_gain, gate_weight, up_weight, down_weight, segments, cotangent):
    floats = jax.tree.map(lambda array_in: array_in.astype(jnp.float32), (hidden, attn_gain, query_weight, key_matrix, value_matrix, output_weight, ffn_gain, gate_weight, up_weight, down_weight))

    def forward(stream, gain_one, weight_query, weight_key, weight_value, weight_output, gain_two, weight_gate, weight_up, weight_down):
        return forward_all(stream, gain_one, weight_query, weight_key, weight_value, weight_output, gain_two, weight_gate, weight_up, weight_down, segments)
    output, pullback = jax.vjp(forward, *floats)
    gradients = pullback(cotangent.astype(jnp.float32))
    return (output, gradients[0], gradients[1], gradients[2], gradients[3], gradients[4], gradients[5], gradients[6], gradients[7], gradients[8], gradients[9])
```

```python
import functools

import jax
import jax.numpy as jnp
from jax import lax
from jax.experimental import pallas as pl
from jax.experimental.pallas import tpu as pltpu
from jax.sharding import PartitionSpec as P

HEAD = 64
EPS = 1e-06
ROPE_BASE = 10000000.0
ATTN_SCALE = 1.0 / 64.0
RES = 0.22
T = 1024
D = 2048
SLAB = 128
QB = 256
BF = jnp.bfloat16
F32 = jnp.float32
MESH = pl.DeviceIdType.MESH
ANY = pl.BlockSpec(memory_space=pl.ANY)
VM = pl.BlockSpec(memory_space=pltpu.VMEM)


class Place:
    def __init__(self):
        gx = lax.axis_index("gx")
        gy = lax.axis_index("gy")
        self.gx, self.gy = gx, gy
        self.x, self.yl = gx // 2, lax.rem(gx, 2)
        self.yh, self.z, self.c = gy // 8, lax.rem(gy // 2, 4), lax.rem(gy, 2)
        self.y = self.yh * 2 + self.yl
        self.r = self.z * 2 + self.c

    def at(self, x=0, y=0, z=0, c=0):
        xx = lax.rem(self.x + x + 4, 4)
        yy = lax.rem(self.y + y + 4, 4)
        zz = lax.rem(self.z + z + 4, 4)
        cc = lax.rem(self.c + c, 2)
        return (xx * 2 + lax.rem(yy, 2), (yy // 2) * 8 + zz * 2 + cc)

    def step(self, axis, k):
        return self.at(**{axis: k})

    def pos(self, axis, k):
        return lax.rem(getattr(self, axis) + k + 4, 4)


class Wire:
    def __init__(self, place, send, recv):
        self.place, self.send_sem, self.recv_sem = place, send, recv
        self.count = 0
        self.sent = []

    def send(self, src, dst, to):
        i = self.count
        self.count += 1
        cp = pltpu.make_async_remote_copy(
            src_ref=src,
            dst_ref=dst,
            send_sem=self.send_sem.at[i],
            recv_sem=self.recv_sem.at[i],
            device_id=to,
            device_id_type=MESH,
        )
        cp.start()
        self.sent.append(cp)
        return cp

    def copy(self, src, dst):
        i = self.count
        self.count += 1
        cp = pltpu.make_async_copy(src, dst, self.send_sem.at[i])
        cp.start()
        return cp

    def drain(self):
        for cp in self.sent:
            cp.wait_send()
        self.sent = []


def greet(peers):
    barrier = pltpu.get_barrier_semaphore()
    for peer in peers:
        pl.semaphore_signal(barrier, inc=1, device_id=peer, device_id_type=MESH)
    pl.semaphore_wait(barrier, len(peers))


def ring_peers(p):
    return [p.at(x=1), p.at(x=-1), p.at(y=1), p.at(y=-1)]


def row_peers(p):
    out = []
    for y in (0, 2):
        for z in range(4):
            for c in range(2):
                if (y, z, c) != (0, 0, 0):
                    out.append((y, z, c, p.at(y=y, z=z, c=c)))
    return out


def line_peers(p):
    return [p.at(c=1), p.at(z=1), p.at(z=-1)]


class WeightGather:
    def __init__(self, wire, src, dst, start, rows, order):
        self.w, self.src, self.dst = wire, src, dst
        self.r0, self.n, self.order = start, rows, order
        self.a1, self.a2 = ("x", "y") if order == 0 else ("y", "x")

    def one(self, k, half=None):
        p = self.w.place
        x, y = (p.pos("x", k), p.y) if self.a1 == "x" else (p.x, p.pos("y", k))
        return self.dst.at[y // 2, x, lax.rem(y, 2), self.span(half)]

    def four(self, k, half=None):
        p = self.w.place
        if self.a2 == "y":
            y = p.pos("y", k)
            return self.dst.at[y // 2, :, lax.rem(y, 2), self.span(half)]
        return self.dst.at[:, p.pos("x", k), :, self.span(half)]

    def span(self, half):
        if half is None:
            return pl.ds(self.r0, self.n)
        return pl.ds(self.r0 + half * (self.n // 2), self.n // 2)

    def s1(self):
        w, p = self.w, self.w.place
        own = self.src.at[pl.ds(self.r0, self.n)]
        self.local = w.copy(own, self.one(0))
        self.up = w.send(own, self.one(0), p.step(self.a1, 1))
        self.down = w.send(own, self.one(0), p.step(self.a1, -1))

    def s2(self):
        w, p = self.w, self.w.place
        self.up.wait_recv()
        self.up2 = w.send(self.one(-1, 0), self.one(-1, 0), p.step(self.a1, 1))
        self.down.wait_recv()
        self.down2 = w.send(self.one(1, 1), self.one(1, 1), p.step(self.a1, -1))

    def s3(self):
        w, p = self.w, self.w.place
        self.local.wait()
        self.up2.wait_recv()
        self.down2.wait_recv()
        self.up3 = w.send(self.four(0), self.four(0), p.step(self.a2, 1))
        self.down3 = w.send(self.four(0), self.four(0), p.step(self.a2, -1))

    def s4(self):
        w, p = self.w, self.w.place
        self.up3.wait_recv()
        self.up4 = w.send(self.four(-1, 0), self.four(-1, 0), p.step(self.a2, 1))
        self.down3.wait_recv()
        self.down4 = w.send(self.four(1, 1), self.four(1, 1), p.step(self.a2, -1))

    def s5(self):
        self.up4.wait_recv()
        self.down4.wait_recv()


class RowGather:
    def __init__(self, wire, src, dst):
        self.w, self.src, self.dst = wire, src, dst

    def block(self, yh, k, c=None):
        p = self.w.place
        c = p.c if c is None else c
        gy = yh * 8 + p.pos("z", k) * 2 + c
        return self.dst.at[:, pl.ds(pl.multiple_of(gy * 128, 128), 128)]

    def out(self, src, yh, k):
        b = self.block(yh, k)
        self.cores.append(self.w.send(src, b, self.w.place.at(c=1)))

    def s1(self):
        w, p = self.w, self.w.place
        self.cores = []
        mine = self.src.at[pl.ds(pl.multiple_of(p.yh * T, T), T)]
        other = self.src.at[pl.ds(pl.multiple_of((1 - p.yh) * T, T), T)]
        own = self.block(p.yh, 0)
        self.local = w.copy(mine, own)
        self.swap = w.send(other, own, p.at(y=2))
        self.up0 = w.send(mine, own, p.at(z=1))
        self.down0 = w.send(mine, own, p.at(z=-1))
        self.out(mine, p.yh, 0)

    def s2(self):
        w, p = self.w, self.w.place
        self.swap.wait_recv()
        b = self.block(1 - p.yh, 0)
        self.up1 = w.send(b, b, p.at(z=1))
        self.down1 = w.send(b, b, p.at(z=-1))
        self.out(b, 1 - p.yh, 0)

    def s3(self):
        w, p = self.w, self.w.place
        self.up0.wait_recv()
        b = self.block(p.yh, -1)
        self.up2 = w.send(b, b, p.at(z=1))
        self.out(b, p.yh, -1)
        self.down0.wait_recv()
        self.out(self.block(p.yh, 1), p.yh, 1)
        self.down1.wait_recv()
        b = self.block(1 - p.yh, 1)
        self.down2 = w.send(b, b, p.at(z=-1))
        self.out(b, 1 - p.yh, 1)
        self.up1.wait_recv()
        self.out(self.block(1 - p.yh, -1), 1 - p.yh, -1)

    def s4(self):
        p = self.w.place
        self.up2.wait_recv()
        self.out(self.block(p.yh, 2), p.yh, 2)
        self.down2.wait_recv()
        self.out(self.block(1 - p.yh, 2), 1 - p.yh, 2)

    def s5(self):
        self.local.wait()
        for cp in self.cores:
            cp.wait_recv()


def gather_kernel(
    hidden, cot, wq, wo, gate, up, down, gains,
    h_out, c_out, q_out, o_out, g_out, u_out, d_out, gain_out, q_tmp, o_tmp,
    send, recv,
):
    p = Place()
    w = Wire(p, send, recv)
    rows = row_peers(p)
    greet(ring_peers(p) + [dev for _, _, _, dev in rows])
    h = RowGather(w, hidden, h_out)
    c = RowGather(w, cot, c_out)
    aq = WeightGather(w, wq, q_tmp, 0, 256, 0)
    ao = WeightGather(w, wo, o_tmp, 0, 128, 1)
    big = [
        WeightGather(w, gate, g_out, 0, 256, 0),
        WeightGather(w, up, u_out, 0, 256, 1),
        WeightGather(w, down, d_out, 0, 256, 0),
        WeightGather(w, down, d_out, 256, 256, 1),
    ]
    h.s1()
    aq.s1()
    ao.s1()
    own = gain_out.at[p.gy]
    glocal = w.copy(gains, own)
    gcopies = [w.send(gains, own, dev) for _, _, _, dev in rows]
    for b in big:
        b.s1()
    h.s2()
    aq.s2()
    ao.s2()
    h.s3()
    c.s1()
    aq.s3()
    ao.s3()
    c.s2()
    h.s4()
    for b in big:
        b.s2()
    aq.s4()
    ao.s4()
    for b in big:
        b.s3()
    c.s3()
    aq.s5()
    ao.s5()
    swaps = []
    for tmp, out in ((q_tmp, q_out), (o_tmp, o_out)):
        swaps.append(w.send(tmp.at[1 - p.c], out.at[p.c], p.at(c=1)))
    locals_ = [w.copy(q_tmp.at[p.c], q_out.at[p.c]), w.copy(o_tmp.at[p.c], o_out.at[p.c])]
    c.s4()
    h.s5()
    for b in big:
        b.s4()
    c.s5()
    for b in big:
        b.s5()
    for cp in swaps:
        cp.wait_recv()
    for cp in locals_:
        cp.wait()
    glocal.wait()
    for cp in gcopies:
        cp.wait_recv()
    w.drain()


def call_gather(hidden, cot, wq, wo, gate, up, down, gains):
    n = 140
    shapes = [
        ((T, D), BF), ((T, D), BF),
        ((2, 4, 2, 256, 192), BF), ((2, 4, 2, 128, 256), BF),
        ((2, 4, 2, 256, 512), BF), ((2, 4, 2, 256, 512), BF), ((2, 4, 2, 512, 256), BF),
        ((16, 8, 128), F32),
        ((2, 4, 2, 256, 192), BF), ((2, 4, 2, 128, 256), BF),
    ]
    return pl.pallas_call(
        gather_kernel,
        out_shape=[jax.ShapeDtypeStruct(s, d) for s, d in shapes],
        in_specs=[ANY] * 8,
        out_specs=[ANY] * len(shapes),
        scratch_shapes=[pltpu.SemaphoreType.DMA((n,)), pltpu.SemaphoreType.DMA((n,))],
        compiler_params=pltpu.CompilerParams(
            collective_id=0, has_side_effects=True, vmem_limit_bytes=1 << 20
        ),
        name="gather_inputs",
    )(hidden, cot, wq, wo, gate, up, down, gains)[:8]


def add_rows(dst, srcs, rows, step=16):
    def body(i, carry):
        at = pl.ds(pl.multiple_of(i * step, step), step)
        total = srcs[0][at].astype(F32)
        for s in srcs[1:]:
            total = total + s[at].astype(F32)
        dst[at] = total.astype(dst.dtype)
        return carry

    lax.fori_loop(0, rows // step, body, 0)


class LineSum:
    SCRATCH = [
        pltpu.VMEM((4, SLAB, D), BF),
        pltpu.VMEM((4, SLAB, D), BF),
        pltpu.VMEM((2, SLAB // 2, D), BF),
        pltpu.VMEM((2, SLAB, D), BF),
    ]

    def __init__(self, wire, part, got, own, far, near):
        self.w, self.part, self.got, self.own = wire, part, got, own
        self.far, self.near = far, near

    def s1(self):
        w, p = self.w, self.w.place
        self.core = []
        for k in (2, 1, -1, 0):
            z = p.pos("z", k)
            self.core.append(w.send(self.part.at[z, 1 - p.c], self.got.at[z], p.at(c=1)))

    def merge(self, i, k):
        p = self.w.place
        z = p.pos("z", k)
        self.core[i].wait_recv()
        add_rows(self.own.at[z], [self.part.at[z, p.c], self.got.at[z]], SLAB)

    def s2(self):
        w, p = self.w, self.w.place
        self.merge(0, 2)
        z = p.pos("z", 2)
        half = SLAB // 2
        self.up = w.send(self.own.at[z, pl.ds(0, half)], self.far.at[0], p.at(z=1))
        self.down = w.send(self.own.at[z, pl.ds(half, half)], self.far.at[1], p.at(z=-1))
        self.merge(1, 1)
        self.merge(2, -1)

    def s3(self):
        w, p = self.w, self.w.place
        half = SLAB // 2
        self.up.wait_recv()
        z = p.pos("z", 1)
        a = self.own.at[z, pl.ds(0, half)]
        add_rows(a, [a, self.far.at[0]], half)
        self.up2 = w.send(self.own.at[z], self.near.at[0], p.at(z=1))
        self.down.wait_recv()
        z = p.pos("z", -1)
        a = self.own.at[z, pl.ds(half, half)]
        add_rows(a, [a, self.far.at[1]], half)
        self.down2 = w.send(self.own.at[z], self.near.at[1], p.at(z=-1))
        self.merge(3, 0)

    def s4(self):
        self.up2.wait_recv()
        self.down2.wait_recv()

    def total(self, at):
        z = self.w.place.z
        return (
            self.own[z, at].astype(F32)
            + self.near[0, at].astype(F32)
            + self.near[1, at].astype(F32)
        )


class LineGather:
    def __init__(self, wire, src, dst):
        self.w, self.src, self.dst = wire, src, dst

    def slot(self, k, half=None):
        p = self.w.place
        if half is None:
            return self.dst.at[p.pos("z", k), p.c]
        return self.dst.at[p.pos("z", k), p.c, pl.ds(half * (SLAB // 2), SLAB // 2)]

    def s1(self):
        w, p = self.w, self.w.place
        self.up = w.send(self.src, self.slot(0), p.at(z=1))
        self.down = w.send(self.src, self.slot(0), p.at(z=-1))
        self.cores = [w.send(self.src, self.slot(0), p.at(c=1))]
        self.local = w.copy(self.src, self.slot(0))

    def s2(self):
        w, p = self.w, self.w.place
        self.up.wait_recv()
        self.up2 = w.send(self.slot(-1, 0), self.slot(-1, 0), p.at(z=1))
        self.cores.append(w.send(self.slot(-1), self.slot(-1), p.at(c=1)))
        self.down.wait_recv()
        self.down2 = w.send(self.slot(1, 1), self.slot(1, 1), p.at(z=-1))
        self.cores.append(w.send(self.slot(1), self.slot(1), p.at(c=1)))

    def s3(self):
        w, p = self.w, self.w.place
        self.up2.wait_recv()
        self.cores.append(w.send(self.slot(2, 0), self.slot(2, 0), p.at(c=1)))
        self.down2.wait_recv()
        self.cores.append(w.send(self.slot(2, 1), self.slot(2, 1), p.at(c=1)))

    def s4(self):
        self.local.wait()
        for cp in self.cores:
            cp.wait_recv()


class Scatter:
    def __init__(self, wire, src, dst, rows):
        self.w, self.src, self.dst, self.rows = wire, src, dst, rows

    def s1(self):
        w, p = self.w, self.w.place
        mine = self.dst.at[pl.ds(pl.multiple_of(p.yh * T + p.r * SLAB, SLAB), SLAB)]
        self.copies = []
        for y, z, c, dev in self.rows:
            at = pl.ds(pl.multiple_of(dev[1] * 128, 128), 128)
            self.copies.append(w.send(self.src.at[:, at], mine, dev))
        at = pl.ds(pl.multiple_of(p.gy * 128, 128), 128)
        self.local = w.copy(self.src.at[:, at], mine)

    def s2(self):
        self.local.wait()
        for cp in self.copies:
            cp.wait_recv()


def each_rows(rows, step, f):
    def body(i, carry):
        f(pl.ds(pl.multiple_of(i * step, step), step))
        return carry

    lax.fori_loop(0, rows // step, body, 0)


def middle_kernel(
    part, hid, gain, after_out, norm_out, send, recv, got, own, far, near, normed,
):
    p = Place()
    w = Wire(p, send, recv)
    greet(line_peers(p))
    s = LineSum(w, part, got, own, far, near)
    s.s1()
    s.s2()
    s.s3()
    s.s4()

    def finish(at):
        after = hid[at].astype(F32) + RES * s.total(at)
        after_out[at] = after
        inv = lax.rsqrt(jnp.mean(after * after, axis=1, keepdims=True) + EPS)
        normed[at] = (after * inv * gain[...]).astype(BF)

    each_rows(SLAB, 16, finish)
    g = LineGather(w, normed, norm_out)
    g.s1()
    g.s2()
    g.s3()
    g.s4()
    w.drain()


def call_middle(part, hid, gain):
    return pl.pallas_call(
        middle_kernel,
        out_shape=[
            jax.ShapeDtypeStruct((SLAB, D), F32),
            jax.ShapeDtypeStruct((4, 2, SLAB, D), BF),
        ],
        in_specs=[VM, VM, VM],
        out_specs=[VM, ANY],
        scratch_shapes=[pltpu.SemaphoreType.DMA((24,)), pltpu.SemaphoreType.DMA((24,))]
        + LineSum.SCRATCH
        + [pltpu.VMEM((SLAB, D), BF)],
        compiler_params=pltpu.CompilerParams(
            collective_id=1, has_side_effects=True, vmem_limit_bytes=24 << 20
        ),
        name="sum_norm_gather",
    )(part, hid, gain)


class WeightSum:
    @staticmethod
    def scratch(rows, cols):
        h = rows // 2
        return [
            pltpu.VMEM((2, 4, h, cols), BF),
            pltpu.VMEM((2, 4, rows, cols), BF),
            pltpu.VMEM((2, 4, rows, cols), BF),
            pltpu.VMEM((4, rows, cols), BF),
            pltpu.VMEM((2, h, cols), BF),
            pltpu.VMEM((2, rows, cols), BF),
            pltpu.VMEM((2, rows, cols), BF),
        ]

    def __init__(self, wire, part, out, start, rows, order, far, go, came, mid, far2, go2, came2):
        self.w, self.part, self.out = wire, part, out
        self.r0, self.n = start, rows
        self.a1, self.a2 = ("y", "x") if order == 0 else ("x", "y")
        self.far, self.go, self.came, self.mid = far, go, came, mid
        self.far2, self.go2, self.came2 = far2, go2, came2

    def src(self, k, j, half=None):
        p = self.w.place
        span = pl.ds(self.r0, self.n)
        if half is not None:
            span = pl.ds(self.r0 + half * (self.n // 2), self.n // 2)
        if self.a1 == "y":
            y = p.pos("y", k)
            return self.part.at[y // 2, j, lax.rem(y, 2), span]
        return self.part.at[j // 2, p.pos("x", k), j % 2, span]

    def four(self, k, half):
        p = self.w.place
        span = pl.ds(self.r0 + half * (self.n // 2), self.n // 2)
        if self.a1 == "y":
            y = p.pos("y", k)
            return self.part.at[y // 2, :, lax.rem(y, 2), span]
        return self.part.at[:, p.pos("x", k), :, span]

    def s1(self):
        w, p = self.w, self.w.place
        if self.a1 == "y":
            self.up = w.send(self.four(2, 0), self.far.at[0], p.step(self.a1, 1))
            self.down = w.send(self.four(2, 1), self.far.at[1], p.step(self.a1, -1))
        else:
            h = self.n // 2
            f = self.far.reshape(2, 2, 2, h, self.far.shape[-1])
            self.up = w.send(self.four(2, 0), f.at[0], p.step(self.a1, 1))
            self.down = w.send(self.four(2, 1), f.at[1], p.step(self.a1, -1))

    def s2(self):
        w, p = self.w, self.w.place
        h = self.n // 2
        for i, k in ((0, 1), (1, -1)):
            (self.up, self.down)[i].wait_recv()
            for j in range(4):
                lo, hi = pl.ds(i * h, h), pl.ds((1 - i) * h, h)
                add_rows(self.go.at[i, j, lo], [self.src(k, j, i), self.far.at[i, j]], h)
                add_rows(self.go.at[i, j, hi], [self.src(k, j, 1 - i)], h)
            cp = w.send(self.go.at[i], self.came.at[i], p.step(self.a1, k))
            if i == 0:
                self.up2 = cp
            else:
                self.down2 = cp

    def s3(self):
        w, p = self.w, self.w.place
        h = self.n // 2
        self.up2.wait_recv()
        self.down2.wait_recv()
        for j in range(4):
            add_rows(self.mid.at[j], [self.src(0, j), self.came.at[0, j], self.came.at[1, j]], self.n)
        j = p.pos(self.a2, 2)
        self.up3 = w.send(self.mid.at[j, pl.ds(0, h)], self.far2.at[0], p.step(self.a2, 1))
        self.down3 = w.send(self.mid.at[j, pl.ds(h, h)], self.far2.at[1], p.step(self.a2, -1))

    def s4(self):
        w, p = self.w, self.w.place
        h = self.n // 2
        for i, k in ((0, 1), (1, -1)):
            (self.up3, self.down3)[i].wait_recv()
            j = p.pos(self.a2, k)
            lo, hi = pl.ds(i * h, h), pl.ds((1 - i) * h, h)
            add_rows(self.go2.at[i, lo], [self.mid.at[j, lo], self.far2.at[i]], h)
            add_rows(self.go2.at[i, hi], [self.mid.at[j, hi]], h)
            cp = w.send(self.go2.at[i], self.came2.at[i], p.step(self.a2, k))
            if i == 0:
                self.up4 = cp
            else:
                self.down4 = cp

    def s5(self):
        p = self.w.place
        self.up4.wait_recv()
        self.down4.wait_recv()
        j = p.pos(self.a2, 0)
        add_rows(
            self.out.at[pl.ds(self.r0, self.n)],
            [self.mid.at[j], self.came2.at[0], self.came2.at[1]],
            self.n,
        )


def norm_back(grad, scaled, inv, gain):
    e = grad * gain
    inner = jnp.mean(e * scaled, axis=1, keepdims=True)
    return inv * (e - scaled * inner)


def turn_kernel(
    part_g, part_f, after, cot, gain, gg, gu, gd,
    attn_out, grad_after, gain_part, out_cols, o_gate, o_up, o_down,
    send, recv, *sc,
):
    p = Place()
    w = Wire(p, send, recv)
    rows = row_peers(p)
    greet(ring_peers(p) + [dev for _, _, _, dev in rows])
    s = LineSum(w, part_g, *sc[0:4])
    f = LineSum(w, part_f, *sc[4:8])
    attn, outs = sc[8:10]
    k = 10
    big = []
    for part, out, start, order in ((gg, o_gate, 0, 0), (gu, o_up, 0, 1), (gd, o_down, 0, 0), (gd, o_down, 256, 1)):
        big.append(WeightSum(w, part, out, start, 256, order, *sc[k : k + 7]))
        k += 7
    s.s1()
    for b in big:
        b.s1()
    s.s2()
    s.s3()
    f.s1()
    for b in big:
        b.s2()
    s.s4()
    gain_part[...] = jnp.zeros_like(gain_part)

    def finish(at):
        a = after[at]
        inv = lax.rsqrt(jnp.mean(a * a, axis=1, keepdims=True) + EPS)
        scaled = a * inv
        g = s.total(at)
        gs = g * scaled
        gain_part[...] += jnp.sum(gs.reshape(2, 8, D), axis=0)
        ga = cot[at].astype(F32) + norm_back(g, scaled, inv, gain[...])
        grad_after[at] = ga
        attn[at] = (RES * ga).astype(BF)

    each_rows(SLAB, 16, finish)
    a = LineGather(w, attn, attn_out)
    a.s1()
    f.s2()
    a.s2()
    f.s3()
    a.s3()
    for b in big:
        b.s3()
    f.s4()

    def last(at):
        outs[at] = (after[at] + RES * f.total(at)).astype(BF)

    each_rows(SLAB, 16, last)
    o = Scatter(w, outs, out_cols, rows)
    o.s1()
    for b in big:
        b.s4()
    for b in big:
        b.s5()
    a.s4()
    o.s2()
    w.drain()


def call_turn(part_g, part_f, after, cot, gain, gg, gu, gd):
    n = 110
    scratch = [pltpu.SemaphoreType.DMA((n,)), pltpu.SemaphoreType.DMA((n,))]
    scratch += LineSum.SCRATCH * 2
    scratch += [pltpu.VMEM((SLAB, D), BF), pltpu.VMEM((SLAB, D), BF)]
    for cols in (512, 512, 256, 256):
        scratch += WeightSum.scratch(256, cols)
    return pl.pallas_call(
        turn_kernel,
        out_shape=[
            jax.ShapeDtypeStruct((4, 2, SLAB, D), BF),
            jax.ShapeDtypeStruct((SLAB, D), F32),
            jax.ShapeDtypeStruct((8, D), F32),
            jax.ShapeDtypeStruct((2 * T, 128), BF),
            jax.ShapeDtypeStruct((256, 512), F32),
            jax.ShapeDtypeStruct((256, 512), F32),
            jax.ShapeDtypeStruct((512, 256), F32),
        ],
        in_specs=[VM] * 8,
        out_specs=[ANY, VM, VM, ANY, VM, VM, VM],
        scratch_shapes=scratch,
        compiler_params=pltpu.CompilerParams(
            collective_id=2, has_side_effects=True, vmem_limit_bytes=62 << 20
        ),
        name="turn",
    )(part_g, part_f, after, cot, gain, gg, gu, gd)


def end_kernel(
    part, hid, grad_after, gain, gain_two, gq, go,
    hid_cols, o_gain, o_q, o_o,
    send, recv, got, own, far, near, outs, gains, gcame, gsum, gcame2, rq, ro, *sc,
):
    p = Place()
    w = Wire(p, send, recv)
    rows = row_peers(p)
    lanes = [(k, (lax.rem(p.gx + k, 8), p.gy)) for k in range(1, 8)]
    greet([dev for _, _, _, dev in rows] + [dev for _, dev in lanes] + [p.at(y=1), p.at(y=-1)])
    s = LineSum(w, part, got, own, far, near)
    s.s1()
    swaps = [w.send(src.at[1 - p.c], dst.at[p.c], p.at(c=1)) for src, dst in ((gq, rq), (go, ro))]
    own_copies = [w.copy(src.at[p.c], dst.at[p.c]) for src, dst in ((gq, rq), (go, ro))]
    big = [
        WeightSum(w, rq, o_q, 0, 256, 0, *sc[0:7]),
        WeightSum(w, ro, o_o, 0, 128, 1, *sc[7:14]),
    ]
    s.s2()
    for cp in swaps:
        cp.wait_recv()
    for cp in own_copies:
        cp.wait()
    for b in big:
        b.s1()
    s.s3()
    for b in big:
        b.s2()
    s.s4()
    gains[...] = jnp.zeros_like(gains)

    def finish(at):
        a = hid[at].astype(F32)
        inv = lax.rsqrt(jnp.mean(a * a, axis=1, keepdims=True) + EPS)
        scaled = a * inv
        g = s.total(at)
        gs = g * scaled
        gains[0] += jnp.sum(gs.reshape(2, 8, D), axis=0)
        outs[at] = (grad_after[at] + norm_back(g, scaled, inv, gain[...])).astype(BF)

    each_rows(SLAB, 16, finish)
    o = Scatter(w, outs, hid_cols, rows)
    o.s1()
    gains[1] = gain_two[...]
    mine = pl.ds(pl.multiple_of(p.gy * 128, 128), 128)
    gcp = []
    for _, _, _, dev in rows:
        at = pl.ds(pl.multiple_of(dev[1] * 128, 128), 128)
        gcp.append(w.send(gains.at[:, :, at], gcame.at[p.gy], dev))
    glocal = w.copy(gains.at[:, :, mine], gcame.at[p.gy])
    for b in big:
        b.s3()
    for b in big:
        b.s4()
    for cp in gcp:
        cp.wait_recv()
    glocal.wait()
    gsum[...] = jnp.sum(gcame[...], axis=0)
    lcp = [w.send(gsum, gcame2.at[p.gx], dev) for _, dev in lanes]
    llocal = w.copy(gsum, gcame2.at[p.gx])
    for b in big:
        b.s5()
    for cp in lcp:
        cp.wait_recv()
    llocal.wait()
    o_gain[...] = jnp.sum(gcame2[...], axis=0)
    o.s2()
    w.drain()


def call_end(part, hid, grad_after, gain, gain_two, gq, go):
    n = 100
    scratch = [pltpu.SemaphoreType.DMA((n,)), pltpu.SemaphoreType.DMA((n,))]
    scratch += LineSum.SCRATCH
    scratch += [
        pltpu.VMEM((SLAB, D), BF),
        pltpu.VMEM((2, 8, D), F32),
        pltpu.VMEM((16, 2, 8, 128), F32),
        pltpu.VMEM((2, 8, 128), F32),
        pltpu.VMEM((8, 2, 8, 128), F32),
        pltpu.VMEM((2, 4, 2, 256, 192), BF),
        pltpu.VMEM((2, 4, 2, 128, 256), BF),
    ]
    scratch += WeightSum.scratch(256, 192) + WeightSum.scratch(128, 256)
    return pl.pallas_call(
        end_kernel,
        out_shape=[
            jax.ShapeDtypeStruct((2 * T, 128), BF),
            jax.ShapeDtypeStruct((2, 8, 128), F32),
            jax.ShapeDtypeStruct((256, 192), F32),
            jax.ShapeDtypeStruct((128, 256), F32),
        ],
        in_specs=[VM] * 7,
        out_specs=[ANY, VM, VM, VM],
        scratch_shapes=scratch,
        compiler_params=pltpu.CompilerParams(
            collective_id=3, has_side_effects=True, vmem_limit_bytes=40 << 20
        ),
        name="finish",
    )(part, hid, grad_after, gain, gain_two, gq, go)


def contract(a, b, da, db):
    return lax.dot_general(a, b, (((da,), (db,)), ((), ())), preferred_element_type=F32)


def key_range(i):
    start = max(0, (i - 2) * QB)
    return start, (i + 1) * QB


def mask_of(seg_col, seg_row, lo, hi, i):
    same = seg_col[lo:hi] == seg_row[:, i * QB : (i + 1) * QB]
    rows = lo + lax.broadcasted_iota(jnp.int32, (hi - lo, QB), 0)
    cols = i * QB + lax.broadcasted_iota(jnp.int32, (hi - lo, QB), 1)
    return same & (rows <= cols)


def attend_kernel(q, k, vt, seg_col, seg_row, out, lse):
    for i in range(T // QB):
        lo, hi = key_range(i)
        mask = mask_of(seg_col, seg_row, lo, hi, i)
        at = slice(i * QB, (i + 1) * QB)
        s = contract(k[lo:hi], q[0, at], 1, 1) * ATTN_SCALE
        s = jnp.where(mask, s, -1e30)
        top = jnp.max(s, axis=0, keepdims=True)
        e = jnp.exp(s - top)
        total = jnp.sum(e, axis=0, keepdims=True)
        pr = (e * (1.0 / total)).astype(BF)
        out[0, :, at] = contract(vt[:, lo:hi], pr, 1, 0).astype(BF)
        lse[0, :, at] = top + jnp.log(total)


def call_attend(q, k, vt, seg_col, seg_row):
    return pl.pallas_call(
        attend_kernel,
        grid=(4,),
        out_shape=[
            jax.ShapeDtypeStruct((4, HEAD, T), BF),
            jax.ShapeDtypeStruct((4, 1, T), F32),
        ],
        in_specs=[
            pl.BlockSpec((1, T, HEAD), lambda h: (h, 0, 0)),
            pl.BlockSpec((T, HEAD), lambda h: (0, 0)),
            pl.BlockSpec((HEAD, T), lambda h: (0, 0)),
            pl.BlockSpec((T, 1), lambda h: (0, 0)),
            pl.BlockSpec((1, T), lambda h: (0, 0)),
        ],
        out_specs=[
            pl.BlockSpec((1, HEAD, T), lambda h: (h, 0, 0)),
            pl.BlockSpec((1, 1, T), lambda h: (h, 0, 0)),
        ],
        compiler_params=pltpu.CompilerParams(vmem_limit_bytes=40 << 20),
        name="attend",
    )(q, k, vt, seg_col, seg_row)


def attend_back_kernel(q, k, kt, v, g, out_t, gt, lse, seg_col, seg_row, gq, gk, gv):
    @pl.when(pl.program_id(0) == 0)
    def _():
        gk[...] = jnp.zeros_like(gk)
        gv[...] = jnp.zeros_like(gv)

    for i in range(T // QB):
        lo, hi = key_range(i)
        mask = mask_of(seg_col, seg_row, lo, hi, i)
        at = slice(i * QB, (i + 1) * QB)
        qb, gb = q[0, at], g[0, at]
        s = contract(k[lo:hi], qb, 1, 1) * ATTN_SCALE
        pr = jnp.where(mask, jnp.exp(jnp.where(mask, s, -1e30) - lse[0, :, at]), 0.0)
        gp = contract(v[lo:hi], gb, 1, 1)
        inner = jnp.sum(out_t[0, :, at].astype(F32) * gt[0, :, at].astype(F32), axis=0, keepdims=True)
        gs = (pr * (gp - inner)).astype(BF)
        gq[0, :, at] = contract(kt[:, lo:hi], gs, 1, 0) * ATTN_SCALE
        gk[lo:hi] += contract(gs, qb, 1, 0) * ATTN_SCALE
        gv[lo:hi] += contract(pr.astype(BF), gb, 1, 0)


def call_attend_back(q, k, kt, v, g, out_t, gt, lse, seg_col, seg_row):
    per = lambda *s: pl.BlockSpec((1, *s), lambda h: (h, 0, 0))
    all_ = lambda *s: pl.BlockSpec(s, lambda h: (0, 0))
    return pl.pallas_call(
        attend_back_kernel,
        grid=(4,),
        out_shape=[
            jax.ShapeDtypeStruct((4, HEAD, T), F32),
            jax.ShapeDtypeStruct((T, HEAD), F32),
            jax.ShapeDtypeStruct((T, HEAD), F32),
        ],
        in_specs=[
            per(T, HEAD), all_(T, HEAD), all_(HEAD, T), all_(T, HEAD), per(T, HEAD),
            per(HEAD, T), per(HEAD, T), per(1, T), all_(T, 1), all_(1, T),
        ],
        out_specs=[per(HEAD, T), all_(T, HEAD), all_(T, HEAD)],
        compiler_params=pltpu.CompilerParams(vmem_limit_bytes=40 << 20),
        name="attend_back",
    )(q, k, kt, v, g, out_t, gt, lse, seg_col, seg_row)


def rope_tables(segment):
    index = jnp.arange(T, dtype=jnp.int32)
    boundary = jnp.concatenate([jnp.ones((1,), jnp.bool_), segment[1:] != segment[:-1]])
    starts = lax.cummax(jnp.where(boundary, index, 0), axis=0)
    places = (index - starts).astype(F32)
    frequency = ROPE_BASE ** (-jnp.arange(0, HEAD, 2, dtype=F32) / HEAD)
    turned = places[:, None] * frequency
    return (jnp.cos(turned)[:, None], jnp.sin(turned)[:, None])


def rotate(v, cos, sin):
    h = HEAD // 2
    a, b = v[..., :h], v[..., h:]
    return jnp.concatenate([a * cos - b * sin, b * cos + a * sin], axis=-1)


def dot(a, b):
    return jnp.dot(a, b, preferred_element_type=F32)


def by_column_block(w):
    x, y, rows, cols = w.shape
    return w.reshape(x * y, rows, cols).transpose(1, 0, 2).reshape(rows, x * y * cols)


def to_column_blocks(g):
    rows = g.shape[0]
    return g.reshape(rows, 8, 256).transpose(1, 0, 2).reshape(4, 2, rows, 256)


def per_device(
    hidden, attn_gain, wq, wk, wv, wo, ffn_gain, gate, up, down, segments, cotangent,
):
    gy = lax.axis_index("gy")
    yh, r = gy // 8, gy % 8
    gains = jnp.zeros((8, 128), F32).at[0].set(attn_gain).at[1].set(ffn_gain)
    wqkv = jnp.concatenate([wq, wk, wv], axis=1)
    hid, cot, aq, ao, gg, uu, dd, gain_all = call_gather(
        hidden, cotangent, wqkv, wo, gate, up, down, gains
    )
    gain_one = gain_all[:, 0].reshape(1, D)
    gain_two = gain_all[:, 1].reshape(1, D)
    segment = lax.dynamic_index_in_dim(segments, yh, 0, keepdims=False)
    seg_col, seg_row = segment[:, None], segment[None, :]
    cos, sin = rope_tables(segment)

    stream = hid.astype(F32)
    inv_one = lax.rsqrt(jnp.mean(stream * stream, axis=1, keepdims=True) + EPS)
    normed_one = (stream * inv_one * gain_one).astype(BF)
    aq = aq.reshape(2, D, 192)
    lin = [dot(normed_one, aq[j]) for j in range(2)]
    q_lin = jnp.concatenate([v[:, :128] for v in lin], axis=1).reshape(T, 4, HEAD)
    k_lin = jnp.concatenate([v[:, 128:160] for v in lin], axis=1)
    v_lin = jnp.concatenate([v[:, 160:] for v in lin], axis=1)
    q = rotate(q_lin, cos, sin).astype(BF).transpose(1, 0, 2)
    k = rotate(k_lin[:, None], cos, sin).astype(BF)[:, 0]
    v = v_lin.astype(BF)
    heads_t, lse = call_attend(q, k, v.T, seg_col, seg_row)
    heads = heads_t.transpose(2, 0, 1).reshape(T, 4 * HEAD)
    o_full = jnp.concatenate([by_column_block(ao[j]) for j in range(2)], axis=0)
    attn_part = dot(heads, o_full).astype(BF).reshape(4, 2, SLAB, D)
    hid_slab = lax.dynamic_slice_in_dim(hid, r * SLAB, SLAB, 0)
    cot_slab = lax.dynamic_slice_in_dim(cot, r * SLAB, SLAB, 0)
    after, normed_two = call_middle(attn_part, hid_slab, gain_two)
    normed_two = normed_two.reshape(T, D)

    gg, uu = gg.reshape(2, D, 512), uu.reshape(2, D, 512)
    grad_ffn = (RES * cot.astype(F32)).astype(BF)
    ffn_part = 0.0
    norm_part = 0.0
    g_gate, g_up, g_down = [], [], []
    for j in range(2):
        gate_pre = dot(normed_two, gg[j])
        up_pre = dot(normed_two, uu[j])
        sig = jax.nn.sigmoid(gate_pre)
        activated = gate_pre * sig
        hidden_act = (activated * up_pre).astype(BF)
        d_full = by_column_block(dd[j])
        ffn_part += dot(hidden_act, d_full)
        grad_act = contract(grad_ffn, d_full, 1, 1).astype(BF).astype(F32)
        ggp = (grad_act * up_pre * sig * (1.0 + gate_pre * (1.0 - sig))).astype(BF)
        gup = (grad_act * activated).astype(BF)
        norm_part += contract(ggp, gg[j], 1, 1) + contract(gup, uu[j], 1, 1)
        g_gate.append(contract(normed_two, ggp, 0, 0).astype(BF).reshape(4, 2, 256, 512))
        g_up.append(contract(normed_two, gup, 0, 0).astype(BF).reshape(4, 2, 256, 512))
        g_down.append(to_column_blocks(contract(hidden_act, grad_ffn, 0, 0).astype(BF)))
    grad_attn, grad_after, gain_two_part, out_cols, o_gate, o_up, o_down = call_turn(
        norm_part.astype(BF).reshape(4, 2, SLAB, D),
        ffn_part.astype(BF).reshape(4, 2, SLAB, D),
        after, cot_slab, gain_two,
        jnp.stack(g_gate), jnp.stack(g_up), jnp.stack(g_down),
    )
    grad_attn = grad_attn.reshape(T, D)
    grad_o = contract(heads, grad_attn, 0, 0).astype(BF)
    grad_heads = contract(grad_attn, o_full, 1, 1).astype(BF)
    gh = grad_heads.reshape(T, 4, HEAD)
    gq_t, gk, gv = call_attend_back(
        q, k, k.T, v, gh.transpose(1, 0, 2), heads_t, gh.transpose(1, 2, 0), lse, seg_col, seg_row
    )
    gq = rotate(gq_t.transpose(2, 0, 1), cos, -sin).astype(BF).reshape(T, 256)
    gk = rotate(gk[:, None], cos, -sin)[:, 0].astype(BF)
    gv = gv.astype(BF)
    grad_part = 0.0
    g_qkv = []
    for j in range(2):
        g = jnp.concatenate(
            [gq[:, j * 128 : (j + 1) * 128], gk[:, j * 32 : (j + 1) * 32], gv[:, j * 32 : (j + 1) * 32]], axis=1
        )
        grad_part += contract(g, aq[j], 1, 1)
        g_qkv.append(contract(normed_one, g, 0, 0).astype(BF).reshape(4, 2, 256, 192))
    g_o = jnp.stack([to_column_blocks(grad_o[j * 128 : (j + 1) * 128]) for j in range(2)])
    hid_cols, o_gain, o_qkv, o_o = call_end(
        grad_part.astype(BF).reshape(4, 2, SLAB, D),
        hid_slab, grad_after, gain_one, gain_two_part, jnp.stack(g_qkv), g_o,
    )
    both = jnp.sum(o_gain, axis=1)
    return (
        out_cols.astype(F32),
        hid_cols.astype(F32),
        both[0],
        o_qkv[:, :128],
        o_qkv[:, 128:160],
        o_qkv[:, 160:],
        o_o,
        both[1],
        o_gate,
        o_up,
        o_down,
    )


def solution(mesh):
    wide, cols, tall = P("gx", "gy"), P("gy"), P("gy", "gx")
    return jax.shard_map(
        per_device,
        mesh=mesh,
        in_specs=(wide, cols, wide, wide, wide, tall, cols, wide, wide, tall, P("gx", None), wide),
        out_specs=(wide, wide, cols, wide, wide, wide, tall, cols, wide, wide, tall),
        check_vma=False,
    )
```

```python
import functools

import jax
import jax.numpy as jnp
from jax import lax
from jax.experimental import pallas as pl
from jax.experimental.pallas import tpu as pltpu
from jax.sharding import PartitionSpec as P

HEAD = 64
EPS = 1e-06
ROPE_BASE = 10000000.0
ATTN_SCALE = 1.0 / 64.0
RES = 0.22
T = 1024
D = 2048
SLAB = 128
QB = 256
BF = jnp.bfloat16
F32 = jnp.float32
MESH = pl.DeviceIdType.MESH
ANY = pl.BlockSpec(memory_space=pl.ANY)
VM = pl.BlockSpec(memory_space=pltpu.VMEM)


class Place:
    def __init__(self):
        gx = lax.axis_index("gx")
        gy = lax.axis_index("gy")
        self.gx, self.gy = gx, gy
        self.x, self.yl = gx // 2, lax.rem(gx, 2)
        self.yh, self.z, self.c = gy // 8, lax.rem(gy // 2, 4), lax.rem(gy, 2)
        self.y = self.yh * 2 + self.yl
        self.r = self.z * 2 + self.c

    def at(self, x=0, y=0, z=0, c=0):
        xx = lax.rem(self.x + x + 4, 4)
        yy = lax.rem(self.y + y + 4, 4)
        zz = lax.rem(self.z + z + 4, 4)
        cc = lax.rem(self.c + c, 2)
        return (xx * 2 + lax.rem(yy, 2), (yy // 2) * 8 + zz * 2 + cc)

    def step(self, axis, k):
        return self.at(**{axis: k})

    def pos(self, axis, k):
        return lax.rem(getattr(self, axis) + k + 4, 4)


class Wire:
    def __init__(self, place, send, recv):
        self.place, self.send_sem, self.recv_sem = place, send, recv
        self.count = 0
        self.sent = []

    def send(self, src, dst, to):
        i = self.count
        self.count += 1
        cp = pltpu.make_async_remote_copy(
            src_ref=src,
            dst_ref=dst,
            send_sem=self.send_sem.at[i],
            recv_sem=self.recv_sem.at[i],
            device_id=to,
            device_id_type=MESH,
        )
        cp.start()
        self.sent.append(cp)
        return cp

    def copy(self, src, dst):
        i = self.count
        self.count += 1
        cp = pltpu.make_async_copy(src, dst, self.send_sem.at[i])
        cp.start()
        return cp

    def drain(self):
        for cp in self.sent:
            cp.wait_send()
        self.sent = []


def greet(peers):
    barrier = pltpu.get_barrier_semaphore()
    for peer in peers:
        pl.semaphore_signal(barrier, inc=1, device_id=peer, device_id_type=MESH)
    pl.semaphore_wait(barrier, len(peers))


def ring_peers(p):
    return [p.at(x=1), p.at(x=-1), p.at(y=1), p.at(y=-1)]


def row_peers(p):
    out = []
    for y in (0, 2):
        for z in range(4):
            for c in range(2):
                if (y, z, c) != (0, 0, 0):
                    out.append((y, z, c, p.at(y=y, z=z, c=c)))
    return out


def line_peers(p):
    return [p.at(c=1), p.at(z=1), p.at(z=-1)]


class WeightGather:
    def __init__(self, wire, src, dst, start, rows, order):
        self.w, self.src, self.dst = wire, src, dst
        self.r0, self.n, self.order = start, rows, order
        self.a1, self.a2 = ("x", "y") if order == 0 else ("y", "x")

    def one(self, k, half=None):
        p = self.w.place
        x, y = (p.pos("x", k), p.y) if self.a1 == "x" else (p.x, p.pos("y", k))
        return self.dst.at[y // 2, x, lax.rem(y, 2), self.span(half)]

    def four(self, k, half=None):
        p = self.w.place
        if self.a2 == "y":
            y = p.pos("y", k)
            return self.dst.at[y // 2, :, lax.rem(y, 2), self.span(half)]
        return self.dst.at[:, p.pos("x", k), :, self.span(half)]

    def span(self, half):
        if half is None:
            return pl.ds(self.r0, self.n)
        return pl.ds(self.r0 + half * (self.n // 2), self.n // 2)

    def s1(self):
        w, p = self.w, self.w.place
        own = self.src.at[pl.ds(self.r0, self.n)]
        self.local = w.copy(own, self.one(0))
        self.up = w.send(own, self.one(0), p.step(self.a1, 1))
        self.down = w.send(own, self.one(0), p.step(self.a1, -1))

    def s2(self):
        w, p = self.w, self.w.place
        self.up.wait_recv()
        self.up2 = w.send(self.one(-1, 0), self.one(-1, 0), p.step(self.a1, 1))
        self.down.wait_recv()
        self.down2 = w.send(self.one(1, 1), self.one(1, 1), p.step(self.a1, -1))

    def s3(self):
        w, p = self.w, self.w.place
        self.local.wait()
        self.up2.wait_recv()
        self.down2.wait_recv()
        self.up3 = w.send(self.four(0), self.four(0), p.step(self.a2, 1))
        self.down3 = w.send(self.four(0), self.four(0), p.step(self.a2, -1))

    def s4(self):
        w, p = self.w, self.w.place
        self.up3.wait_recv()
        self.up4 = w.send(self.four(-1, 0), self.four(-1, 0), p.step(self.a2, 1))
        self.down3.wait_recv()
        self.down4 = w.send(self.four(1, 1), self.four(1, 1), p.step(self.a2, -1))

    def s5(self):
        self.up4.wait_recv()
        self.down4.wait_recv()


class RowGather:
    def __init__(self, wire, src, dst):
        self.w, self.src, self.dst = wire, src, dst

    def block(self, yh, k, c=None):
        p = self.w.place
        c = p.c if c is None else c
        gy = yh * 8 + p.pos("z", k) * 2 + c
        return self.dst.at[:, pl.ds(pl.multiple_of(gy * 128, 128), 128)]

    def out(self, src, yh, k):
        b = self.block(yh, k)
        self.cores.append(self.w.send(src, b, self.w.place.at(c=1)))

    def s1(self):
        w, p = self.w, self.w.place
        self.cores = []
        mine = self.src.at[pl.ds(pl.multiple_of(p.yh * T, T), T)]
        other = self.src.at[pl.ds(pl.multiple_of((1 - p.yh) * T, T), T)]
        own = self.block(p.yh, 0)
        self.local = w.copy(mine, own)
        self.swap = w.send(other, own, p.at(y=2))
        self.up0 = w.send(mine, own, p.at(z=1))
        self.down0 = w.send(mine, own, p.at(z=-1))
        self.out(mine, p.yh, 0)

    def s2(self):
        w, p = self.w, self.w.place
        self.swap.wait_recv()
        b = self.block(1 - p.yh, 0)
        self.up1 = w.send(b, b, p.at(z=1))
        self.down1 = w.send(b, b, p.at(z=-1))
        self.out(b, 1 - p.yh, 0)

    def s3(self):
        w, p = self.w, self.w.place
        self.up0.wait_recv()
        b = self.block(p.yh, -1)
        self.up2 = w.send(b, b, p.at(z=1))
        self.out(b, p.yh, -1)
        self.down0.wait_recv()
        self.out(self.block(p.yh, 1), p.yh, 1)
        self.down1.wait_recv()
        b = self.block(1 - p.yh, 1)
        self.down2 = w.send(b, b, p.at(z=-1))
        self.out(b, 1 - p.yh, 1)
        self.up1.wait_recv()
        self.out(self.block(1 - p.yh, -1), 1 - p.yh, -1)

    def s4(self):
        p = self.w.place
        self.up2.wait_recv()
        self.out(self.block(p.yh, 2), p.yh, 2)
        self.down2.wait_recv()
        self.out(self.block(1 - p.yh, 2), 1 - p.yh, 2)

    def s5(self):
        self.local.wait()
        for cp in self.cores:
            cp.wait_recv()


def add_rows(dst, srcs, rows, step=16):
    def body(i, carry):
        at = pl.ds(pl.multiple_of(i * step, step), step)
        total = srcs[0][at].astype(F32)
        for s in srcs[1:]:
            total = total + s[at].astype(F32)
        dst[at] = total.astype(dst.dtype)
        return carry

    lax.fori_loop(0, rows // step, body, 0)


class LineSum:
    SCRATCH = [
        pltpu.VMEM((4, SLAB, D), BF),
        pltpu.VMEM((2, SLAB // 2, D), BF),
        pltpu.VMEM((2, SLAB, D), BF),
    ]
    ORDER = (2, 1, -1, 0)

    def __init__(self, wire, part, got, far, near):
        self.w, self.part, self.got = wire, part, got
        self.far, self.near = far, near
        self.core = {}

    def mine(self, k, half=None):
        p = self.w.place
        if half is None:
            return self.part.at[p.pos("z", k), p.c]
        return self.part.at[p.pos("z", k), p.c, pl.ds(half * (SLAB // 2), SLAB // 2)]

    def push(self, k):
        w, p = self.w, self.w.place
        z = p.pos("z", k)
        self.core[k] = w.send(self.part.at[z, 1 - p.c], self.got.at[z], p.at(c=1))

    def merge(self, k):
        z = self.w.place.pos("z", k)
        self.core[k].wait_recv()
        add_rows(self.mine(k), [self.mine(k), self.got.at[z]], SLAB)

    def send_far(self):
        w, p = self.w, self.w.place
        self.up = w.send(self.mine(2, 0), self.far.at[0], p.at(z=1))
        self.down = w.send(self.mine(2, 1), self.far.at[1], p.at(z=-1))

    def send_near(self):
        w, p = self.w, self.w.place
        self.up.wait_recv()
        add_rows(self.mine(1, 0), [self.mine(1, 0), self.far.at[0]], SLAB // 2)
        self.up2 = w.send(self.mine(1), self.near.at[0], p.at(z=1))
        self.down.wait_recv()
        add_rows(self.mine(-1, 1), [self.mine(-1, 1), self.far.at[1]], SLAB // 2)
        self.down2 = w.send(self.mine(-1), self.near.at[1], p.at(z=-1))

    def after_block(self, t):
        self.push(self.ORDER[t])
        if t == 1:
            self.merge(2)
            self.send_far()
        if t == 2:
            self.merge(1)
        if t == 3:
            self.merge(-1)
            self.send_near()
            self.merge(0)

    def wait(self):
        self.up2.wait_recv()
        self.down2.wait_recv()

    def total(self, at):
        p = self.w.place
        return (
            self.part[p.z, p.c, :, at].astype(F32)
            + self.near[0, :, at].astype(F32)
            + self.near[1, :, at].astype(F32)
        )


class LineGather:
    def __init__(self, wire, src, dst):
        self.w, self.src, self.dst = wire, src, dst

    def slot(self, k, half=None):
        p = self.w.place
        if half is None:
            return self.dst.at[p.pos("z", k), p.c]
        return self.dst.at[p.pos("z", k), p.c, pl.ds(half * (SLAB // 2), SLAB // 2)]

    def s1(self):
        w, p = self.w, self.w.place
        self.up = w.send(self.src, self.slot(0), p.at(z=1))
        self.down = w.send(self.src, self.slot(0), p.at(z=-1))
        self.cores = [w.send(self.src, self.slot(0), p.at(c=1))]
        self.local = w.copy(self.src, self.slot(0))

    def s2(self):
        w, p = self.w, self.w.place
        self.up.wait_recv()
        self.up2 = w.send(self.slot(-1, 0), self.slot(-1, 0), p.at(z=1))
        self.cores.append(w.send(self.slot(-1), self.slot(-1), p.at(c=1)))
        self.down.wait_recv()
        self.down2 = w.send(self.slot(1, 1), self.slot(1, 1), p.at(z=-1))
        self.cores.append(w.send(self.slot(1), self.slot(1), p.at(c=1)))

    def s3(self):
        w, p = self.w, self.w.place
        self.up2.wait_recv()
        self.cores.append(w.send(self.slot(2, 0), self.slot(2, 0), p.at(c=1)))
        self.down2.wait_recv()
        self.cores.append(w.send(self.slot(2, 1), self.slot(2, 1), p.at(c=1)))

    def s4(self):
        self.local.wait()
        for cp in self.cores:
            cp.wait_recv()


class Scatter:
    def __init__(self, wire, src, dst, rows):
        self.w, self.src, self.dst, self.rows = wire, src, dst, rows

    def s1(self):
        w, p = self.w, self.w.place
        mine = self.dst.at[pl.ds(pl.multiple_of(p.yh * T + p.r * SLAB, SLAB), SLAB)]
        self.copies = []
        for y, z, c, dev in self.rows:
            at = pl.ds(pl.multiple_of(dev[1] * 128, 128), 128)
            self.copies.append(w.send(self.src.at[:, at], mine, dev))
        at = pl.ds(pl.multiple_of(p.gy * 128, 128), 128)
        self.local = w.copy(self.src.at[:, at], mine)

    def s2(self):
        self.local.wait()
        for cp in self.copies:
            cp.wait_recv()


def each_rows(rows, step, f):
    def body(i, carry):
        f(pl.ds(pl.multiple_of(i * step, step), step))
        return carry

    lax.fori_loop(0, rows // step, body, 0)


COLS = [slice(j * 128, (j + 1) * 128) for j in range(16)]


def contract(a, b, da, db):
    return lax.dot_general(a, b, (((da,), (db,)), ((), ())), preferred_element_type=F32)


def rows_of(i, n):
    return pl.ds(pl.multiple_of(i * n, n), n)


def row_mean(parts):
    total = parts[0]
    for v in parts[1:]:
        total = total + v
    return jnp.sum(total, axis=1, keepdims=True) * (1.0 / D)


def norm_scale(load):
    squares = []
    total = None
    for at in COLS:
        v = load(at)
        total = v * v if total is None else total + v * v
    return lax.rsqrt(jnp.sum(total, axis=1, keepdims=True) * (1.0 / D) + EPS)


def key_window(i):
    return pl.multiple_of(jnp.maximum(i - 2, 0) * QB, QB)


def bias_tile(seg_col, seg_row, lo, n, i):
    first = i * QB
    same = seg_col[pl.ds(lo, n)] == seg_row[:, pl.ds(first, QB)]
    rows = lo + lax.broadcasted_iota(jnp.int32, (n, QB), 0)
    cols = first + lax.broadcasted_iota(jnp.int32, (n, QB), 1)
    return jnp.where(same & (rows <= cols), 0.0, -1e30)


def first_kernel(
    hidden, cot, wq, wo, gate, up, down, gains, seg_cols, seg_rows, freq,
    c_out, g_out, u_out, d_out, q_out, o_out, n1_out, slab_out, qt_out, kt_out, vt_out, ht_out,
    lse_out, after_out, n2_out, gain_out, cos_out, sin_out, q_tmp, o_tmp,
    send, recv, h, n1, w2, o2, qt, kt, vt, ht, part, got, far, near, after, normed,
    gain, seg_col, seg_row, cos, sin, bias, lse,
):
    p = Place()
    w = Wire(p, send, recv)
    rows = row_peers(p)
    greet(ring_peers(p) + [dev for _, _, _, dev in rows])
    hg = RowGather(w, hidden, h)
    cg = RowGather(w, cot, c_out)
    aq = WeightGather(w, wq, q_tmp, 0, 256, 0)
    ao = WeightGather(w, wo, o_tmp, 0, 128, 1)
    big = [
        WeightGather(w, gate, g_out, 0, 256, 0),
        WeightGather(w, up, u_out, 0, 256, 1),
        WeightGather(w, down, d_out, 0, 256, 0),
        WeightGather(w, down, d_out, 256, 256, 1),
    ]
    hg.s1()
    aq.s1()
    ao.s1()
    own = pl.ds(pl.multiple_of(p.gy * 128, 128), 128)
    glocal = w.copy(gains, gain.at[:, own])
    gcopies = [w.send(gains, gain.at[:, own], dev) for _, _, _, dev in rows]

    seg_row[...] = jnp.where(p.yh == 0, seg_rows[0:1], seg_rows[1:2])
    seg_col[...] = jnp.where(p.yh == 0, seg_cols[:, 0:1], seg_cols[:, 1:2])
    earlier = jnp.zeros((8, T), F32)
    for b in range(8):
        less = seg_col[b * 128 : (b + 1) * 128] < seg_row[...]
        earlier = earlier + jnp.sum(jnp.where(less, 1.0, 0.0).reshape(16, 8, T), axis=0)
    starts = jnp.sum(earlier, axis=0, keepdims=True)
    places = lax.broadcasted_iota(jnp.int32, (1, T), 1).astype(F32) - starts
    turned = freq[...] * places
    cos[...] = jnp.cos(turned)
    sin[...] = jnp.sin(turned)

    hg.s2()
    aq.s2()
    ao.s2()
    for b in big:
        b.s1()
    hg.s3()
    aq.s3()
    ao.s3()
    hg.s4()
    aq.s4()
    ao.s4()
    cg.s1()
    for b in big:
        b.s2()
    aq.s5()
    ao.s5()
    swaps = [w.send(tmp.at[1 - p.c], out.at[p.c], p.at(c=1)) for tmp, out in ((q_tmp, q_out), (o_tmp, o_out))]
    kept = [w.copy(q_tmp.at[p.c], q_out.at[p.c]), w.copy(o_tmp.at[p.c], o_out.at[p.c])]
    for cp in kept:
        cp.wait()
    for cp in swaps:
        cp.wait_recv()
    loads = [w.copy(q_out.at[j], w2.at[j].reshape(4, 2, 256, 192)) for j in range(2)]
    for j in range(2):
        for g in range(8):
            loads.append(
                w.copy(o_out.at[j, g // 2, g % 2], o2.at[pl.ds(j * 128, 128), pl.ds(g * 256, 256)])
            )
    hg.s5()
    cg.s2()
    glocal.wait()
    for cp in gcopies:
        cp.wait_recv()
    for cp in loads:
        cp.wait()
    for b in big:
        b.s3()

    def project(i, carry):
        at = rows_of(i, QB)
        inv = norm_scale(lambda c: h[at, c].astype(F32))
        for c in COLS:
            n1[at, c] = (h[at, c].astype(F32) * inv * gain[0:1, c]).astype(BF)
        ct, st = cos[:, at], sin[:, at]
        keys = []
        for j in range(2):
            lin = contract(n1[at], w2[j], 1, 0)
            qj = lin[:, :128].T
            kv = lin[:, 128:].T
            for hh in range(2):
                a, b = qj[hh * 64 : hh * 64 + 32], qj[hh * 64 + 32 : hh * 64 + 64]
                qt[2 * j + hh, 0:32, at] = (a * ct - b * st).astype(BF) * ATTN_SCALE
                qt[2 * j + hh, 32:64, at] = (b * ct + a * st).astype(BF) * ATTN_SCALE
            keys.append(kv[:32])
            vt[j * 32 : (j + 1) * 32, at] = kv[32:].astype(BF)
        a, b = keys
        kt[0:32, at] = (a * ct - b * st).astype(BF)
        kt[32:64, at] = (b * ct + a * st).astype(BF)
        return carry

    lax.fori_loop(0, 4, project, 0)
    exports = [
        w.copy(n1, n1_out),
        w.copy(h.at[pl.ds(pl.multiple_of(p.r * SLAB, SLAB), SLAB)], slab_out),
        w.copy(qt, qt_out), w.copy(kt, kt_out), w.copy(vt, vt_out),
    ]
    gain_out[...] = gain[...]
    cos_out[...] = cos[...]
    sin_out[...] = sin[...]
    cg.s3()
    s = LineSum(w, part, got, far, near)
    for t, k in enumerate(LineSum.ORDER):
        i = p.pos("z", k)
        lo = key_window(i)
        at = rows_of(i, QB)
        keys = pl.ds(lo, 3 * QB)
        bias[...] = bias_tile(seg_col, seg_row, lo, 3 * QB, pl.multiple_of(i, 1))

        def head(n, carry):
            sc = contract(kt[:, keys], qt[n, :, at], 0, 0) + bias[...]
            top = jnp.max(sc, axis=0, keepdims=True)
            e = jnp.exp(sc - top)
            total = jnp.sum(e, axis=0, keepdims=True)
            o = contract(vt[:, keys], e.astype(BF), 1, 0) * (1.0 / total)
            ht[n, :, at] = o.astype(BF)
            lse[pl.ds(n, 1), at] = top + jnp.log(total)
            return carry

        lax.fori_loop(0, 4, head, 0)
        block = ht[:, :, at].reshape(256, QB)
        for b in range(4):
            cols = slice(b * 512, (b + 1) * 512)
            o = contract(block, o2[:, cols], 0, 0).astype(BF)
            part[i, 0, :, cols] = o[:SLAB]
            part[i, 1, :, cols] = o[SLAB:]
        s.after_block(t)
        if t == 1:
            cg.s4()
    exports += [w.copy(ht, ht_out), w.copy(lse, lse_out)]
    s.wait()
    slab = pl.ds(pl.multiple_of(p.r * SLAB, SLAB), SLAB)
    for c in COLS:
        after[:, c] = h[slab, c].astype(F32) + RES * s.total(c)
    inv = norm_scale(lambda c: after[:, c])
    for c in COLS:
        normed[:, c] = (after[:, c] * inv * gain[1:2, c]).astype(BF)
    g = LineGather(w, normed, n2_out)
    g.s1()
    exports.append(w.copy(after, after_out))
    for b in big:
        b.s4()
    g.s2()
    g.s3()
    cg.s5()
    for b in big:
        b.s5()
    g.s4()
    for cp in exports:
        cp.wait()
    w.drain()


def call_first(hidden, cot, wq, wo, gate, up, down, gains, seg_cols, seg_rows, freq):
    n = 190
    weights = [((2, 4, 2, 256, 192), BF), ((2, 4, 2, 128, 256), BF)]
    shapes = [
        ((T, D), BF),
        ((2, 4, 2, 256, 512), BF), ((2, 4, 2, 256, 512), BF), ((2, 4, 2, 512, 256), BF),
        *weights,
        ((T, D), BF), ((SLAB, D), BF),
        ((4, HEAD, T), BF), ((HEAD, T), BF), ((HEAD, T), BF), ((4, HEAD, T), BF),
        ((8, T), F32), ((SLAB, D), F32), ((4, 2, SLAB, D), BF),
        ((8, D), F32), ((32, T), F32), ((32, T), F32),
        *weights,
    ]
    out_specs = [ANY] * 15 + [VM] * 3 + [ANY] * 2
    scratch = [
        pltpu.SemaphoreType.DMA((n,)), pltpu.SemaphoreType.DMA((n,)),
        pltpu.VMEM((T, D), BF), pltpu.VMEM((T, D), BF),
        pltpu.VMEM((2, D, 192), BF), pltpu.VMEM((256, D), BF),
        pltpu.VMEM((4, HEAD, T), BF), pltpu.VMEM((HEAD, T), BF), pltpu.VMEM((HEAD, T), BF),
        pltpu.VMEM((4, HEAD, T), BF), pltpu.VMEM((4, 2, SLAB, D), BF),
        *LineSum.SCRATCH,
        pltpu.VMEM((SLAB, D), F32), pltpu.VMEM((SLAB, D), BF),
        pltpu.VMEM((8, D), F32), pltpu.VMEM((T, 1), jnp.int32), pltpu.VMEM((1, T), jnp.int32),
        pltpu.VMEM((32, T), F32), pltpu.VMEM((32, T), F32), pltpu.VMEM((3 * QB, QB), F32),
        pltpu.VMEM((8, T), F32),
    ]
    return pl.pallas_call(
        first_kernel,
        out_shape=[jax.ShapeDtypeStruct(s, d) for s, d in shapes],
        in_specs=[ANY] * 7 + [VM] * 4,
        out_specs=out_specs,
        scratch_shapes=scratch,
        compiler_params=pltpu.CompilerParams(
            collective_id=0, has_side_effects=True, vmem_limit_bytes=48 << 20
        ),
        name="first",
    )(hidden, cot, wq, wo, gate, up, down, gains, seg_cols, seg_rows, freq)[:18]


class WeightSum:
    @staticmethod
    def scratch(rows, cols):
        h = rows // 2
        return [
            pltpu.VMEM((2, 4, h, cols), BF),
            pltpu.VMEM((2, 4, rows, cols), BF),
            pltpu.VMEM((2, h, cols), BF),
            pltpu.VMEM((2, rows, cols), BF),
        ]

    def __init__(self, wire, part, out, start, rows, order, far, came, far2, came2):
        self.w, self.part, self.out = wire, part, out
        self.r0, self.n = start, rows
        self.a1, self.a2 = ("y", "x") if order == 0 else ("x", "y")
        self.far, self.came, self.far2, self.came2 = far, came, far2, came2

    def span(self, half):
        if half is None:
            return pl.ds(self.r0, self.n)
        return pl.ds(self.r0 + half * (self.n // 2), self.n // 2)

    def src(self, k, j, half=None):
        p = self.w.place
        if self.a1 == "y":
            y = p.pos("y", k)
            return self.part.at[y // 2, j, lax.rem(y, 2), self.span(half)]
        return self.part.at[j // 2, p.pos("x", k), lax.rem(j, 2), self.span(half)]

    def four(self, k, half=None, part=None):
        p = self.w.place
        part = self.part if part is None else part
        if self.a1 == "y":
            y = p.pos("y", k)
            return part.at[y // 2, :, lax.rem(y, 2), self.span(half)]
        return part.at[:, p.pos("x", k), :, self.span(half)]

    def land(self, ref, i):
        if self.a1 == "y":
            return ref.at[i]
        return ref.reshape(2, 2, 2, *ref.shape[2:]).at[i]

    def s1(self, part=None):
        w, p = self.w, self.w.place
        self.up = w.send(self.four(2, 0, part), self.land(self.far, 0), p.step(self.a1, 1))
        self.down = w.send(self.four(2, 1, part), self.land(self.far, 1), p.step(self.a1, -1))

    def s2(self):
        w, p = self.w, self.w.place
        h = self.n // 2
        self.up.wait_recv()
        for j in range(4):
            a = self.src(1, j, 0)
            add_rows(a, [a, self.far.at[0, j]], h)
        self.up2 = w.send(self.four(1), self.land(self.came, 0), p.step(self.a1, 1))
        self.down.wait_recv()
        for j in range(4):
            a = self.src(-1, j, 1)
            add_rows(a, [a, self.far.at[1, j]], h)
        self.down2 = w.send(self.four(-1), self.land(self.came, 1), p.step(self.a1, -1))

    def s3(self):
        w, p = self.w, self.w.place
        self.up2.wait_recv()
        self.down2.wait_recv()
        for k in (2, 1, -1, 0):
            j = p.pos(self.a2, k)
            a = self.src(0, j)
            add_rows(a, [a, self.came.at[0, j], self.came.at[1, j]], self.n)
            if k == 2:
                self.up3 = w.send(self.src(0, j, 0), self.far2.at[0], p.step(self.a2, 1))
                self.down3 = w.send(self.src(0, j, 1), self.far2.at[1], p.step(self.a2, -1))

    def s4(self):
        w, p = self.w, self.w.place
        h = self.n // 2
        self.up3.wait_recv()
        j = p.pos(self.a2, 1)
        a = self.src(0, j, 0)
        add_rows(a, [a, self.far2.at[0]], h)
        self.up4 = w.send(self.src(0, j), self.came2.at[0], p.step(self.a2, 1))
        self.down3.wait_recv()
        j = p.pos(self.a2, -1)
        a = self.src(0, j, 1)
        add_rows(a, [a, self.far2.at[1]], h)
        self.down4 = w.send(self.src(0, j), self.came2.at[1], p.step(self.a2, -1))

    def s5(self):
        self.up4.wait_recv()
        self.down4.wait_recv()
        j = self.w.place.pos(self.a2, 0)
        add_rows(
            self.out.at[pl.ds(self.r0, self.n)],
            [self.src(0, j), self.came2.at[0], self.came2.at[1]],
            self.n,
        )


def second_kernel(
    n2_in, cot_in, g_in, u_in, d_in, after_in, gain_in,
    attn_out, grad_after, gain_part, out_cols, o_down, gg_out, gu_out,
    send, recv, n2, cot, gw, uw, dw, ha, ggp, gup, gd, pf, pg, attn, outs, after, gain, slab, *sc,
):
    p = Place()
    w = Wire(p, send, recv)
    rows = row_peers(p)
    greet(ring_peers(p) + [dev for _, _, _, dev in rows])
    l_n2 = w.copy(n2_in, n2)
    l_g = w.copy(g_in, gw)
    l_u = w.copy(u_in, uw)
    l_c = w.copy(cot_in, cot)
    l_d = [
        w.copy(d_in.at[j, g], dw.at[j, :, pl.ds(g * 256, 256)]) for j in range(2) for g in range(8)
    ]
    l_s = [
        w.copy(after_in, after), w.copy(gain_in, gain),
        w.copy(cot_in.at[pl.ds(pl.multiple_of(p.r * SLAB, SLAB), SLAB)], slab),
    ]
    f = LineSum(w, pf, *sc[0:3])
    s = LineSum(w, pg, *sc[3:6])
    sums = [
        WeightSum(w, gd, o_down, 0, 256, 0, *sc[6:10]),
        WeightSum(w, gd, o_down, 256, 256, 1, *sc[10:14]),
    ]
    l_n2.wait()
    l_g.wait()
    l_u.wait()
    l_c.wait()
    for cp in l_d:
        cp.wait()
    for t, k in enumerate(LineSum.ORDER):
        i = p.pos("z", k)
        at = rows_of(i, QB)

        def units(j, carry):
            gate = contract(n2[at], gw[j], 1, 0)
            upp = contract(n2[at], uw[j], 1, 0)
            ga = (RES * contract(cot[at], dw[j], 1, 1)).astype(BF).astype(F32)
            sig = 1.0 / (1.0 + jnp.exp(-gate))
            act = gate * sig
            ha[j, at] = (act * upp).astype(BF)
            ggp[j, at] = (ga * upp * sig * (1.0 + gate * (1.0 - sig))).astype(BF)
            gup[j, at] = (ga * act).astype(BF)
            return carry

        lax.fori_loop(0, 2, units, 0)
        for b in range(4):
            cols = slice(b * 512, (b + 1) * 512)
            o = (contract(ha[0, at], dw[0, :, cols], 1, 0) + contract(ha[1, at], dw[1, :, cols], 1, 0)).astype(BF)
            pf[i, 0, :, cols] = o[:SLAB]
            pf[i, 1, :, cols] = o[SLAB:]
        f.after_block(t)
    for t, k in enumerate(LineSum.ORDER):
        i = p.pos("z", k)
        at = rows_of(i, QB)
        for b in range(4):
            cols = slice(b * 512, (b + 1) * 512)
            o = contract(ggp[0, at], gw[0, cols], 1, 1) + contract(gup[0, at], uw[0, cols], 1, 1)
            o = o + contract(ggp[1, at], gw[1, cols], 1, 1) + contract(gup[1, at], uw[1, cols], 1, 1)
            o = o.astype(BF)
            pg[i, 0, :, cols] = o[:SLAB]
            pg[i, 1, :, cols] = o[SLAB:]
        s.after_block(t)

    def down_grad(g, carry):
        at = rows_of(g, 256)
        for j in range(2):
            gd[j, g // 2, lax.rem(g, 2)] = (RES * contract(ha[j], cot[:, at], 0, 0)).astype(BF)
        return carry

    lax.fori_loop(0, 8, down_grad, 0)
    for b in sums:
        b.s1()

    def in_grad(g, carry):
        at = rows_of(g, 256)
        for j in range(2):
            gw[j, at] = contract(n2[:, at], ggp[j], 0, 0).astype(BF)
            uw[j, at] = contract(n2[:, at], gup[j], 0, 0).astype(BF)
        return carry

    lax.fori_loop(0, 4, in_grad, 0)
    for b in sums:
        b.s2()
    lax.fori_loop(4, 8, in_grad, 0)
    e_g = w.copy(gw, gg_out)
    e_u = w.copy(uw, gu_out)
    for cp in l_s:
        cp.wait()
    s.wait()
    inv = norm_scale(lambda c: after[:, c])
    total = None
    for c in COLS:
        g = s.total(c)
        scaled = after[:, c] * inv
        gs = g * scaled
        gain_part[:, c] = jnp.sum(gs.reshape(SLAB // 8, 8, 128), axis=0)
        e = gs * gain[1:2, c]
        total = e if total is None else total + e
    inner = jnp.sum(total, axis=1, keepdims=True) * (1.0 / D)
    for c in COLS:
        e = s.total(c) * gain[1:2, c]
        v = slab[:, c].astype(F32) + inv * (e - after[:, c] * inv * inner)
        grad_after[:, c] = v
        attn[:, c] = (RES * v).astype(BF)
    a = LineGather(w, attn, attn_out)
    a.s1()
    f.wait()
    for c in COLS:
        outs[:, c] = (after[:, c] + RES * f.total(c)).astype(BF)
    o = Scatter(w, outs, out_cols, rows)
    o.s1()
    for b in sums:
        b.s3()
    a.s2()
    a.s3()
    for b in sums:
        b.s4()
    for b in sums:
        b.s5()
    a.s4()
    o.s2()
    e_g.wait()
    e_u.wait()
    w.drain()


def call_second(n2, cot, g, u, d, after, gain):
    n = 120
    scratch = [
        pltpu.SemaphoreType.DMA((n,)), pltpu.SemaphoreType.DMA((n,)),
        pltpu.VMEM((T, D), BF), pltpu.VMEM((T, D), BF),
        pltpu.VMEM((2, D, 512), BF), pltpu.VMEM((2, D, 512), BF), pltpu.VMEM((2, 512, D), BF),
        pltpu.VMEM((2, T, 512), BF), pltpu.VMEM((2, T, 512), BF), pltpu.VMEM((2, T, 512), BF),
        pltpu.VMEM((2, 4, 2, 512, 256), BF),
        pltpu.VMEM((4, 2, SLAB, D), BF), pltpu.VMEM((4, 2, SLAB, D), BF),
        pltpu.VMEM((SLAB, D), BF), pltpu.VMEM((SLAB, D), BF), pltpu.VMEM((SLAB, D), F32),
        pltpu.VMEM((8, D), F32), pltpu.VMEM((SLAB, D), BF),
    ]
    scratch += LineSum.SCRATCH * 2
    scratch += WeightSum.scratch(256, 256) * 2
    return pl.pallas_call(
        second_kernel,
        out_shape=[
            jax.ShapeDtypeStruct((4, 2, SLAB, D), BF),
            jax.ShapeDtypeStruct((SLAB, D), F32),
            jax.ShapeDtypeStruct((8, D), F32),
            jax.ShapeDtypeStruct((2 * T, 128), BF),
            jax.ShapeDtypeStruct((512, 256), F32),
            jax.ShapeDtypeStruct((2, D, 512), BF),
            jax.ShapeDtypeStruct((2, D, 512), BF),
        ],
        in_specs=[ANY] * 7,
        out_specs=[ANY, VM, VM, ANY, VM, ANY, ANY],
        scratch_shapes=scratch,
        compiler_params=pltpu.CompilerParams(
            collective_id=1, has_side_effects=True, vmem_limit_bytes=62 << 20
        ),
        name="second",
    )(n2, cot, g, u, d, after, gain)


def key_range(i):
    return max(0, (i - 2) * QB), (i + 1) * QB


def third_kernel(
    ga_in, hid, grad_after, gain, gain_two, w2_in, o_in, n1_in, qt, kt, vt, ht, lse,
    cos, sin, seg_cols, seg_rows, gg_in, gu_in,
    hid_cols, o_gain, o_q, o_o, o_gate, o_up,
    send, recv, ga, n1, w2, o2, ght, gt, gn, gk, gv, bias, seg_col, seg_row,
    part, got, far, near, outs, gains, gcame, gsum, gcame2, tq, to, rq, ro, gg, gu, *sc,
):
    p = Place()
    w = Wire(p, send, recv)
    rows = row_peers(p)
    lanes = [(k, (lax.rem(p.gx + k, 8), p.gy)) for k in range(1, 8)]
    greet([dev for _, _, _, dev in rows] + [dev for _, dev in lanes] + [p.at(y=1), p.at(y=-1)])
    big = []
    k = 0
    for src, part_, out, n, order in (
        (gg_in, gg, o_gate, 128, 0), (gg_in, gg, o_gate, 128, 1),
        (gu_in, gu, o_up, 128, 0), (gu_in, gu, o_up, 128, 1),
    ):
        big.append((WeightSum(w, part_, out, order * 128, n, order, *sc[k : k + 4]), src))
        k += 4
    sq = WeightSum(w, rq, o_q, 0, 256, 0, *sc[k : k + 4])
    so = WeightSum(w, ro, o_o, 0, 128, 1, *sc[k + 4 : k + 8])
    for b, src in big:
        b.s1(src)
    l_ga = w.copy(ga_in, ga)
    l_o = [
        w.copy(o_in.at[j, g // 2, g % 2], o2.at[pl.ds(j * 128, 128), pl.ds(g * 256, 256)])
        for j in range(2)
        for g in range(8)
    ]
    l_big = [w.copy(gg_in, gg), w.copy(gu_in, gu)]
    l_n1 = w.copy(n1_in, n1)
    l_w2 = [w.copy(w2_in.at[j], w2.at[j].reshape(4, 2, 256, 192)) for j in range(2)]
    seg_row[...] = jnp.where(p.yh == 0, seg_rows[0:1], seg_rows[1:2])
    seg_col[...] = jnp.where(p.yh == 0, seg_cols[:, 0:1], seg_cols[:, 1:2])
    gk[...] = jnp.zeros_like(gk)
    gv[...] = jnp.zeros_like(gv)
    gt[:, 192:] = jnp.zeros((2, 64, T), BF)
    l_ga.wait()
    for cp in l_o:
        cp.wait()

    def heads_grad(i, carry):
        at = rows_of(i, QB)
        ght[:, :, at] = contract(o2[...], ga[at], 1, 1).astype(BF).reshape(4, HEAD, QB)
        return carry

    lax.fori_loop(0, 4, heads_grad, 0)

    def out_grad(dst, j):
        hj = ht[pl.ds(j * 2, 2)].reshape(128, T)
        for g in range(8):
            dst[g // 2, g % 2] = contract(hj, ga[:, g * 256 : (g + 1) * 256], 1, 0).astype(BF)

    out_grad(to, 1 - p.c)
    swap_o = w.send(to, ro.at[p.c], p.at(c=1))
    out_grad(ro.at[p.c], p.c)
    for i in range(4):
        lo, hi = key_range(i)
        at = slice(i * QB, (i + 1) * QB)
        bias[: hi - lo] = bias_tile(seg_col, seg_row, lo, hi - lo, i)

        def head(n, carry):
            q = qt[n, :, at]
            g = ght[n, :, at]
            sc_ = contract(kt[:, lo:hi], q, 0, 0) + bias[: hi - lo]
            pr = jnp.exp(sc_ - lse[pl.ds(n, 1), at])
            gp = contract(vt[:, lo:hi], g, 0, 0)
            inner = jnp.sum(ht[n, :, at].astype(F32) * g.astype(F32), axis=0, keepdims=True)
            gs = (pr * (gp - inner)).astype(BF)
            gq = contract(kt[:, lo:hi], gs, 1, 0) * ATTN_SCALE
            a, b = gq[:32], gq[32:]
            first = pl.multiple_of(lax.rem(n, 2) * 64, 64)
            gt[n // 2, pl.ds(first, 32), at] = (a * cos[:, at] + b * sin[:, at]).astype(BF)
            gt[n // 2, pl.ds(first + 32, 32), at] = (b * cos[:, at] - a * sin[:, at]).astype(BF)
            gk[:, lo:hi] += contract(q, gs, 1, 1)
            gv[:, lo:hi] += contract(g, pr.astype(BF), 1, 1)
            return carry

        lax.fori_loop(0, 4, head, 0)
        if i == 1:
            for cp in l_big:
                cp.wait()
            for b, _ in big:
                b.s2()
    a, b = gk[:32], gk[32:]
    gt[0, 128:160] = (a * cos[...] + b * sin[...]).astype(BF)
    gt[1, 128:160] = (b * cos[...] - a * sin[...]).astype(BF)
    gt[0, 160:192] = gv[:32].astype(BF)
    gt[1, 160:192] = gv[32:].astype(BF)
    for j in range(2):
        for i in range(4):
            gn[j, i * QB : (i + 1) * QB] = gt[j, :, i * QB : (i + 1) * QB].T
    for cp in l_w2:
        cp.wait()
    s = LineSum(w, part, got, far, near)
    for t, k in enumerate(LineSum.ORDER):
        i = p.pos("z", k)
        at = rows_of(i, QB)
        for b in range(4):
            cols = slice(b * 512, (b + 1) * 512)
            o = contract(gn[0, at, :192], w2[0, cols], 1, 1) + contract(gn[1, at, :192], w2[1, cols], 1, 1)
            o = o.astype(BF)
            part[i, 0, :, cols] = o[:SLAB]
            part[i, 1, :, cols] = o[SLAB:]
        s.after_block(t)
    l_n1.wait()

    def in_grad(dst, j):
        def body(g, carry):
            dst[g // 2, lax.rem(g, 2)] = contract(n1[:, rows_of(g, 256)], gn[j, :, :192], 0, 0).astype(BF)
            return carry

        lax.fori_loop(0, 8, body, 0)

    in_grad(tq, 1 - p.c)
    swap_q = w.send(tq, rq.at[p.c], p.at(c=1))
    in_grad(rq.at[p.c], p.c)
    swap_o.wait_recv()
    so.s1()
    swap_q.wait_recv()
    sq.s1()
    for b, _ in big:
        b.s3()
    s.wait()
    inv = norm_scale(lambda c: hid[:, c].astype(F32))
    total = None
    for c in COLS:
        g = s.total(c)
        scaled = hid[:, c].astype(F32) * inv
        gs = g * scaled
        gains[0, :, c] = jnp.sum(gs.reshape(SLAB // 8, 8, 128), axis=0)
        e = gs * gain[0:1, c]
        total = e if total is None else total + e
    inner = jnp.sum(total, axis=1, keepdims=True) * (1.0 / D)
    for c in COLS:
        e = s.total(c) * gain[0:1, c]
        v = grad_after[:, c] + inv * (e - hid[:, c].astype(F32) * inv * inner)
        outs[:, c] = v.astype(BF)
    o = Scatter(w, outs, hid_cols, rows)
    o.s1()
    gains[1] = gain_two[...]
    mine = pl.ds(pl.multiple_of(p.gy * 128, 128), 128)
    gcp = []
    for _, _, _, dev in rows:
        at = pl.ds(pl.multiple_of(dev[1] * 128, 128), 128)
        gcp.append(w.send(gains.at[:, :, at], gcame.at[p.gy], dev))
    glocal = w.copy(gains.at[:, :, mine], gcame.at[p.gy])
    so.s2()
    sq.s2()
    for b, _ in big:
        b.s4()
    for cp in gcp:
        cp.wait_recv()
    glocal.wait()
    gsum[...] = jnp.sum(gcame[...], axis=0)
    lcp = [w.send(gsum, gcame2.at[p.gx], dev) for _, dev in lanes]
    llocal = w.copy(gsum, gcame2.at[p.gx])
    so.s3()
    sq.s3()
    for b, _ in big:
        b.s5()
    so.s4()
    sq.s4()
    so.s5()
    sq.s5()
    for cp in lcp:
        cp.wait_recv()
    llocal.wait()
    o_gain[...] = jnp.sum(gcame2[...], axis=0)
    o.s2()
    w.drain()


def call_third(*args):
    n = 160
    scratch = [
        pltpu.SemaphoreType.DMA((n,)), pltpu.SemaphoreType.DMA((n,)),
        pltpu.VMEM((T, D), BF), pltpu.VMEM((T, D), BF),
        pltpu.VMEM((2, D, 192), BF), pltpu.VMEM((256, D), BF),
        pltpu.VMEM((4, HEAD, T), BF), pltpu.VMEM((2, 256, T), BF), pltpu.VMEM((2, T, 256), BF),
        pltpu.VMEM((HEAD, T), F32), pltpu.VMEM((HEAD, T), F32), pltpu.VMEM((3 * QB, QB), F32),
        pltpu.VMEM((T, 1), jnp.int32), pltpu.VMEM((1, T), jnp.int32),
        pltpu.VMEM((4, 2, SLAB, D), BF),
        *LineSum.SCRATCH,
        pltpu.VMEM((SLAB, D), BF),
        pltpu.VMEM((2, 8, D), F32),
        pltpu.VMEM((16, 2, 8, 128), F32),
        pltpu.VMEM((2, 8, 128), F32),
        pltpu.VMEM((8, 2, 8, 128), F32),
        pltpu.VMEM((4, 2, 256, 192), BF),
        pltpu.VMEM((4, 2, 128, 256), BF),
        pltpu.VMEM((2, 4, 2, 256, 192), BF),
        pltpu.VMEM((2, 4, 2, 128, 256), BF),
        pltpu.VMEM((2, 4, 2, 256, 512), BF),
        pltpu.VMEM((2, 4, 2, 256, 512), BF),
    ]
    scratch += WeightSum.scratch(128, 512) * 4
    scratch += WeightSum.scratch(256, 192) + WeightSum.scratch(128, 256)
    return pl.pallas_call(
        third_kernel,
        out_shape=[
            jax.ShapeDtypeStruct((2 * T, 128), BF),
            jax.ShapeDtypeStruct((2, 8, 128), F32),
            jax.ShapeDtypeStruct((256, 192), F32),
            jax.ShapeDtypeStruct((128, 256), F32),
            jax.ShapeDtypeStruct((256, 512), F32),
            jax.ShapeDtypeStruct((256, 512), F32),
        ],
        in_specs=[ANY, VM, VM, VM, VM, ANY, ANY, ANY] + [VM] * 9 + [ANY, ANY],
        out_specs=[ANY, VM, VM, VM, VM, VM],
        scratch_shapes=scratch,
        compiler_params=pltpu.CompilerParams(
            collective_id=2, has_side_effects=True, vmem_limit_bytes=62 << 20
        ),
        name="third",
    )(*args)


def per_device(
    hidden, attn_gain, wq, wk, wv, wo, ffn_gain, gate, up, down, segments, cotangent,
):
    gains = jnp.zeros((8, 128), F32).at[0].set(attn_gain).at[1].set(ffn_gain)
    wqkv = jnp.concatenate([wq, wk, wv], axis=1)
    freq = (ROPE_BASE ** (-jnp.arange(0, HEAD, 2, dtype=F32) / HEAD))[:, None]
    seg_cols = segments.T
    (
        cot, gg, uu, dd, aq, ao, n1, hid_slab, qt, kt, vt, ht, lse, after, n2, gain, cos, sin
    ) = call_first(hidden, cotangent, wqkv, wo, gate, up, down, gains, seg_cols, segments, freq)
    grad_attn, grad_after, gain_two, out_cols, o_down, g_gate, g_up = call_second(
        n2.reshape(T, D), cot, gg.reshape(2, D, 512), uu.reshape(2, D, 512),
        dd.reshape(2, 8, 512, 256), after, gain,
    )
    hid_cols, o_gain, o_qkv, o_o, o_gate, o_up = call_third(
        grad_attn.reshape(T, D), hid_slab, grad_after, gain, gain_two, aq, ao, n1,
        qt, kt, vt, ht, lse, cos, sin, seg_cols, segments,
        g_gate.reshape(2, 4, 2, 256, 512), g_up.reshape(2, 4, 2, 256, 512),
    )
    both = jnp.sum(o_gain, axis=1)
    return (
        out_cols.astype(F32),
        hid_cols.astype(F32),
        both[0],
        o_qkv[:, :128],
        o_qkv[:, 128:160],
        o_qkv[:, 160:],
        o_o,
        both[1],
        o_gate,
        o_up,
        o_down,
    )


def solution(mesh):
    wide, cols, tall = P("gx", "gy"), P("gy"), P("gy", "gx")
    return jax.shard_map(
        per_device,
        mesh=mesh,
        in_specs=(wide, cols, wide, wide, wide, tall, cols, wide, wide, tall, P("gx", None), wide),
        out_specs=(wide, wide, cols, wide, wide, wide, tall, cols, wide, wide, tall),
        check_vma=False,
    )
```

```python
import functools

import jax
import jax.numpy as jnp
from jax import lax
from jax.experimental import pallas as pl
from jax.experimental.pallas import tpu as pltpu
from jax.sharding import PartitionSpec as P

HEAD = 64
EPS = 1e-06
ROPE_BASE = 10000000.0
ATTN_SCALE = 1.0 / 64.0
RES = 0.22
T = 1024
D = 2048
SLAB = 128
QB = 256
BF = jnp.bfloat16
F32 = jnp.float32
MESH = pl.DeviceIdType.MESH
ANY = pl.BlockSpec(memory_space=pl.ANY)
VM = pl.BlockSpec(memory_space=pltpu.VMEM)


class Place:
    def __init__(self):
        gx = lax.axis_index("gx")
        gy = lax.axis_index("gy")
        self.gx, self.gy = gx, gy
        self.x, self.yl = gx // 2, lax.rem(gx, 2)
        self.yh, self.z, self.c = gy // 8, lax.rem(gy // 2, 4), lax.rem(gy, 2)
        self.y = self.yh * 2 + self.yl
        self.r = self.z * 2 + self.c

    def at(self, x=0, y=0, z=0, c=0):
        xx = lax.rem(self.x + x + 4, 4)
        yy = lax.rem(self.y + y + 4, 4)
        zz = lax.rem(self.z + z + 4, 4)
        cc = lax.rem(self.c + c, 2)
        return (xx * 2 + lax.rem(yy, 2), (yy // 2) * 8 + zz * 2 + cc)

    def step(self, axis, k):
        return self.at(**{axis: k})

    def pos(self, axis, k):
        return lax.rem(getattr(self, axis) + k + 4, 4)


class Wire:
    def __init__(self, place, send, recv):
        self.place, self.send_sem, self.recv_sem = place, send, recv
        self.starts, self.lands = 0, 0
        self.sent = []

    def send(self, src, dst, to):
        i, j = self.starts, self.lands
        self.starts, self.lands = i + 1, j + 1
        cp = pltpu.make_async_remote_copy(
            src_ref=src,
            dst_ref=dst,
            send_sem=self.send_sem.at[i],
            recv_sem=self.recv_sem.at[j],
            device_id=to,
            device_id_type=MESH,
        )
        cp.start()
        self.sent.append(cp)
        return cp

    def copy(self, src, dst):
        i = self.starts
        self.starts += 1
        cp = pltpu.make_async_copy(src, dst, self.send_sem.at[i])
        cp.start()
        return cp

    def drain(self):
        for cp in self.sent:
            cp.wait_send()
        self.sent = []


def greet(peers):
    barrier = pltpu.get_barrier_semaphore()
    for peer in peers:
        pl.semaphore_signal(barrier, inc=1, device_id=peer, device_id_type=MESH)
    pl.semaphore_wait(barrier, len(peers))


def ring_peers(p):
    return [p.at(x=1), p.at(x=-1), p.at(y=1), p.at(y=-1)]


def row_peers(p):
    out = []
    for y in (0, 2):
        for z in range(4):
            for c in range(2):
                if (y, z, c) != (0, 0, 0):
                    out.append((y, z, c, p.at(y=y, z=z, c=c)))
    return out


def line_peers(p):
    return [p.at(c=1), p.at(z=1), p.at(z=-1)]


class WeightGather:
    def __init__(self, wire, src, dst, start, rows, order, stage=None):
        self.w, self.src, self.dst, self.stage = wire, src, dst, stage
        self.r0, self.n, self.order = start, rows, order
        self.a1, self.a2 = ("x", "y") if order == 0 else ("y", "x")

    def one(self, k, half=None):
        p = self.w.place
        x, y = (p.pos("x", k), p.y) if self.a1 == "x" else (p.x, p.pos("y", k))
        return self.dst.at[y // 2, x, lax.rem(y, 2), self.span(half)]

    def four(self, k, half=None):
        p = self.w.place
        if self.a2 == "y":
            y = p.pos("y", k)
            return self.dst.at[y // 2, :, lax.rem(y, 2), self.span(half)]
        return self.dst.at[:, p.pos("x", k), :, self.span(half)]

    def span(self, half):
        if half is None:
            return pl.ds(self.r0, self.n)
        return pl.ds(self.r0 + half * (self.n // 2), self.n // 2)

    def s1(self):
        w, p = self.w, self.w.place
        own = self.src.at[pl.ds(self.r0, self.n)]
        if self.stage is None:
            self.local = w.copy(own, self.one(0))
        else:
            self.local = w.copy(own, self.stage.at[pl.ds(self.r0, self.n)])
        self.up = w.send(own, self.one(0), p.step(self.a1, 1))
        self.down = w.send(own, self.one(0), p.step(self.a1, -1))

    def s2(self):
        w, p = self.w, self.w.place
        if self.stage is not None:
            self.local.wait()
            self.local = w.copy(self.stage.at[pl.ds(self.r0, self.n)], self.one(0))
        self.up.wait_recv()
        self.up2 = w.send(self.one(-1, 0), self.one(-1, 0), p.step(self.a1, 1))
        self.down.wait_recv()
        self.down2 = w.send(self.one(1, 1), self.one(1, 1), p.step(self.a1, -1))

    def s3(self):
        w, p = self.w, self.w.place
        self.local.wait()
        self.up2.wait_recv()
        self.down2.wait_recv()
        self.up3 = w.send(self.four(0), self.four(0), p.step(self.a2, 1))
        self.down3 = w.send(self.four(0), self.four(0), p.step(self.a2, -1))

    def s4(self):
        w, p = self.w, self.w.place
        self.up3.wait_recv()
        self.up4 = w.send(self.four(-1, 0), self.four(-1, 0), p.step(self.a2, 1))
        self.down3.wait_recv()
        self.down4 = w.send(self.four(1, 1), self.four(1, 1), p.step(self.a2, -1))

    def s5(self):
        self.up4.wait_recv()
        self.down4.wait_recv()


class RowGather:
    def __init__(self, wire, src, dst, stage=None):
        self.w, self.src, self.dst, self.stage = wire, src, dst, stage

    def block(self, yh, k, c=None):
        p = self.w.place
        c = p.c if c is None else c
        gy = yh * 8 + p.pos("z", k) * 2 + c
        return self.dst.at[:, pl.ds(pl.multiple_of(gy * 128, 128), 128)]

    def out(self, src, yh, k):
        b = self.block(yh, k)
        self.cores.append(self.w.send(src, b, self.w.place.at(c=1)))

    def s1(self):
        w, p = self.w, self.w.place
        self.cores = []
        mine = self.src.at[pl.ds(pl.multiple_of(p.yh * T, T), T)]
        other = self.src.at[pl.ds(pl.multiple_of((1 - p.yh) * T, T), T)]
        own = self.block(p.yh, 0)
        self.local = w.copy(mine, own if self.stage is None else self.stage)
        self.swap = w.send(other, own, p.at(y=2))
        self.up0 = w.send(mine, own, p.at(z=1))
        self.down0 = w.send(mine, own, p.at(z=-1))
        self.out(mine, p.yh, 0)

    def s2(self):
        w, p = self.w, self.w.place
        if self.stage is not None:
            self.local.wait()
            self.local = w.copy(self.stage, self.block(p.yh, 0))
        self.swap.wait_recv()
        b = self.block(1 - p.yh, 0)
        self.up1 = w.send(b, b, p.at(z=1))
        self.down1 = w.send(b, b, p.at(z=-1))
        self.out(b, 1 - p.yh, 0)

    def s3(self):
        w, p = self.w, self.w.place
        self.up0.wait_recv()
        b = self.block(p.yh, -1)
        self.up2 = w.send(b, b, p.at(z=1))
        self.out(b, p.yh, -1)
        self.down0.wait_recv()
        self.out(self.block(p.yh, 1), p.yh, 1)
        self.down1.wait_recv()
        b = self.block(1 - p.yh, 1)
        self.down2 = w.send(b, b, p.at(z=-1))
        self.out(b, 1 - p.yh, 1)
        self.up1.wait_recv()
        self.out(self.block(1 - p.yh, -1), 1 - p.yh, -1)

    def s4(self):
        p = self.w.place
        self.up2.wait_recv()
        self.out(self.block(p.yh, 2), p.yh, 2)
        self.down2.wait_recv()
        self.out(self.block(1 - p.yh, 2), 1 - p.yh, 2)

    def s5(self):
        self.local.wait()
        for cp in self.cores:
            cp.wait_recv()


def add_rows(dst, srcs, rows):
    step = max(16, min(rows, 32768 // dst.shape[-1]))
    while rows % step:
        step //= 2

    def body(i, carry):
        at = pl.ds(pl.multiple_of(i * step, step), step)
        total = srcs[0][at].astype(F32)
        for v in srcs[1:]:
            total = total + v[at].astype(F32)
        dst[at] = total.astype(dst.dtype)
        return carry

    lax.fori_loop(0, rows // step, body, 0)


class LineSum:
    SCRATCH = [
        pltpu.VMEM((4, SLAB, D), BF),
        pltpu.VMEM((2, SLAB // 2, D), BF),
        pltpu.VMEM((2, SLAB, D), BF),
    ]
    ORDER = (2, 1, -1, 0)

    def __init__(self, wire, part, got, far, near):
        self.w, self.part, self.got = wire, part, got
        self.far, self.near = far, near
        self.core = {}
        self.last = []

    def mine(self, k, half=None):
        p = self.w.place
        if half is None:
            return self.part.at[p.pos("z", k), p.c]
        return self.part.at[p.pos("z", k), p.c, pl.ds(half * (SLAB // 2), SLAB // 2)]

    def push(self, k):
        w, p = self.w, self.w.place
        z = p.pos("z", k)
        self.core[k] = w.send(self.part.at[z, 1 - p.c], self.got.at[z], p.at(c=1))

    def merge(self, k):
        z = self.w.place.pos("z", k)
        self.core[k].wait_recv()
        add_rows(self.mine(k), [self.mine(k), self.got.at[z]], SLAB)

    def send_far(self):
        w, p = self.w, self.w.place
        self.up = w.send(self.mine(2, 0), self.far.at[0], p.at(z=1))
        self.down = w.send(self.mine(2, 1), self.far.at[1], p.at(z=-1))

    def near_first(self, i):
        self.near_half(1 if i == 0 else -1, i, 1 - i)

    def near_second(self, i):
        k, far = (1, self.up) if i == 0 else (-1, self.down)
        far.wait_recv()
        add_rows(self.mine(k, i), [self.mine(k, i), self.far.at[i]], SLAB // 2)
        self.near_half(k, i, i)

    def near_half(self, k, i, h):
        at = pl.ds(h * (SLAB // 2), SLAB // 2)
        self.last.append(self.w.send(self.mine(k, h), self.near.at[i, at], self.w.place.at(z=k)))

    def after_block(self, t):
        self.push(self.ORDER[t])
        if t == 1:
            self.merge(2)
            self.send_far()
        if t == 2:
            self.merge(1)
            self.near_first(0)
        if t == 3:
            self.merge(-1)
            self.near_first(1)
            self.merge(0)

    def finish(self):
        self.near_second(0)
        self.near_second(1)

    def wait(self):
        for cp in self.last:
            cp.wait_recv()

    def total(self, at):
        p = self.w.place
        return (
            self.part[p.z, p.c, :, at].astype(F32)
            + self.near[0, :, at].astype(F32)
            + self.near[1, :, at].astype(F32)
        )


class LineGather:
    def __init__(self, wire, src, dst):
        self.w, self.src, self.dst = wire, src, dst

    def slot(self, k, half=None):
        p = self.w.place
        if half is None:
            return self.dst.at[p.pos("z", k), p.c]
        return self.dst.at[p.pos("z", k), p.c, pl.ds(half * (SLAB // 2), SLAB // 2)]

    def s1(self):
        w, p = self.w, self.w.place
        self.up = w.send(self.src, self.slot(0), p.at(z=1))
        self.down = w.send(self.src, self.slot(0), p.at(z=-1))
        self.cores = [w.send(self.src, self.slot(0), p.at(c=1))]
        self.local = w.copy(self.src, self.slot(0))

    def s2(self):
        w, p = self.w, self.w.place
        self.up.wait_recv()
        self.up2 = w.send(self.slot(-1, 0), self.slot(-1, 0), p.at(z=1))
        self.cores.append(w.send(self.slot(-1), self.slot(-1), p.at(c=1)))
        self.down.wait_recv()
        self.down2 = w.send(self.slot(1, 1), self.slot(1, 1), p.at(z=-1))
        self.cores.append(w.send(self.slot(1), self.slot(1), p.at(c=1)))

    def s3(self):
        w, p = self.w, self.w.place
        self.up2.wait_recv()
        self.cores.append(w.send(self.slot(2, 0), self.slot(2, 0), p.at(c=1)))
        self.down2.wait_recv()
        self.cores.append(w.send(self.slot(2, 1), self.slot(2, 1), p.at(c=1)))

    def s4(self):
        self.local.wait()
        for cp in self.cores:
            cp.wait_recv()


class Scatter:
    def __init__(self, wire, src, dst, rows):
        self.w, self.src, self.dst, self.rows = wire, src, dst, rows

    def s1(self):
        w, p = self.w, self.w.place
        mine = self.dst.at[pl.ds(pl.multiple_of(p.yh * T + p.r * SLAB, SLAB), SLAB)]
        self.copies = []
        for y, z, c, dev in self.rows:
            at = pl.ds(pl.multiple_of(dev[1] * 128, 128), 128)
            self.copies.append(w.send(self.src.at[:, at], mine, dev))
        at = pl.ds(pl.multiple_of(p.gy * 128, 128), 128)
        self.local = w.copy(self.src.at[:, at], mine)

    def s2(self):
        self.local.wait()
        for cp in self.copies:
            cp.wait_recv()


def each_rows(rows, step, f):
    def body(i, carry):
        f(pl.ds(pl.multiple_of(i * step, step), step))
        return carry

    lax.fori_loop(0, rows // step, body, 0)


COLS = [slice(j * 128, (j + 1) * 128) for j in range(16)]


def contract(a, b, da, db):
    return lax.dot_general(a, b, (((da,), (db,)), ((), ())), preferred_element_type=F32)


def rows_of(i, n):
    return pl.ds(pl.multiple_of(i * n, n), n)


def row_mean(parts):
    total = parts[0]
    for v in parts[1:]:
        total = total + v
    return jnp.sum(total, axis=1, keepdims=True) * (1.0 / D)


def norm_scale(load):
    squares = []
    total = None
    for at in COLS:
        v = load(at)
        total = v * v if total is None else total + v * v
    return lax.rsqrt(jnp.sum(total, axis=1, keepdims=True) * (1.0 / D) + EPS)


def unpack(packed, wide):
    for g in range(8):
        src = packed.at[g // 2, g % 2]
        wide[g * 256 : (g + 1) * 256, :128] = src[:256]
        kv = src[256:]
        wide[g * 256 : g * 256 + 128, 128:192] = kv[:, :64]
        wide[g * 256 + 128 : (g + 1) * 256, 128:192] = kv[:, 64:]


def spread(blocks, wide, j):
    for g in range(8):
        wide[rows_of(j, 128), g * 256 : (g + 1) * 256] = blocks[g // 2, g % 2]


def key_window(i):
    return pl.multiple_of(jnp.maximum(i - 2, 0) * QB, QB)


def pick_segment(p, segs, seg_row, seg_col):
    row = jnp.where(p.yh == 0, segs[0:1], segs[1:2])
    seg_row[...] = row
    wide = jnp.broadcast_to(row.astype(F32), (128, T)).T
    seg_col[...] = wide[:, 0:1].astype(jnp.int32)


def bias_tile(seg_col, seg_row, lo, n, i):
    first = i * QB
    same = seg_col[pl.ds(lo, n)] == seg_row[:, pl.ds(first, QB)]
    rows = lo + lax.broadcasted_iota(jnp.int32, (n, QB), 0)
    cols = first + lax.broadcasted_iota(jnp.int32, (n, QB), 1)
    return jnp.where(same & (rows <= cols), 0.0, -1e30)


def first_kernel(
    hidden, cot, wq, wo, gate, up, down, gains, segs, freq,
    c_out, g_out, u_out, d_out, w2_out, o2_out, n1_out, slab_out, qt_out, kt_out, vt_out, ht_out,
    lse_out, after_out, n2_out, act_out, gain_out, cos_out, sin_out,
    send, recv, h, n1, q_tmp, o_tmp, q_got, o_got, w2, o2, qt, kt, vt, ht, part, got, far, near,
    after, normed, gain, seg_col, seg_row, cos, sin, bias, lse, v_cot, v_gate, v_up, v_down,
    dw, cv, act,
):
    p = Place()
    w = Wire(p, send, recv)
    rows = row_peers(p)
    greet(ring_peers(p) + [dev for _, _, _, dev in rows])
    hg = RowGather(w, hidden, h)
    cg = RowGather(w, cot, c_out, v_cot)
    aq = [WeightGather(w, wq, q_tmp, 192 * i, 192, i) for i in range(2)]
    ao = [WeightGather(w, wo, o_tmp, 64 * i, 64, i) for i in range(2)]
    gu = [WeightGather(w, gate, g_out, 0, 256, 0, v_gate), WeightGather(w, up, u_out, 0, 256, 1, v_up)]
    dn = [WeightGather(w, down, d_out, 256 * i, 256, i, v_down) for i in range(2)]

    def each(group, stage):
        for b in group:
            getattr(b, stage)()

    each(aq, "s1")
    hg.s1()
    each(ao, "s1")
    each(dn, "s1")
    own = pl.ds(pl.multiple_of(p.gy * 128, 128), 128)
    glocal = w.copy(gains, gain.at[:, own])
    gcopies = [w.send(gains, gain.at[:, own], dev) for _, _, _, dev in rows]

    pick_segment(p, segs, seg_row, seg_col)
    earlier = jnp.zeros((8, T), F32)
    for b in range(8):
        less = seg_col[b * 128 : (b + 1) * 128] < seg_row[...]
        earlier = earlier + jnp.sum(jnp.where(less, 1.0, 0.0).reshape(16, 8, T), axis=0)
    starts = jnp.sum(earlier, axis=0, keepdims=True)
    places = lax.broadcasted_iota(jnp.int32, (1, T), 1).astype(F32) - starts
    turned = freq[...] * places
    cos[...] = jnp.cos(turned)
    sin[...] = jnp.sin(turned)

    each(aq, "s2")
    each(aq, "s3")
    hg.s2()
    each(ao, "s2")
    each(dn, "s2")
    each(aq, "s4")
    each(ao, "s3")
    each(gu, "s1")
    hg.s3()
    each(aq, "s5")
    q_swap = w.send(q_tmp.at[1 - p.c], q_got, p.at(c=1))
    unpack(q_tmp.at[p.c], w2.at[p.c])
    hg.s4()
    cg.s1()
    q_swap.wait_recv()
    unpack(q_got, w2.at[1 - p.c])
    hg.s5()
    each(ao, "s4")
    glocal.wait()
    for cp in gcopies:
        cp.wait_recv()

    def project(i, carry):
        at = rows_of(i, QB)
        inv = norm_scale(lambda c: h[at, c].astype(F32))
        for c in COLS:
            n1[at, c] = (h[at, c].astype(F32) * inv * gain[0:1, c]).astype(BF)
        ct, st = cos[:, at], sin[:, at]
        keys = []
        for j in range(2):
            lin = contract(n1[at], w2[j, :, :192], 1, 0)
            qj = lin[:, :128].T
            kv = lin[:, 128:].T
            for hh in range(2):
                a, b = qj[hh * 64 : hh * 64 + 32], qj[hh * 64 + 32 : hh * 64 + 64]
                qt[2 * j + hh, 0:32, at] = (a * ct - b * st).astype(BF) * ATTN_SCALE
                qt[2 * j + hh, 32:64, at] = (b * ct + a * st).astype(BF) * ATTN_SCALE
            keys.append(kv[:32])
            vt[j * 32 : (j + 1) * 32, at] = kv[32:].astype(BF)
        a, b = keys
        kt[0:32, at] = (a * ct - b * st).astype(BF)
        kt[32:64, at] = (b * ct + a * st).astype(BF)
        return carry

    lax.fori_loop(0, 4, project, 0)
    exports = [
        w.copy(w2, w2_out),
        w.copy(n1, n1_out),
        w.copy(h.at[pl.ds(pl.multiple_of(p.r * SLAB, SLAB), SLAB)], slab_out),
        w.copy(qt, qt_out), w.copy(kt, kt_out), w.copy(vt, vt_out),
    ]
    each(dn, "s3")
    cg.s2()
    gain_out[...] = gain[...]
    cos_out[...] = cos[...]
    sin_out[...] = sin[...]
    s = LineSum(w, part, got, far, near)
    for t, k in enumerate(LineSum.ORDER):
        i = p.pos("z", k)
        lo = key_window(i)
        at = rows_of(i, QB)
        keys = pl.ds(lo, 3 * QB)
        bias[...] = bias_tile(seg_col, seg_row, lo, 3 * QB, pl.multiple_of(i, 1))

        def head(n, carry):
            sc = contract(kt[:, keys], qt[n, :, at], 0, 0) + bias[...]
            top = jnp.max(sc, axis=0, keepdims=True)
            e = jnp.exp(sc - top)
            total = jnp.sum(e, axis=0, keepdims=True)
            o = contract(vt[:, keys], e.astype(BF), 1, 0) * (1.0 / total)
            ht[n, :, at] = o.astype(BF)
            lse[pl.ds(n, 1), at] = top + jnp.log(total)
            return carry

        lax.fori_loop(0, 4, head, 0)
        if t == 0:
            each(ao, "s5")
            o_swap = w.send(o_tmp.at[1 - p.c], o_got, p.at(c=1))
            spread(o_tmp.at[p.c], o2, p.c)
            o_swap.wait_recv()
            spread(o_got, o2, 1 - p.c)
            exports.append(w.copy(o2, o2_out))
        block = ht[:, :, at].reshape(256, QB)
        for b in range(4):
            cols = slice(b * 512, (b + 1) * 512)
            o = contract(block, o2[:, cols], 0, 0).astype(BF)
            part[i, 0, :, cols] = o[:SLAB]
            part[i, 1, :, cols] = o[SLAB:]
        s.after_block(t)
        if t == 0:
            each(gu, "s2")
            cg.s3()
        if t == 1:
            each(dn, "s4")
        if t == 2:
            each(gu, "s3")
            cg.s4()
    exports += [w.copy(ht, ht_out), w.copy(lse, lse_out)]
    s.finish()
    each(dn, "s5")
    loads = [
        w.copy(d_out.at[j, g // 2, g % 2], dw.at[j, :, pl.ds(g * 256, 256)]) for j in range(2) for g in range(8)
    ]
    cg.s5()
    loads.append(w.copy(c_out, cv))
    for cp in loads:
        cp.wait()

    def act_grad(i, carry):
        at = rows_of(i, 512)
        for j in range(2):
            act[j, at] = (RES * contract(cv[at], dw[j], 1, 1)).astype(BF)
        return carry

    lax.fori_loop(0, 2, act_grad, 0)
    exports.append(w.copy(act, act_out))
    s.wait()
    slab = pl.ds(pl.multiple_of(p.r * SLAB, SLAB), SLAB)
    for c in COLS:
        after[:, c] = h[slab, c].astype(F32) + RES * s.total(c)
    inv = norm_scale(lambda c: after[:, c])
    for c in COLS:
        normed[:, c] = (after[:, c] * inv * gain[1:2, c]).astype(BF)
    g = LineGather(w, normed, n2_out)
    g.s1()
    exports.append(w.copy(after, after_out))
    each(gu, "s4")
    g.s2()
    g.s3()
    each(gu, "s5")
    g.s4()
    for cp in exports:
        cp.wait()
    w.drain()


def call_first(*args):
    shapes = [
        ((T, D), BF),
        ((2, 4, 2, 256, 512), BF), ((2, 4, 2, 256, 512), BF), ((2, 4, 2, 512, 256), BF),
        ((2, D, 256), BF), ((256, D), BF),
        ((T, D), BF), ((SLAB, D), BF),
        ((4, HEAD, T), BF), ((HEAD, T), BF), ((HEAD, T), BF), ((4, HEAD, T), BF),
        ((8, T), F32), ((SLAB, D), F32), ((4, 2, SLAB, D), BF), ((2, T, 512), BF),
        ((8, D), F32), ((32, T), F32), ((32, T), F32),
    ]
    out_specs = [ANY] * 16 + [VM] * 3
    scratch = [
        pltpu.SemaphoreType.DMA((175,)), pltpu.SemaphoreType.DMA((130,)),
        pltpu.VMEM((T, D), BF), pltpu.VMEM((T, D), BF),
        pltpu.VMEM((2, 4, 2, 384, 128), BF), pltpu.VMEM((2, 4, 2, 128, 256), BF),
        pltpu.VMEM((4, 2, 384, 128), BF), pltpu.VMEM((4, 2, 128, 256), BF),
        pltpu.VMEM((2, D, 256), BF), pltpu.VMEM((256, D), BF),
        pltpu.VMEM((4, HEAD, T), BF), pltpu.VMEM((HEAD, T), BF), pltpu.VMEM((HEAD, T), BF),
        pltpu.VMEM((4, HEAD, T), BF), pltpu.VMEM((4, 2, SLAB, D), BF),
        *LineSum.SCRATCH,
        pltpu.VMEM((SLAB, D), F32), pltpu.VMEM((SLAB, D), BF),
        pltpu.VMEM((8, D), F32), pltpu.VMEM((T, 1), jnp.int32), pltpu.VMEM((1, T), jnp.int32),
        pltpu.VMEM((32, T), F32), pltpu.VMEM((32, T), F32), pltpu.VMEM((3 * QB, QB), F32),
        pltpu.VMEM((8, T), F32),
        pltpu.VMEM((T, 128), BF), pltpu.VMEM((256, 512), BF), pltpu.VMEM((256, 512), BF),
        pltpu.VMEM((512, 256), BF),
        pltpu.VMEM((2, 512, D), BF), pltpu.VMEM((T, D), BF), pltpu.VMEM((2, T, 512), BF),
    ]
    return pl.pallas_call(
        first_kernel,
        out_shape=[jax.ShapeDtypeStruct(s, d) for s, d in shapes],
        in_specs=[ANY] * 8 + [VM] * 2,
        out_specs=out_specs,
        scratch_shapes=scratch,
        compiler_params=pltpu.CompilerParams(
            collective_id=0, has_side_effects=True, vmem_limit_bytes=62 << 20
        ),
        name="first",
    )(*args)


class WeightSum:
    @staticmethod
    def scratch(rows, cols):
        h = rows // 2
        return [
            pltpu.VMEM((2, 4, h, cols), BF),
            pltpu.VMEM((2, 4, rows, cols), BF),
            pltpu.VMEM((2, h, cols), BF),
            pltpu.VMEM((2, rows, cols), BF),
        ]

    def __init__(self, wire, part, out, start, rows, order, far, came, far2, came2):
        self.w, self.part, self.out = wire, part, out
        self.r0, self.n = start, rows
        self.a1, self.a2 = ("y", "x") if order == 0 else ("x", "y")
        self.far, self.came, self.far2, self.came2 = far, came, far2, came2

    def span(self, half):
        if half is None:
            return pl.ds(self.r0, self.n)
        return pl.ds(self.r0 + half * (self.n // 2), self.n // 2)

    def src(self, k, j, half=None):
        p = self.w.place
        if self.a1 == "y":
            y = p.pos("y", k)
            return self.part.at[y // 2, j, lax.rem(y, 2), self.span(half)]
        return self.part.at[j // 2, p.pos("x", k), lax.rem(j, 2), self.span(half)]

    def four(self, k, half=None, part=None):
        p = self.w.place
        part = self.part if part is None else part
        if self.a1 == "y":
            y = p.pos("y", k)
            return part.at[y // 2, :, lax.rem(y, 2), self.span(half)]
        return part.at[:, p.pos("x", k), :, self.span(half)]

    def land(self, ref, i):
        if self.a1 == "y":
            return ref.at[i]
        return ref.reshape(2, 2, 2, *ref.shape[2:]).at[i]

    def s1(self, part=None):
        w, p = self.w, self.w.place
        self.up = w.send(self.four(2, 0, part), self.land(self.far, 0), p.step(self.a1, 1))
        self.down = w.send(self.four(2, 1, part), self.land(self.far, 1), p.step(self.a1, -1))

    def s2(self):
        w, p = self.w, self.w.place
        h = self.n // 2
        self.up.wait_recv()
        for j in range(4):
            a = self.src(1, j, 0)
            add_rows(a, [a, self.far.at[0, j]], h)
        self.up2 = w.send(self.four(1), self.land(self.came, 0), p.step(self.a1, 1))
        self.down.wait_recv()
        for j in range(4):
            a = self.src(-1, j, 1)
            add_rows(a, [a, self.far.at[1, j]], h)
        self.down2 = w.send(self.four(-1), self.land(self.came, 1), p.step(self.a1, -1))

    def s3(self):
        w, p = self.w, self.w.place
        self.up2.wait_recv()
        self.down2.wait_recv()
        for k in (2, 1, -1, 0):
            j = p.pos(self.a2, k)
            a = self.src(0, j)
            add_rows(a, [a, self.came.at[0, j], self.came.at[1, j]], self.n)
            if k == 2:
                self.up3 = w.send(self.src(0, j, 0), self.far2.at[0], p.step(self.a2, 1))
                self.down3 = w.send(self.src(0, j, 1), self.far2.at[1], p.step(self.a2, -1))

    def s4(self):
        w, p = self.w, self.w.place
        h = self.n // 2
        self.up3.wait_recv()
        j = p.pos(self.a2, 1)
        a = self.src(0, j, 0)
        add_rows(a, [a, self.far2.at[0]], h)
        self.up4 = w.send(self.src(0, j), self.came2.at[0], p.step(self.a2, 1))
        self.down3.wait_recv()
        j = p.pos(self.a2, -1)
        a = self.src(0, j, 1)
        add_rows(a, [a, self.far2.at[1]], h)
        self.down4 = w.send(self.src(0, j), self.came2.at[1], p.step(self.a2, -1))

    def s5(self):
        self.up4.wait_recv()
        self.down4.wait_recv()
        j = self.w.place.pos(self.a2, 0)
        add_rows(
            self.out.at[pl.ds(self.r0, self.n)],
            [self.src(0, j), self.came2.at[0], self.came2.at[1]],
            self.n,
        )


def second_kernel(
    n2_in, cot_in, g_in, u_in, d_in, after_in, gain_in, act_in,
    attn_out, grad_after, gain_part, out_cols, o_down, o_gate, gu_out,
    send, recv, n2, pg, gw, uw, dw, ggp, ha, gup, gd, pf, attn, outs, after, gain, slab, *sc,
):
    p = Place()
    w = Wire(p, send, recv)
    rows = row_peers(p)
    greet(ring_peers(p) + [dev for _, _, _, dev in rows])
    cot = pg.reshape(T, D)
    loads = []
    for j in range(2):
        part = [w.copy(g_in.at[j], gw.at[j]), w.copy(u_in.at[j], uw.at[j]), w.copy(act_in.at[j], ggp.at[j])]
        part += [w.copy(n2_in, n2)] if j == 0 else []
        loads.append(part)
    l_d = [w.copy(d_in.at[j, g], dw.at[j, :, pl.ds(g * 256, 256)]) for j in range(2) for g in range(8)]
    l_c = w.copy(cot_in, cot)
    l_s = [
        w.copy(after_in, after), w.copy(gain_in, gain),
    ]
    f = LineSum(w, pf, *sc[0:3])
    s = LineSum(w, pg, *sc[3:6])
    down = [WeightSum(w, gd, o_down, 256 * i, 256, i, *sc[6 + 4 * i : 10 + 4 * i]) for i in range(2)]
    gparts = gw.reshape(2, 4, 2, 256, 512)
    gates = [WeightSum(w, gparts, o_gate, 128 * i, 128, i, *sc[14 + 4 * i : 18 + 4 * i]) for i in range(2)]

    def each(group, stage):
        for b in group:
            getattr(b, stage)()

    for t, k in enumerate(LineSum.ORDER):
        i = p.pos("z", k)
        at = rows_of(i, QB)

        def units(j, carry):
            gate = contract(n2[at], gw[j], 1, 0)
            upp = contract(n2[at], uw[j], 1, 0)
            ga = ggp[j, at].astype(F32)
            sig = 1.0 / (1.0 + jnp.exp(-gate))
            silu = gate * sig
            ha[j, at] = (silu * upp).astype(BF)
            ggp[j, at] = (ga * upp * sig * (1.0 + gate * (1.0 - sig))).astype(BF)
            gup[j, at] = (ga * silu).astype(BF)
            return carry

        if t == 0:
            for j in range(2):
                for cp in loads[j]:
                    cp.wait()
                units(j, 0)
            for cp in l_d:
                cp.wait()
        else:
            lax.fori_loop(0, 2, units, 0)
        for b in range(4):
            cols = slice(b * 512, (b + 1) * 512)
            o = (contract(ha[0, at], dw[0, :, cols], 1, 0) + contract(ha[1, at], dw[1, :, cols], 1, 0)).astype(BF)
            pf[i, 0, :, cols] = o[:SLAB]
            pf[i, 1, :, cols] = o[SLAB:]
        f.after_block(t)

    def down_grad(g, carry):
        at = rows_of(g, 512)
        for j in range(2):
            v = (RES * contract(ha[j], cot[:, at], 0, 0)).astype(BF)
            gd[j, g, 0] = v[:, :256]
            gd[j, g, 1] = v[:, 256:]
        return carry

    l_c.wait()
    lax.fori_loop(0, 4, down_grad, 0)
    slab[...] = cot[rows_of(p.r, SLAB)]
    f.finish()
    each(down, "s1")
    for t, k in enumerate(LineSum.ORDER):
        i = p.pos("z", k)
        at = rows_of(i, QB)
        for b in range(4):
            cols = slice(b * 512, (b + 1) * 512)
            o = contract(ggp[0, at], gw[0, cols], 1, 1) + contract(gup[0, at], uw[0, cols], 1, 1)
            o = o + contract(ggp[1, at], gw[1, cols], 1, 1) + contract(gup[1, at], uw[1, cols], 1, 1)
            o = o.astype(BF)
            pg[i, 0, :, cols] = o[:SLAB]
            pg[i, 1, :, cols] = o[SLAB:]
        s.after_block(t)
        if t == 1:
            each(down, "s2")

    def gate_grad(g, carry):
        at = rows_of(g, 512)
        for j in range(2):
            gw[j, at] = contract(n2[:, at], ggp[j], 0, 0).astype(BF)
        return carry

    def up_grad(g, carry):
        at = rows_of(g, 512)
        for j in range(2):
            uw[j, at] = contract(n2[:, at], gup[j], 0, 0).astype(BF)
        return carry

    lax.fori_loop(0, 1, gate_grad, 0)
    s.finish()
    lax.fori_loop(1, 4, gate_grad, 0)
    each(gates, "s1")
    lax.fori_loop(0, 2, up_grad, 0)
    each(down, "s3")
    for cp in l_s:
        cp.wait()
    s.wait()
    inv = norm_scale(lambda c: after[:, c])
    total = None
    for c in COLS:
        g = s.total(c)
        scaled = after[:, c] * inv
        gs = g * scaled
        gain_part[:, c] = jnp.sum(gs.reshape(SLAB // 8, 8, 128), axis=0)
        e = gs * gain[1:2, c]
        total = e if total is None else total + e
    inner = jnp.sum(total, axis=1, keepdims=True) * (1.0 / D)
    for c in COLS:
        e = s.total(c) * gain[1:2, c]
        v = slab[:, c].astype(F32) + inv * (e - after[:, c] * inv * inner)
        grad_after[:, c] = v
        attn[:, c] = (RES * v).astype(BF)
    a = LineGather(w, attn, attn_out)
    a.s1()
    each(gates, "s2")
    lax.fori_loop(2, 4, up_grad, 0)
    e_u = w.copy(uw, gu_out)
    each(down, "s4")
    f.wait()
    for c in COLS:
        outs[:, c] = (after[:, c] + RES * f.total(c)).astype(BF)
    each(down, "s5")
    a.s2()
    each(gates, "s3")
    o = Scatter(w, outs, out_cols, rows)
    o.s1()
    a.s3()
    each(gates, "s4")
    a.s4()
    each(gates, "s5")
    o.s2()
    e_u.wait()
    w.drain()


def call_second(*args):
    scratch = [
        pltpu.SemaphoreType.DMA((105,)), pltpu.SemaphoreType.DMA((76,)),
        pltpu.VMEM((T, D), BF), pltpu.VMEM((4, 2, SLAB, D), BF),
        pltpu.VMEM((2, D, 512), BF), pltpu.VMEM((2, D, 512), BF), pltpu.VMEM((2, 512, D), BF),
        pltpu.VMEM((2, T, 512), BF), pltpu.VMEM((2, T, 512), BF), pltpu.VMEM((2, T, 512), BF),
        pltpu.VMEM((2, 4, 2, 512, 256), BF),
        pltpu.VMEM((4, 2, SLAB, D), BF),
        pltpu.VMEM((SLAB, D), BF), pltpu.VMEM((SLAB, D), BF), pltpu.VMEM((SLAB, D), F32),
        pltpu.VMEM((8, D), F32), pltpu.VMEM((SLAB, D), BF),
    ]
    scratch += LineSum.SCRATCH * 2
    scratch += WeightSum.scratch(256, 256) * 2 + WeightSum.scratch(128, 512) * 2
    return pl.pallas_call(
        second_kernel,
        out_shape=[
            jax.ShapeDtypeStruct((4, 2, SLAB, D), BF),
            jax.ShapeDtypeStruct((SLAB, D), F32),
            jax.ShapeDtypeStruct((8, D), F32),
            jax.ShapeDtypeStruct((2 * T, 128), BF),
            jax.ShapeDtypeStruct((512, 256), F32),
            jax.ShapeDtypeStruct((256, 512), F32),
            jax.ShapeDtypeStruct((2, D, 512), BF),
        ],
        in_specs=[ANY] * 8,
        out_specs=[ANY, VM, VM, ANY, VM, VM, ANY],
        scratch_shapes=scratch,
        compiler_params=pltpu.CompilerParams(
            collective_id=1, has_side_effects=True, vmem_limit_bytes=62 << 20
        ),
        name="second",
    )(*args)


def key_range(i):
    return max(0, (i - 2) * QB), (i + 1) * QB


def third_kernel(
    ga_in, hid_in, grad_after_in, gain_in, gain_two_in, w2_in, o_in, n1_in, qt_in, kt_in, vt_in, ht_in,
    lse_in, cos_in, sin_in, gu_in, segs,
    hid_cols, o_gain, o_q, o_o, o_up,
    send, recv, ga, n1, w2, o2, ght, gt, gn, gk, gv, bias, seg_col, seg_row,
    part, got, far, near, outs, gains, gcame, gsum, gcame2, tq, to, rq, ro, gu,
    hid, grad_after, gain, gain_two, qt, kt, vt, ht, lse, cos, sin, *sc,
):
    p = Place()
    w = Wire(p, send, recv)
    rows = row_peers(p)
    lanes = [(k, (lax.rem(p.gx + k, 8), p.gy)) for k in range(1, 8)]
    l_ga = [w.copy(ga_in, ga), w.copy(o_in, o2), w.copy(ht_in, ht)]
    l_qk = [w.copy(a, b) for a, b in ((qt_in, qt), (kt_in, kt), (vt_in, vt), (lse_in, lse), (cos_in, cos), (sin_in, sin))]
    greet([dev for _, _, _, dev in rows] + [dev for _, dev in lanes] + [p.at(y=1), p.at(y=-1)])
    big = [WeightSum(w, gu, o_up, 128 * i, 128, i, *sc[4 * i : 4 * i + 4]) for i in range(2)]
    sq = [WeightSum(w, rq, o_q, 192 * i, 192, i, *sc[8 + 4 * i : 12 + 4 * i]) for i in range(2)]
    so = [WeightSum(w, ro, o_o, 64 * i, 64, i, *sc[16 + 4 * i : 20 + 4 * i]) for i in range(2)]

    def each(group, stage):
        for b in group:
            getattr(b, stage)()

    for b in big:
        b.s1(gu_in)
    l_big = [w.copy(gu_in, gu)]
    l_n1 = w.copy(n1_in, n1)
    l_w2 = [w.copy(w2_in, w2)]
    l_s = [w.copy(a, b) for a, b in ((hid_in, hid), (grad_after_in, grad_after), (gain_in, gain), (gain_two_in, gain_two))]
    pick_segment(p, segs, seg_row, seg_col)
    gk[...] = jnp.zeros_like(gk)
    gv[...] = jnp.zeros_like(gv)
    gt[:, 192:] = jnp.zeros((2, 64, T), BF)
    for cp in l_ga:
        cp.wait()

    def heads_grad(i, carry):
        at = rows_of(i, QB)
        ght[:, :, at] = contract(o2[...], ga[at], 1, 1).astype(BF).reshape(4, HEAD, QB)
        return carry

    lax.fori_loop(0, 4, heads_grad, 0)

    def out_grad(dst, j):
        hj = ht[pl.ds(j * 2, 2)].reshape(128, T)
        for g in range(8):
            dst[g // 2, g % 2] = contract(hj, ga[:, g * 256 : (g + 1) * 256], 1, 0).astype(BF)

    out_grad(to, 1 - p.c)
    swap_o = w.send(to, ro.at[p.c], p.at(c=1))
    out_grad(ro.at[p.c], p.c)
    for cp in l_qk:
        cp.wait()
    for i in range(4):
        lo, hi = key_range(i)
        at = slice(i * QB, (i + 1) * QB)
        bias[: hi - lo] = bias_tile(seg_col, seg_row, lo, hi - lo, i)

        def head(n, carry):
            q = qt[n, :, at]
            g = ght[n, :, at]
            sc_ = contract(kt[:, lo:hi], q, 0, 0) + bias[: hi - lo]
            pr = jnp.exp(sc_ - lse[pl.ds(n, 1), at])
            gp = contract(vt[:, lo:hi], g, 0, 0)
            inner = jnp.sum(ht[n, :, at].astype(F32) * g.astype(F32), axis=0, keepdims=True)
            gs = (pr * (gp - inner)).astype(BF)
            gq = contract(kt[:, lo:hi], gs, 1, 0) * ATTN_SCALE
            a, b = gq[:32], gq[32:]
            first = pl.multiple_of(lax.rem(n, 2) * 64, 64)
            gt[n // 2, pl.ds(first, 32), at] = (a * cos[:, at] + b * sin[:, at]).astype(BF)
            gt[n // 2, pl.ds(first + 32, 32), at] = (b * cos[:, at] - a * sin[:, at]).astype(BF)
            gk[:, lo:hi] += contract(q, gs, 1, 1)
            gv[:, lo:hi] += contract(g, pr.astype(BF), 1, 1)
            return carry

        lax.fori_loop(0, 4, head, 0)
        if i == 0:
            swap_o.wait_recv()
            each(so, "s1")
        if i == 1:
            for cp in l_big:
                cp.wait()
            each(big, "s2")
        if i == 2:
            each(so, "s2")
    a, b = gk[:32], gk[32:]
    gt[0, 128:160] = (a * cos[...] + b * sin[...]).astype(BF)
    gt[1, 128:160] = (b * cos[...] - a * sin[...]).astype(BF)
    gt[0, 160:192] = gv[:32].astype(BF)
    gt[1, 160:192] = gv[32:].astype(BF)
    other = 1 - p.c
    for i in range(4):
        gn[i * QB : (i + 1) * QB, :256] = gt[other, :, i * QB : (i + 1) * QB].T
        gn[i * QB : (i + 1) * QB, 256:] = gt[p.c, :, i * QB : (i + 1) * QB].T
    for cp in l_w2:
        cp.wait()
    s = LineSum(w, part, got, far, near)
    for t, k in enumerate(LineSum.ORDER):
        i = p.pos("z", k)
        at = rows_of(i, QB)
        for b in range(4):
            cols = slice(b * 512, (b + 1) * 512)
            o = contract(gn[at, :192], w2[other, cols, :192], 1, 1) + contract(gn[at, 256:448], w2[p.c, cols, :192], 1, 1)
            o = o.astype(BF)
            part[i, 0, :, cols] = o[:SLAB]
            part[i, 1, :, cols] = o[SLAB:]
        s.after_block(t)
    l_n1.wait()

    def in_grad(g, carry):
        v = contract(n1[:, rows_of(g, 512)], gn[...], 0, 0).astype(BF)
        for half in range(2):
            for dst, first in ((tq, 0), (rq.at[p.c], 256)):
                u = v[half * 256 : half * 256 + 256, first : first + 256]
                dst[g, half, :256] = u[:, :128]
                dst[g, half, 256:, :64] = u[:128, 128:192]
                dst[g, half, 256:, 64:] = u[128:, 128:192]
        return carry

    each(so, "s3")
    lax.fori_loop(0, 4, in_grad, 0)
    swap_q = w.send(tq, rq.at[p.c], p.at(c=1))
    s.finish()
    swap_q.wait_recv()
    each(sq, "s1")
    each(big, "s3")
    each(so, "s4")
    for cp in l_s:
        cp.wait()
    each(sq, "s2")
    each(big, "s4")
    s.wait()
    inv = norm_scale(lambda c: hid[:, c].astype(F32))
    total = None
    for c in COLS:
        g = s.total(c)
        scaled = hid[:, c].astype(F32) * inv
        gs = g * scaled
        gains[0, :, c] = jnp.sum(gs.reshape(SLAB // 8, 8, 128), axis=0)
        e = gs * gain[0:1, c]
        total = e if total is None else total + e
    inner = jnp.sum(total, axis=1, keepdims=True) * (1.0 / D)
    for c in COLS:
        e = s.total(c) * gain[0:1, c]
        v = grad_after[:, c] + inv * (e - hid[:, c].astype(F32) * inv * inner)
        outs[:, c] = v.astype(BF)
    gains[1] = gain_two[...]
    mine = pl.ds(pl.multiple_of(p.gy * 128, 128), 128)
    gcp = []
    for _, _, _, dev in rows:
        at = pl.ds(pl.multiple_of(dev[1] * 128, 128), 128)
        gcp.append(w.send(gains.at[:, :, at], gcame.at[p.gy], dev))
    glocal = w.copy(gains.at[:, :, mine], gcame.at[p.gy])
    o = Scatter(w, outs, hid_cols, rows)
    o.s1()
    each(sq, "s3")
    for cp in gcp:
        cp.wait_recv()
    glocal.wait()
    gsum[...] = jnp.sum(gcame[...], axis=0)
    lcp = [w.send(gsum, gcame2.at[p.gx], dev) for _, dev in lanes]
    llocal = w.copy(gsum, gcame2.at[p.gx])
    each(sq, "s4")
    each(big, "s5")
    each(so, "s5")
    for cp in lcp:
        cp.wait_recv()
    llocal.wait()
    o_gain[...] = jnp.sum(gcame2[...], axis=0)
    each(sq, "s5")
    o.s2()
    w.drain()


def call_third(*args):
    scratch = [
        pltpu.SemaphoreType.DMA((116,)), pltpu.SemaphoreType.DMA((97,)),
        pltpu.VMEM((T, D), BF), pltpu.VMEM((T, D), BF),
        pltpu.VMEM((2, D, 256), BF), pltpu.VMEM((256, D), BF),
        pltpu.VMEM((4, HEAD, T), BF), pltpu.VMEM((2, 256, T), BF), pltpu.VMEM((T, 512), BF),
        pltpu.VMEM((HEAD, T), F32), pltpu.VMEM((HEAD, T), F32), pltpu.VMEM((3 * QB, QB), F32),
        pltpu.VMEM((T, 1), jnp.int32), pltpu.VMEM((1, T), jnp.int32),
        pltpu.VMEM((4, 2, SLAB, D), BF),
        *LineSum.SCRATCH,
        pltpu.VMEM((SLAB, D), BF),
        pltpu.VMEM((2, 8, D), F32),
        pltpu.VMEM((16, 2, 8, 128), F32),
        pltpu.VMEM((2, 8, 128), F32),
        pltpu.VMEM((8, 2, 8, 128), F32),
        pltpu.VMEM((4, 2, 384, 128), BF),
        pltpu.VMEM((4, 2, 128, 256), BF),
        pltpu.VMEM((2, 4, 2, 384, 128), BF),
        pltpu.VMEM((2, 4, 2, 128, 256), BF),
        pltpu.VMEM((2, 4, 2, 256, 512), BF),
        pltpu.VMEM((SLAB, D), BF), pltpu.VMEM((SLAB, D), F32),
        pltpu.VMEM((8, D), F32), pltpu.VMEM((8, D), F32),
        pltpu.VMEM((4, HEAD, T), BF), pltpu.VMEM((HEAD, T), BF), pltpu.VMEM((HEAD, T), BF),
        pltpu.VMEM((4, HEAD, T), BF), pltpu.VMEM((8, T), F32),
        pltpu.VMEM((32, T), F32), pltpu.VMEM((32, T), F32),
    ]
    scratch += WeightSum.scratch(128, 512) * 2
    scratch += WeightSum.scratch(192, 128) * 2 + WeightSum.scratch(64, 256) * 2
    return pl.pallas_call(
        third_kernel,
        out_shape=[
            jax.ShapeDtypeStruct((2 * T, 128), BF),
            jax.ShapeDtypeStruct((2, 8, 128), F32),
            jax.ShapeDtypeStruct((384, 128), F32),
            jax.ShapeDtypeStruct((128, 256), F32),
            jax.ShapeDtypeStruct((256, 512), F32),
        ],
        in_specs=[ANY] * 16 + [VM],
        out_specs=[ANY, VM, VM, VM, VM],
        scratch_shapes=scratch,
        compiler_params=pltpu.CompilerParams(
            collective_id=2, has_side_effects=True, vmem_limit_bytes=62 << 20
        ),
        name="third",
    )(*args)


def outputs_kernel(
    cols, hid, gains, qkv, o, gate, up, down,
    x_cols, x_hid, x_gain, x_q, x_k, x_v, x_o, x_gain2, x_gate, x_up, x_down,
):
    x_cols[...] = cols[...].astype(F32)
    x_hid[...] = hid[...].astype(F32)
    x_gain[...] = jnp.sum(gains[0], axis=0, keepdims=True)
    x_gain2[...] = jnp.sum(gains[1], axis=0, keepdims=True)
    x_q[...] = qkv[:256]
    kv = qkv[256:]
    x_k[:128] = kv[:, :32]
    x_k[128:] = kv[:, 64:96]
    x_v[:128] = kv[:, 32:64]
    x_v[128:] = kv[:, 96:]
    x_o[...] = o[...]
    x_gate[...] = gate[...]
    x_up[...] = up[...]
    x_down[...] = down[...]


def call_outputs(*args):
    shapes = [
        (2 * T, 128), (2 * T, 128), (1, 128), (256, 128), (256, 32), (256, 32), (128, 256), (1, 128),
        (256, 512), (256, 512), (512, 256),
    ]
    return pl.pallas_call(
        outputs_kernel,
        out_shape=[jax.ShapeDtypeStruct(v, F32) for v in shapes],
        in_specs=[VM] * 8,
        out_specs=[VM] * 11,
        compiler_params=pltpu.CompilerParams(vmem_limit_bytes=40 << 20),
        name="outputs",
    )(*args)


def per_device(
    hidden, attn_gain, wq, wk, wv, wo, ffn_gain, gate, up, down, segments, cotangent,
):
    gains = jnp.concatenate([attn_gain[None], ffn_gain[None], jnp.zeros((6, 128), F32)], axis=0)
    kv = jnp.concatenate([wk[:128], wv[:128], wk[128:], wv[128:]], axis=1)
    wqkv = jnp.concatenate([wq, kv], axis=0)
    freq = (ROPE_BASE ** (-jnp.arange(0, HEAD, 2, dtype=F32) / HEAD))[:, None]
    (
        cot, gg, uu, dd, w2, o2, n1, hid_slab, qt, kt, vt, ht, lse, after, n2, act, gain, cos, sin
    ) = call_first(hidden, cotangent, wqkv, wo, gate, up, down, gains, segments, freq)
    grad_attn, grad_after, gain_two, out_cols, o_down, o_gate, g_up = call_second(
        n2.reshape(T, D), cot, gg.reshape(2, D, 512), uu.reshape(2, D, 512),
        dd.reshape(2, 8, 512, 256), after, gain, act,
    )
    hid_cols, o_gain, o_qkv, o_o, o_up = call_third(
        grad_attn.reshape(T, D), hid_slab, grad_after, gain, gain_two, w2, o2, n1,
        qt, kt, vt, ht, lse, cos, sin, g_up.reshape(2, 4, 2, 256, 512), segments,
    )
    res = call_outputs(out_cols, hid_cols, o_gain, o_qkv, o_o, o_gate, o_up, o_down)
    return (res[0], res[1], res[2].reshape(128), *res[3:7], res[7].reshape(128), *res[8:])


def solution(mesh):
    wide, cols, tall = P("gx", "gy"), P("gy"), P("gy", "gx")
    return jax.shard_map(
        per_device,
        mesh=mesh,
        in_specs=(wide, cols, wide, wide, wide, tall, cols, wide, wide, tall, P("gx", None), wide),
        out_specs=(wide, wide, cols, wide, wide, wide, tall, cols, wide, wide, tall),
        check_vma=False,
    )
```

```python
import functools

import jax
import jax.numpy as jnp
import numpy as np
from jax import lax
from jax.experimental import pallas as pl
from jax.experimental.pallas import tpu as pltpu
from jax.sharding import PartitionSpec as P

HEAD = 64
EPS = 1e-06
ROPE_BASE = 10000000.0
ATTN_SCALE = 1.0 / 64.0
RES = 0.22
T = 1024
D = 2048
SLAB = 128
QB = 256
BF = jnp.bfloat16
F32 = jnp.float32
MESH = pl.DeviceIdType.MESH
ANY = pl.BlockSpec(memory_space=pl.ANY)
VM = pl.BlockSpec(memory_space=pltpu.VMEM)


class Place:
    def __init__(self):
        gx = lax.axis_index("gx")
        gy = lax.axis_index("gy")
        self.gx, self.gy = gx, gy
        self.x, self.yl = gx // 2, lax.rem(gx, 2)
        self.yh, self.z, self.c = gy // 8, lax.rem(gy // 2, 4), lax.rem(gy, 2)
        self.y = self.yh * 2 + self.yl
        self.r = self.z * 2 + self.c

    def at(self, x=0, y=0, z=0, c=0):
        xx = lax.rem(self.x + x + 4, 4)
        yy = lax.rem(self.y + y + 4, 4)
        zz = lax.rem(self.z + z + 4, 4)
        cc = lax.rem(self.c + c, 2)
        return (xx * 2 + lax.rem(yy, 2), (yy // 2) * 8 + zz * 2 + cc)

    def step(self, axis, k):
        return self.at(**{axis: k})

    def pos(self, axis, k):
        return lax.rem(getattr(self, axis) + k + 4, 4)


class Wire:
    def __init__(self, place, send, recv):
        self.place, self.send_sem, self.recv_sem = place, send, recv
        self.starts, self.lands = 0, 0
        self.sent = []

    def send(self, src, dst, to):
        i, j = self.starts, self.lands
        self.starts, self.lands = i + 1, j + 1
        cp = pltpu.make_async_remote_copy(
            src_ref=src,
            dst_ref=dst,
            send_sem=self.send_sem.at[i],
            recv_sem=self.recv_sem.at[j],
            device_id=to,
            device_id_type=MESH,
        )
        cp.start()
        self.sent.append(cp)
        return cp

    def copy(self, src, dst):
        i = self.starts
        self.starts += 1
        cp = pltpu.make_async_copy(src, dst, self.send_sem.at[i])
        cp.start()
        return cp

    def drain(self):
        for cp in self.sent:
            cp.wait_send()
        self.sent = []


def greet(peers):
    barrier = pltpu.get_barrier_semaphore()
    for peer in peers:
        pl.semaphore_signal(barrier, inc=1, device_id=peer, device_id_type=MESH)
    pl.semaphore_wait(barrier, len(peers))


def ring_peers(p):
    return [p.at(x=1), p.at(x=-1), p.at(y=1), p.at(y=-1)]


def row_peers(p):
    out = []
    for y in (0, 2):
        for z in range(4):
            for c in range(2):
                if (y, z, c) != (0, 0, 0):
                    out.append((y, z, c, p.at(y=y, z=z, c=c)))
    return out


def line_peers(p):
    return [p.at(c=1), p.at(z=1), p.at(z=-1)]


class WeightGather:
    def __init__(self, wire, src, dst, start, rows, order, stage=None):
        self.w, self.src, self.dst, self.stage = wire, src, dst, stage
        self.r0, self.n, self.order = start, rows, order
        self.a1, self.a2 = ("x", "y") if order == 0 else ("y", "x")

    def one(self, k, half=None):
        p = self.w.place
        x, y = (p.pos("x", k), p.y) if self.a1 == "x" else (p.x, p.pos("y", k))
        return self.dst.at[y // 2, x, lax.rem(y, 2), self.span(half)]

    def four(self, k, half=None):
        p = self.w.place
        if self.a2 == "y":
            y = p.pos("y", k)
            return self.dst.at[y // 2, :, lax.rem(y, 2), self.span(half)]
        return self.dst.at[:, p.pos("x", k), :, self.span(half)]

    def span(self, half):
        if half is None:
            return pl.ds(self.r0, self.n)
        return pl.ds(self.r0 + half * (self.n // 2), self.n // 2)

    def s1(self):
        w, p = self.w, self.w.place
        own = self.src.at[pl.ds(self.r0, self.n)]
        if self.stage is None:
            self.local = w.copy(own, self.one(0))
        else:
            self.local = w.copy(own, self.stage.at[pl.ds(self.r0, self.n)])
        self.up = w.send(own, self.one(0), p.step(self.a1, 1))
        self.down = w.send(own, self.one(0), p.step(self.a1, -1))

    def s2(self):
        w, p = self.w, self.w.place
        if self.stage is not None:
            self.local.wait()
            self.local = w.copy(self.stage.at[pl.ds(self.r0, self.n)], self.one(0))
        self.up.wait_recv()
        self.up2 = w.send(self.one(-1, 0), self.one(-1, 0), p.step(self.a1, 1))
        self.down.wait_recv()
        self.down2 = w.send(self.one(1, 1), self.one(1, 1), p.step(self.a1, -1))

    def s3(self):
        w, p = self.w, self.w.place
        self.local.wait()
        self.up2.wait_recv()
        self.down2.wait_recv()
        self.up3 = w.send(self.four(0), self.four(0), p.step(self.a2, 1))
        self.down3 = w.send(self.four(0), self.four(0), p.step(self.a2, -1))

    def s4(self):
        w, p = self.w, self.w.place
        self.up3.wait_recv()
        self.up4 = w.send(self.four(-1, 0), self.four(-1, 0), p.step(self.a2, 1))
        self.down3.wait_recv()
        self.down4 = w.send(self.four(1, 1), self.four(1, 1), p.step(self.a2, -1))

    def s5(self):
        self.up4.wait_recv()
        self.down4.wait_recv()


class RowGather:
    def __init__(self, wire, src, dst, stage=None):
        self.w, self.src, self.dst, self.stage = wire, src, dst, stage

    def block(self, yh, k, c=None):
        p = self.w.place
        c = p.c if c is None else c
        gy = yh * 8 + p.pos("z", k) * 2 + c
        return self.dst.at[:, pl.ds(pl.multiple_of(gy * 128, 128), 128)]

    def out(self, src, yh, k):
        b = self.block(yh, k)
        self.cores.append(self.w.send(src, b, self.w.place.at(c=1)))

    def s0(self):
        w, p = self.w, self.w.place
        self.cores = []
        mine = self.src.at[pl.ds(pl.multiple_of(p.yh * T, T), T)]
        other = self.src.at[pl.ds(pl.multiple_of((1 - p.yh) * T, T), T)]
        own = self.block(p.yh, 0)
        self.local = w.copy(mine, own if self.stage is None else self.stage)
        self.swap = w.send(other, own, p.at(y=2))

    def s1(self):
        w, p = self.w, self.w.place
        mine = self.src.at[pl.ds(pl.multiple_of(p.yh * T, T), T)]
        own = self.block(p.yh, 0)
        self.up0 = w.send(mine, own, p.at(z=1))
        self.down0 = w.send(mine, own, p.at(z=-1))
        self.out(mine, p.yh, 0)

    def s2(self):
        w, p = self.w, self.w.place
        if self.stage is not None:
            self.local.wait()
            self.local = w.copy(self.stage, self.block(p.yh, 0))
        self.swap.wait_recv()
        b = self.block(1 - p.yh, 0)
        self.up1 = w.send(b, b, p.at(z=1))
        self.down1 = w.send(b, b, p.at(z=-1))
        self.out(b, 1 - p.yh, 0)

    def s3(self):
        w, p = self.w, self.w.place
        self.up0.wait_recv()
        b = self.block(p.yh, -1)
        self.up2 = w.send(b, b, p.at(z=1))
        self.out(b, p.yh, -1)
        self.down0.wait_recv()
        self.out(self.block(p.yh, 1), p.yh, 1)
        self.down1.wait_recv()
        b = self.block(1 - p.yh, 1)
        self.down2 = w.send(b, b, p.at(z=-1))
        self.out(b, 1 - p.yh, 1)
        self.up1.wait_recv()
        self.out(self.block(1 - p.yh, -1), 1 - p.yh, -1)

    def s4(self):
        p = self.w.place
        self.up2.wait_recv()
        self.out(self.block(p.yh, 2), p.yh, 2)
        self.down2.wait_recv()
        self.out(self.block(1 - p.yh, 2), 1 - p.yh, 2)

    def s5(self):
        self.local.wait()
        for cp in self.cores:
            cp.wait_recv()


def add_rows(dst, srcs, rows):
    step = max(16, min(rows, 32768 // dst.shape[-1]))
    while rows % step:
        step //= 2

    def body(i, carry):
        at = pl.ds(pl.multiple_of(i * step, step), step)
        total = srcs[0][at].astype(F32)
        for v in srcs[1:]:
            total = total + v[at].astype(F32)
        dst[at] = total.astype(dst.dtype)
        return carry

    lax.fori_loop(0, rows // step, body, 0)


class LineSum:
    SCRATCH = [
        pltpu.VMEM((4, SLAB, D), BF),
        pltpu.VMEM((2, SLAB // 2, D), BF),
        pltpu.VMEM((2, SLAB, D), BF),
    ]
    ORDER = (2, 1, -1, 0)

    def __init__(self, wire, part, got, far, near):
        self.w, self.part, self.got = wire, part, got
        self.far, self.near = far, near
        self.core = {}
        self.last = []

    def mine(self, k, half=None):
        p = self.w.place
        if half is None:
            return self.part.at[p.pos("z", k), p.c]
        return self.part.at[p.pos("z", k), p.c, pl.ds(half * (SLAB // 2), SLAB // 2)]

    def push(self, k):
        w, p = self.w, self.w.place
        z = p.pos("z", k)
        self.core[k] = w.send(self.part.at[z, 1 - p.c], self.got.at[z], p.at(c=1))

    def merge(self, k):
        z = self.w.place.pos("z", k)
        self.core[k].wait_recv()
        add_rows(self.mine(k), [self.mine(k), self.got.at[z]], SLAB)

    def send_far(self):
        w, p = self.w, self.w.place
        self.up = w.send(self.mine(2, 0), self.far.at[0], p.at(z=1))
        self.down = w.send(self.mine(2, 1), self.far.at[1], p.at(z=-1))

    def near_first(self, i):
        self.near_half(1 if i == 0 else -1, i, 1 - i)

    def near_second(self, i):
        k, far = (1, self.up) if i == 0 else (-1, self.down)
        far.wait_recv()
        add_rows(self.mine(k, i), [self.mine(k, i), self.far.at[i]], SLAB // 2)
        self.near_half(k, i, i)

    def near_half(self, k, i, h):
        at = pl.ds(h * (SLAB // 2), SLAB // 2)
        self.last.append(self.w.send(self.mine(k, h), self.near.at[i, at], self.w.place.at(z=k)))

    def after_block(self, t):
        self.push(self.ORDER[t])
        if t == 1:
            self.merge(2)
            self.send_far()
        if t == 2:
            self.merge(1)
            self.near_first(0)
        if t == 3:
            self.merge(-1)
            self.near_first(1)
            self.merge(0)

    def finish(self):
        self.near_second(0)
        self.near_second(1)

    def wait(self):
        for cp in self.last:
            cp.wait_recv()

    def total(self, at):
        p = self.w.place
        return (
            self.part[p.z, p.c, :, at].astype(F32)
            + self.near[0, :, at].astype(F32)
            + self.near[1, :, at].astype(F32)
        )


class LineGather:
    def __init__(self, wire, src, dst):
        self.w, self.src, self.dst = wire, src, dst

    def slot(self, k, half=None):
        p = self.w.place
        if half is None:
            return self.dst.at[p.pos("z", k), p.c]
        return self.dst.at[p.pos("z", k), p.c, pl.ds(half * (SLAB // 2), SLAB // 2)]

    def s1(self):
        w, p = self.w, self.w.place
        self.up = w.send(self.src, self.slot(0), p.at(z=1))
        self.down = w.send(self.src, self.slot(0), p.at(z=-1))
        self.cores = [w.send(self.src, self.slot(0), p.at(c=1))]
        self.local = w.copy(self.src, self.slot(0))

    def s2(self):
        w, p = self.w, self.w.place
        self.up.wait_recv()
        self.up2 = w.send(self.slot(-1, 0), self.slot(-1, 0), p.at(z=1))
        self.cores.append(w.send(self.slot(-1), self.slot(-1), p.at(c=1)))
        self.down.wait_recv()
        self.down2 = w.send(self.slot(1, 1), self.slot(1, 1), p.at(z=-1))
        self.cores.append(w.send(self.slot(1), self.slot(1), p.at(c=1)))

    def s3(self):
        w, p = self.w, self.w.place
        self.up2.wait_recv()
        self.cores.append(w.send(self.slot(2, 0), self.slot(2, 0), p.at(c=1)))
        self.down2.wait_recv()
        self.cores.append(w.send(self.slot(2, 1), self.slot(2, 1), p.at(c=1)))

    def s4(self):
        self.local.wait()
        for cp in self.cores:
            cp.wait_recv()


class Scatter:
    def __init__(self, wire, src, dst, rows):
        self.w, self.src, self.dst, self.rows = wire, src, dst, rows

    def s1(self):
        w, p = self.w, self.w.place
        mine = self.dst.at[pl.ds(pl.multiple_of(p.yh * T + p.r * SLAB, SLAB), SLAB)]
        self.copies = []
        for y, z, c, dev in self.rows:
            at = pl.ds(pl.multiple_of(dev[1] * 128, 128), 128)
            self.copies.append(w.send(self.src.at[:, at], mine, dev))
        at = pl.ds(pl.multiple_of(p.gy * 128, 128), 128)
        self.local = w.copy(self.src.at[:, at], mine)

    def s2(self):
        self.local.wait()
        for cp in self.copies:
            cp.wait_recv()


def each_rows(rows, step, f):
    def body(i, carry):
        f(pl.ds(pl.multiple_of(i * step, step), step))
        return carry

    lax.fori_loop(0, rows // step, body, 0)


COLS = [slice(j * 128, (j + 1) * 128) for j in range(16)]


def contract(a, b, da, db):
    return lax.dot_general(a, b, (((da,), (db,)), ((), ())), preferred_element_type=F32)


def rows_of(i, n):
    return pl.ds(pl.multiple_of(i * n, n), n)


def row_mean(parts):
    total = parts[0]
    for v in parts[1:]:
        total = total + v
    return jnp.sum(total, axis=1, keepdims=True) * (1.0 / D)


def norm_scale(load):
    squares = []
    total = None
    for at in COLS:
        v = load(at)
        total = v * v if total is None else total + v * v
    return lax.rsqrt(jnp.sum(total, axis=1, keepdims=True) * (1.0 / D) + EPS)


def unpack(packed, wide, out_rows, j):
    for g in range(8):
        src = packed.at[g // 2, g % 2]
        wide[g * 256 : (g + 1) * 256, :128] = src[:256]
        kv = src[256:384]
        wide[g * 256 : g * 256 + 128, 128:192] = kv[:, :64]
        wide[g * 256 + 128 : (g + 1) * 256, 128:192] = kv[:, 64:]
        out_rows[rows_of(j, 128), g * 256 : g * 256 + 128] = src[384:512]
        out_rows[rows_of(j, 128), g * 256 + 128 : (g + 1) * 256] = src[512:]


def key_window(i):
    return pl.multiple_of(jnp.maximum(i - 2, 0) * QB, QB)


def pick_segment(p, segs, seg_row, seg_col):
    row = jnp.where(p.yh == 0, segs[0:1], segs[1:2])
    seg_row[...] = row
    wide = jnp.broadcast_to(row.astype(F32), (128, T)).T
    seg_col[...] = wide[:, 0:1].astype(jnp.int32)


def bias_tile(seg_col, seg_row, lo, n, i):
    first = i * QB
    same = seg_col[pl.ds(lo, n)] == seg_row[:, pl.ds(first, QB)]
    rows = lo + lax.broadcasted_iota(jnp.int32, (n, QB), 0)
    cols = first + lax.broadcasted_iota(jnp.int32, (n, QB), 1)
    return jnp.where(same & (rows <= cols), 0.0, -1e30)


def first_kernel(
    hidden, cot, gate, up, down, wo, wq, wkt, wvt, gain_a, gain_b, segs, freq,
    c_out, g_out, u_out, d_out, w2_out, o2_out, n1_out, slab_out, qt_out, kt_out, vt_out, ht_out,
    lse_out, after_out, n2_out, act_out, gain_out, cos_out, sin_out,
    send, recv, h, n1, q_tmp, q_got, w2, o2, qt, kt, vt, ht, part, got, far, near,
    after, normed, gain, seg_col, seg_row, cos, sin, bias, lse, v_cot, v_gate, v_up, v_down,
    dw, cv, act, v_q, gains,
):
    p = Place()
    w = Wire(p, send, recv)
    v_q[:256] = wq[...]
    kv = [wkt[:, :128], wvt[:, :128], wkt[:, 128:], wvt[:, 128:]]
    v_q[256:384] = jnp.concatenate(kv, axis=0).astype(F32).T.astype(BF)
    v_q[384:512] = wo[:, :128]
    v_q[512:] = wo[:, 128:]
    gains[...] = jnp.zeros_like(gains)
    gains[0:1] = gain_a[...]
    gains[1:2] = gain_b[...]
    rows = row_peers(p)
    greet(ring_peers(p) + [dev for _, _, _, dev in rows])
    hg = RowGather(w, hidden, h)
    cg = RowGather(w, cot, c_out, v_cot)
    aq = [WeightGather(w, v_q, q_tmp, 320 * i, 320, i) for i in range(2)]
    gu = [WeightGather(w, gate, g_out, 0, 256, 0, v_gate), WeightGather(w, up, u_out, 0, 256, 1, v_up)]
    dn = [WeightGather(w, down, d_out, 256 * i, 256, i, v_down) for i in range(2)]

    def each(group, stage):
        for b in group:
            getattr(b, stage)()

    each(aq, "s1")
    hg.s0()
    hg.s1()
    own = pl.ds(pl.multiple_of(p.gy * 128, 128), 128)
    glocal = w.copy(gains, gain.at[:, own])
    gcopies = [w.send(gains, gain.at[:, own], dev) for _, _, _, dev in rows]

    pick_segment(p, segs, seg_row, seg_col)
    earlier = jnp.zeros((8, T), F32)
    for b in range(8):
        less = seg_col[b * 128 : (b + 1) * 128] < seg_row[...]
        earlier = earlier + jnp.sum(jnp.where(less, 1.0, 0.0).reshape(16, 8, T), axis=0)
    starts = jnp.sum(earlier, axis=0, keepdims=True)
    places = lax.broadcasted_iota(jnp.int32, (1, T), 1).astype(F32) - starts
    turned = freq[...] * places
    cos[...] = jnp.cos(turned)
    sin[...] = jnp.sin(turned)

    each(aq, "s2")
    each(aq, "s3")
    hg.s2()
    each(dn, "s1")
    cg.s0()
    each(aq, "s4")
    hg.s3()
    each(aq, "s5")
    q_swap = w.send(q_tmp.at[1 - p.c], q_got, p.at(c=1))
    unpack(q_tmp.at[p.c], w2.at[p.c], o2, p.c)
    each(dn, "s2")
    hg.s4()
    cg.s1()
    each(gu, "s1")
    q_swap.wait_recv()
    unpack(q_got, w2.at[1 - p.c], o2, 1 - p.c)
    hg.s5()
    cg.s2()
    glocal.wait()
    for cp in gcopies:
        cp.wait_recv()

    def project(i, carry):
        at = rows_of(i, QB)
        inv = norm_scale(lambda c: h[at, c].astype(F32))
        for c in COLS:
            n1[at, c] = (h[at, c].astype(F32) * inv * gain[0:1, c]).astype(BF)
        ct, st = cos[:, at], sin[:, at]
        keys = []
        for j in range(2):
            lin = contract(n1[at], w2[j, :, :192], 1, 0)
            qj = lin[:, :128].T
            kv = lin[:, 128:].T
            for hh in range(2):
                a, b = qj[hh * 64 : hh * 64 + 32], qj[hh * 64 + 32 : hh * 64 + 64]
                qt[2 * j + hh, 0:32, at] = (a * ct - b * st).astype(BF) * ATTN_SCALE
                qt[2 * j + hh, 32:64, at] = (b * ct + a * st).astype(BF) * ATTN_SCALE
            keys.append(kv[:32])
            vt[j * 32 : (j + 1) * 32, at] = kv[32:].astype(BF)
        a, b = keys
        kt[0:32, at] = (a * ct - b * st).astype(BF)
        kt[32:64, at] = (b * ct + a * st).astype(BF)
        return carry

    lax.fori_loop(0, 4, project, 0)
    exports = [
        w.copy(w2, w2_out), w.copy(o2, o2_out),
        w.copy(n1, n1_out),
        w.copy(h.at[pl.ds(pl.multiple_of(p.r * SLAB, SLAB), SLAB)], slab_out),
        w.copy(qt, qt_out), w.copy(kt, kt_out), w.copy(vt, vt_out),
    ]
    each(dn, "s3")
    gain_out[...] = gain[...]
    cos_out[...] = cos[...]
    sin_out[...] = sin[...]
    s = LineSum(w, part, got, far, near)

    def attend(t):
        i = p.pos("z", LineSum.ORDER[t])
        lo = key_window(i)
        at = rows_of(i, QB)
        keys = pl.ds(lo, 3 * QB)
        bias[...] = bias_tile(seg_col, seg_row, lo, 3 * QB, pl.multiple_of(i, 1))

        def head(n, carry):
            sc = contract(kt[:, keys], qt[n, :, at], 0, 0) + bias[...]
            top = jnp.max(sc, axis=0, keepdims=True)
            e = jnp.exp(sc - top)
            total = jnp.sum(e, axis=0, keepdims=True)
            o = contract(vt[:, keys], e.astype(BF), 1, 0) * (1.0 / total)
            ht[n, :, at] = o.astype(BF)
            lse[pl.ds(n, 1), at] = top + jnp.log(total)
            return carry

        lax.fori_loop(0, 4, head, 0)

    def out_project(t):
        i = p.pos("z", LineSum.ORDER[t])
        block = ht[:, :, rows_of(i, QB)].reshape(256, QB)
        for b in range(4):
            cols = slice(b * 512, (b + 1) * 512)
            o = contract(block, o2[:, cols], 0, 0).astype(BF)
            part[i, 0, :, cols] = o[:SLAB]
            part[i, 1, :, cols] = o[SLAB:]
        s.after_block(t)

    attend(0)
    out_project(0)
    each(gu, "s2")
    attend(1)
    out_project(1)
    cg.s3()
    attend(2)
    out_project(2)
    attend(3)
    out_project(3)
    exports += [w.copy(ht, ht_out), w.copy(lse, lse_out)]
    s.finish()
    each(dn, "s4")
    each(gu, "s3")
    cg.s4()
    s.wait()
    slab = pl.ds(pl.multiple_of(p.r * SLAB, SLAB), SLAB)
    for c in COLS:
        after[:, c] = h[slab, c].astype(F32) + RES * s.total(c)
    inv = norm_scale(lambda c: after[:, c])
    for c in COLS:
        normed[:, c] = (after[:, c] * inv * gain[1:2, c]).astype(BF)
    g = LineGather(w, normed, n2_out)
    g.s1()
    exports.append(w.copy(after, after_out))
    each(dn, "s5")
    loads = [
        w.copy(d_out.at[j, g // 2, g % 2], dw.at[j, :, pl.ds(g * 256, 256)]) for j in range(2) for g in range(8)
    ]
    cg.s5()
    loads.append(w.copy(c_out, cv))
    for cp in loads:
        cp.wait()

    def act_grad(i, carry):
        at = rows_of(i, 512)
        for j in range(2):
            act[j, at] = (RES * contract(cv[at], dw[j], 1, 1)).astype(BF)
        return carry

    lax.fori_loop(0, 2, act_grad, 0)
    exports.append(w.copy(act, act_out))
    g.s2()
    each(gu, "s4")
    g.s3()
    each(gu, "s5")
    g.s4()
    for cp in exports:
        cp.wait()
    w.drain()


def call_first(*args):
    shapes = [
        ((T, D), BF),
        ((2, 4, 2, 256, 512), BF), ((2, 4, 2, 256, 512), BF), ((2, 4, 2, 512, 256), BF),
        ((2, D, 256), BF), ((256, D), BF),
        ((T, D), BF), ((SLAB, D), BF),
        ((4, HEAD, T), BF), ((HEAD, T), BF), ((HEAD, T), BF), ((4, HEAD, T), BF),
        ((8, T), F32), ((SLAB, D), F32), ((4, 2, SLAB, D), BF), ((2, T, 512), BF),
        ((8, D), F32), ((32, T), F32), ((32, T), F32),
    ]
    out_specs = [ANY] * 16 + [VM] * 3
    scratch = [
        pltpu.SemaphoreType.DMA((156,)), pltpu.SemaphoreType.DMA((113,)),
        pltpu.VMEM((T, D), BF), pltpu.VMEM((T, D), BF),
        pltpu.VMEM((2, 4, 2, 640, 128), BF), pltpu.VMEM((4, 2, 640, 128), BF),
        pltpu.VMEM((2, D, 256), BF), pltpu.VMEM((256, D), BF),
        pltpu.VMEM((4, HEAD, T), BF), pltpu.VMEM((HEAD, T), BF), pltpu.VMEM((HEAD, T), BF),
        pltpu.VMEM((4, HEAD, T), BF), pltpu.VMEM((4, 2, SLAB, D), BF),
        *LineSum.SCRATCH,
        pltpu.VMEM((SLAB, D), F32), pltpu.VMEM((SLAB, D), BF),
        pltpu.VMEM((8, D), F32), pltpu.VMEM((T, 1), jnp.int32), pltpu.VMEM((1, T), jnp.int32),
        pltpu.VMEM((32, T), F32), pltpu.VMEM((32, T), F32), pltpu.VMEM((3 * QB, QB), F32),
        pltpu.VMEM((8, T), F32),
        pltpu.VMEM((T, 128), BF), pltpu.VMEM((256, 512), BF), pltpu.VMEM((256, 512), BF),
        pltpu.VMEM((512, 256), BF),
        pltpu.VMEM((2, 512, D), BF), pltpu.VMEM((T, D), BF), pltpu.VMEM((2, T, 512), BF),
        pltpu.VMEM((640, 128), BF), pltpu.VMEM((8, 128), F32),
    ]
    return pl.pallas_call(
        first_kernel,
        out_shape=[jax.ShapeDtypeStruct(s, d) for s, d in shapes],
        in_specs=[ANY] * 5 + [VM] * 8,
        out_specs=out_specs,
        scratch_shapes=scratch,
        compiler_params=pltpu.CompilerParams(
            collective_id=0, has_side_effects=True, vmem_limit_bytes=62 << 20
        ),
        name="first",
    )(*args)


class WeightSum:
    @staticmethod
    def scratch(rows, cols):
        h = rows // 2
        return [
            pltpu.VMEM((2, 4, h, cols), BF),
            pltpu.VMEM((2, 4, rows, cols), BF),
            pltpu.VMEM((2, h, cols), BF),
            pltpu.VMEM((2, rows, cols), BF),
        ]

    def __init__(self, wire, part, out, start, rows, order, far, came, far2, came2):
        self.w, self.part, self.out = wire, part, out
        self.r0, self.n = start, rows
        self.a1, self.a2 = ("y", "x") if order == 0 else ("x", "y")
        self.far, self.came, self.far2, self.came2 = far, came, far2, came2

    def span(self, half):
        if half is None:
            return pl.ds(self.r0, self.n)
        return pl.ds(self.r0 + half * (self.n // 2), self.n // 2)

    def src(self, k, j, half=None):
        p = self.w.place
        if self.a1 == "y":
            y = p.pos("y", k)
            return self.part.at[y // 2, j, lax.rem(y, 2), self.span(half)]
        return self.part.at[j // 2, p.pos("x", k), lax.rem(j, 2), self.span(half)]

    def four(self, k, half=None, part=None):
        p = self.w.place
        part = self.part if part is None else part
        if self.a1 == "y":
            y = p.pos("y", k)
            return part.at[y // 2, :, lax.rem(y, 2), self.span(half)]
        return part.at[:, p.pos("x", k), :, self.span(half)]

    def land(self, ref, i):
        if self.a1 == "y":
            return ref.at[i]
        return ref.reshape(2, 2, 2, *ref.shape[2:]).at[i]

    def s1(self, part=None):
        w, p = self.w, self.w.place
        self.up = w.send(self.four(2, 0, part), self.land(self.far, 0), p.step(self.a1, 1))
        self.down = w.send(self.four(2, 1, part), self.land(self.far, 1), p.step(self.a1, -1))

    def s2(self):
        w, p = self.w, self.w.place
        h = self.n // 2
        self.up.wait_recv()
        for j in range(4):
            a = self.src(1, j, 0)
            add_rows(a, [a, self.far.at[0, j]], h)
        self.up2 = w.send(self.four(1), self.land(self.came, 0), p.step(self.a1, 1))
        self.down.wait_recv()
        for j in range(4):
            a = self.src(-1, j, 1)
            add_rows(a, [a, self.far.at[1, j]], h)
        self.down2 = w.send(self.four(-1), self.land(self.came, 1), p.step(self.a1, -1))

    def s3(self):
        w, p = self.w, self.w.place
        self.up2.wait_recv()
        self.down2.wait_recv()
        for k in (2, 1, -1, 0):
            j = p.pos(self.a2, k)
            a = self.src(0, j)
            add_rows(a, [a, self.came.at[0, j], self.came.at[1, j]], self.n)
            if k == 2:
                self.up3 = w.send(self.src(0, j, 0), self.far2.at[0], p.step(self.a2, 1))
                self.down3 = w.send(self.src(0, j, 1), self.far2.at[1], p.step(self.a2, -1))

    def s4(self):
        w, p = self.w, self.w.place
        h = self.n // 2
        self.up3.wait_recv()
        j = p.pos(self.a2, 1)
        a = self.src(0, j, 0)
        add_rows(a, [a, self.far2.at[0]], h)
        self.up4 = w.send(self.src(0, j), self.came2.at[0], p.step(self.a2, 1))
        self.down3.wait_recv()
        j = p.pos(self.a2, -1)
        a = self.src(0, j, 1)
        add_rows(a, [a, self.far2.at[1]], h)
        self.down4 = w.send(self.src(0, j), self.came2.at[1], p.step(self.a2, -1))

    def s5(self):
        self.up4.wait_recv()
        self.down4.wait_recv()
        j = self.w.place.pos(self.a2, 0)
        add_rows(
            self.out.at[pl.ds(self.r0, self.n)],
            [self.src(0, j), self.came2.at[0], self.came2.at[1]],
            self.n,
        )


def second_kernel(
    n2_in, cot_in, g_in, u_in, d_in, after_in, gain_in, act_in,
    attn_out, grad_after_out, gain_part, out_cols, o_down, o_gate, gu_out,
    send, recv, n2, pg, gw, uw, dw, ggp, ha, gup, gd, pf, attn, outs, after, gain, slab, v_down, v_gate, *sc,
):
    p = Place()
    w = Wire(p, send, recv)
    cot = pg.reshape(T, D)
    loads = []
    for j in range(2):
        part = [w.copy(g_in.at[j], gw.at[j]), w.copy(u_in.at[j], uw.at[j]), w.copy(act_in.at[j], ggp.at[j])]
        part += [w.copy(n2_in, n2)] if j == 0 else []
        loads.append(part)
    l_d = [w.copy(d_in.at[j, g], dw.at[j, :, pl.ds(g * 256, 256)]) for j in range(2) for g in range(8)]
    l_c = w.copy(cot_in, cot)
    l_s = [
        w.copy(after_in, after), w.copy(gain_in, gain),
    ]
    rows = row_peers(p)
    greet(ring_peers(p) + [dev for _, _, _, dev in rows])
    f = LineSum(w, pf, *sc[0:3])
    s = LineSum(w, pg, *sc[3:6])
    down = [WeightSum(w, gd, v_down, 256 * i, 256, i, *sc[6 + 4 * i : 10 + 4 * i]) for i in range(2)]
    gparts = gw.reshape(2, 4, 2, 256, 512)
    gates = [WeightSum(w, gparts, v_gate, 128 * i, 128, i, *sc[14 + 4 * i : 18 + 4 * i]) for i in range(2)]

    def each(group, stage):
        for b in group:
            getattr(b, stage)()

    for t, k in enumerate(LineSum.ORDER):
        i = p.pos("z", k)
        at = rows_of(i, QB)

        def units(j, carry):
            gate = contract(n2[at], gw[j], 1, 0)
            upp = contract(n2[at], uw[j], 1, 0)
            ga = ggp[j, at].astype(F32)
            sig = 1.0 / (1.0 + jnp.exp(-gate))
            silu = gate * sig
            ha[j, at] = (silu * upp).astype(BF)
            ggp[j, at] = (ga * upp * sig * (1.0 + gate * (1.0 - sig))).astype(BF)
            gup[j, at] = (ga * silu).astype(BF)
            return carry

        if t == 0:
            for j in range(2):
                for cp in loads[j]:
                    cp.wait()
                units(j, 0)
            for cp in l_d:
                cp.wait()
        else:
            lax.fori_loop(0, 2, units, 0)
        for b in range(4):
            cols = slice(b * 512, (b + 1) * 512)
            o = (contract(ha[0, at], dw[0, :, cols], 1, 0) + contract(ha[1, at], dw[1, :, cols], 1, 0)).astype(BF)
            pf[i, 0, :, cols] = o[:SLAB]
            pf[i, 1, :, cols] = o[SLAB:]
        f.after_block(t)

    def down_grad(g, carry):
        at = rows_of(g, 512)
        for j in range(2):
            v = (RES * contract(ha[j], cot[:, at], 0, 0)).astype(BF)
            gd[j, g, 0] = v[:, :256]
            gd[j, g, 1] = v[:, 256:]
        return carry

    l_c.wait()
    lax.fori_loop(0, 4, down_grad, 0)
    slab[...] = cot[rows_of(p.r, SLAB)]
    f.finish()
    each(down, "s1")
    for t, k in enumerate(LineSum.ORDER):
        i = p.pos("z", k)
        at = rows_of(i, QB)
        for b in range(4):
            cols = slice(b * 512, (b + 1) * 512)
            o = contract(ggp[0, at], gw[0, cols], 1, 1) + contract(gup[0, at], uw[0, cols], 1, 1)
            o = o + contract(ggp[1, at], gw[1, cols], 1, 1) + contract(gup[1, at], uw[1, cols], 1, 1)
            o = o.astype(BF)
            pg[i, 0, :, cols] = o[:SLAB]
            pg[i, 1, :, cols] = o[SLAB:]
        s.after_block(t)
        if t == 1:
            each(down, "s2")

    def gate_grad(g, carry):
        at = rows_of(g, 512)
        for j in range(2):
            gw[j, at] = contract(n2[:, at], ggp[j], 0, 0).astype(BF)
        return carry

    def up_grad(g, carry):
        at = rows_of(g, 512)
        for j in range(2):
            uw[j, at] = contract(n2[:, at], gup[j], 0, 0).astype(BF)
        return carry

    lax.fori_loop(0, 1, gate_grad, 0)
    s.finish()
    lax.fori_loop(1, 4, gate_grad, 0)
    each(gates, "s1")
    lax.fori_loop(0, 2, up_grad, 0)
    each(down, "s3")
    for cp in l_s:
        cp.wait()
    f.wait()
    for c in COLS:
        outs[:, c] = (after[:, c] + RES * f.total(c)).astype(BF)
    s.wait()
    inv = norm_scale(lambda c: after[:, c])
    total = None
    for c in COLS:
        g = s.total(c)
        scaled = after[:, c] * inv
        gs = g * scaled
        gain_part[:, c] = jnp.sum(gs.reshape(SLAB // 8, 8, 128), axis=0)
        e = gs * gain[1:2, c]
        total = e if total is None else total + e
    inner = jnp.sum(total, axis=1, keepdims=True) * (1.0 / D)
    for c in COLS:
        e = s.total(c) * gain[1:2, c]
        v = slab[:, c].astype(F32) + inv * (e - after[:, c] * inv * inner)
        after[:, c] = v
        attn[:, c] = (RES * v).astype(BF)
    a = LineGather(w, attn, attn_out)
    a.s1()
    each(gates, "s2")
    lax.fori_loop(2, 4, up_grad, 0)
    e_u = w.copy(uw, gu_out)
    each(down, "s4")
    a.s2()
    each(gates, "s3")
    o = Scatter(w, outs, out_cols, rows)
    o.s1()
    each(down, "s5")
    e_out = [w.copy(after, grad_after_out), w.copy(v_down, o_down)]
    a.s3()
    each(gates, "s4")
    a.s4()
    each(gates, "s5")
    e_out.append(w.copy(v_gate, o_gate))
    o.s2()
    e_u.wait()
    for cp in e_out:
        cp.wait()
    w.drain()


def call_second(*args):
    scratch = [
        pltpu.SemaphoreType.DMA((108,)), pltpu.SemaphoreType.DMA((76,)),
        pltpu.VMEM((T, D), BF), pltpu.VMEM((4, 2, SLAB, D), BF),
        pltpu.VMEM((2, D, 512), BF), pltpu.VMEM((2, D, 512), BF), pltpu.VMEM((2, 512, D), BF),
        pltpu.VMEM((2, T, 512), BF), pltpu.VMEM((2, T, 512), BF), pltpu.VMEM((2, T, 512), BF),
        pltpu.VMEM((2, 4, 2, 512, 256), BF),
        pltpu.VMEM((4, 2, SLAB, D), BF),
        pltpu.VMEM((SLAB, D), BF), pltpu.VMEM((SLAB, D), BF), pltpu.VMEM((SLAB, D), F32),
        pltpu.VMEM((8, D), F32), pltpu.VMEM((SLAB, D), BF),
        pltpu.VMEM((512, 256), F32), pltpu.VMEM((256, 512), F32),
    ]
    scratch += LineSum.SCRATCH * 2
    scratch += WeightSum.scratch(256, 256) * 2 + WeightSum.scratch(128, 512) * 2
    return pl.pallas_call(
        second_kernel,
        out_shape=[
            jax.ShapeDtypeStruct((4, 2, SLAB, D), BF),
            jax.ShapeDtypeStruct((SLAB, D), F32),
            jax.ShapeDtypeStruct((8, D), F32),
            jax.ShapeDtypeStruct((2 * T, 128), BF),
            jax.ShapeDtypeStruct((512, 256), F32),
            jax.ShapeDtypeStruct((256, 512), F32),
            jax.ShapeDtypeStruct((2, D, 512), BF),
        ],
        in_specs=[ANY] * 8,
        out_specs=[ANY, ANY, VM, ANY, ANY, ANY, ANY],
        scratch_shapes=scratch,
        compiler_params=pltpu.CompilerParams(
            collective_id=1, has_side_effects=True, vmem_limit_bytes=62 << 20
        ),
        name="second",
    )(*args)


def key_range(i):
    return max(0, (i - 2) * QB), (i + 1) * QB


def third_kernel(
    ga_in, hid_in, grad_after_in, gain_in, gain_two_in, w2_in, o_in, n1_in, qt_in, kt_in, vt_in, ht_in,
    lse_in, cos_in, sin_in, gu_in, segs,
    hid_cols, o_gain, o_q, o_o, o_up,
    send, recv, ga, n1, w2, o2, ght, gt, gn, gk, gv, bias, seg_col, seg_row,
    part, got, far, near, outs, gains, gcame, gsum, gcame2, tq, to, rq, ro, gu,
    hid, grad_after, gain, gain_two, qt, kt, vt, ht, lse, cos, sin, *sc,
):
    p = Place()
    w = Wire(p, send, recv)
    rows = row_peers(p)
    lanes = [(k, (lax.rem(p.gx + k, 8), p.gy)) for k in range(1, 8)]
    l_ga = [w.copy(ga_in, ga), w.copy(o_in, o2), w.copy(ht_in, ht)]
    l_qk = [w.copy(a, b) for a, b in ((qt_in, qt), (kt_in, kt), (vt_in, vt), (lse_in, lse), (cos_in, cos), (sin_in, sin))]
    greet([dev for _, _, _, dev in rows] + [dev for _, dev in lanes] + [p.at(y=1), p.at(y=-1)])
    big = [WeightSum(w, gu, o_up, 128 * i, 128, i, *sc[4 * i : 4 * i + 4]) for i in range(2)]
    sq = [WeightSum(w, rq, o_q, 192 * i, 192, i, *sc[8 + 4 * i : 12 + 4 * i]) for i in range(2)]
    so = [WeightSum(w, ro, o_o, 64 * i, 64, i, *sc[16 + 4 * i : 20 + 4 * i]) for i in range(2)]

    def each(group, stage):
        for b in group:
            getattr(b, stage)()

    for b in big:
        b.s1(gu_in)
    l_big = [w.copy(gu_in, gu)]
    l_n1 = w.copy(n1_in, n1)
    l_w2 = [w.copy(w2_in, w2)]
    l_s = [w.copy(a, b) for a, b in ((hid_in, hid), (grad_after_in, grad_after), (gain_in, gain), (gain_two_in, gain_two))]
    pick_segment(p, segs, seg_row, seg_col)
    gk[...] = jnp.zeros_like(gk)
    gv[...] = jnp.zeros_like(gv)
    gt[:, 192:] = jnp.zeros((2, 64, T), BF)
    for cp in l_ga:
        cp.wait()

    def heads_grad(i, carry):
        at = rows_of(i, QB)
        ght[:, :, at] = contract(o2[...], ga[at], 1, 1).astype(BF).reshape(4, HEAD, QB)
        return carry

    lax.fori_loop(0, 4, heads_grad, 0)

    def out_grad(dst, j):
        hj = ht[pl.ds(j * 2, 2)].reshape(128, T)
        for g in range(8):
            dst[g // 2, g % 2] = contract(hj, ga[:, g * 256 : (g + 1) * 256], 1, 0).astype(BF)

    out_grad(to, 1 - p.c)
    swap_o = w.send(to, ro.at[p.c], p.at(c=1))
    out_grad(ro.at[p.c], p.c)
    for cp in l_qk:
        cp.wait()
    for i in range(4):
        lo, hi = key_range(i)
        at = slice(i * QB, (i + 1) * QB)
        bias[: hi - lo] = bias_tile(seg_col, seg_row, lo, hi - lo, i)

        def head(n, carry):
            q = qt[n, :, at]
            g = ght[n, :, at]
            sc_ = contract(kt[:, lo:hi], q, 0, 0) + bias[: hi - lo]
            pr = jnp.exp(sc_ - lse[pl.ds(n, 1), at])
            gp = contract(vt[:, lo:hi], g, 0, 0)
            inner = jnp.sum(ht[n, :, at].astype(F32) * g.astype(F32), axis=0, keepdims=True)
            gs = (pr * (gp - inner)).astype(BF)
            gq = contract(kt[:, lo:hi], gs, 1, 0) * ATTN_SCALE
            a, b = gq[:32], gq[32:]
            first = pl.multiple_of(lax.rem(n, 2) * 64, 64)
            gt[n // 2, pl.ds(first, 32), at] = (a * cos[:, at] + b * sin[:, at]).astype(BF)
            gt[n // 2, pl.ds(first + 32, 32), at] = (b * cos[:, at] - a * sin[:, at]).astype(BF)
            gk[:, lo:hi] += contract(q, gs, 1, 1)
            gv[:, lo:hi] += contract(g, pr.astype(BF), 1, 1)
            return carry

        lax.fori_loop(0, 4, head, 0)
        if i == 0:
            swap_o.wait_recv()
            each(so, "s1")
        if i == 1:
            for cp in l_big:
                cp.wait()
            each(big, "s2")
        if i == 2:
            each(so, "s2")
    a, b = gk[:32], gk[32:]
    gt[0, 128:160] = (a * cos[...] + b * sin[...]).astype(BF)
    gt[1, 128:160] = (b * cos[...] - a * sin[...]).astype(BF)
    gt[0, 160:192] = gv[:32].astype(BF)
    gt[1, 160:192] = gv[32:].astype(BF)
    other = 1 - p.c
    for i in range(4):
        gn[i * QB : (i + 1) * QB, :256] = gt[other, :, i * QB : (i + 1) * QB].T
        gn[i * QB : (i + 1) * QB, 256:] = gt[p.c, :, i * QB : (i + 1) * QB].T
    for cp in l_w2:
        cp.wait()
    s = LineSum(w, part, got, far, near)
    for t, k in enumerate(LineSum.ORDER):
        i = p.pos("z", k)
        at = rows_of(i, QB)
        for b in range(4):
            cols = slice(b * 512, (b + 1) * 512)
            o = contract(gn[at, :192], w2[other, cols, :192], 1, 1) + contract(gn[at, 256:448], w2[p.c, cols, :192], 1, 1)
            o = o.astype(BF)
            part[i, 0, :, cols] = o[:SLAB]
            part[i, 1, :, cols] = o[SLAB:]
        s.after_block(t)
    l_n1.wait()

    def in_grad(g, carry):
        v = contract(n1[:, rows_of(g, 512)], gn[...], 0, 0).astype(BF)
        for half in range(2):
            for dst, first in ((tq, 0), (rq.at[p.c], 256)):
                u = v[half * 256 : half * 256 + 256, first : first + 256]
                dst[g, half, :256] = u[:, :128]
                dst[g, half, 256:, :64] = u[:128, 128:192]
                dst[g, half, 256:, 64:] = u[128:, 128:192]
        return carry

    lax.fori_loop(0, 3, in_grad, 0)
    s.finish()
    lax.fori_loop(3, 4, in_grad, 0)
    swap_q = w.send(tq, rq.at[p.c], p.at(c=1))
    each(so, "s3")
    each(big, "s3")
    swap_q.wait_recv()
    each(sq, "s1")
    each(so, "s4")
    each(big, "s4")
    for cp in l_s:
        cp.wait()
    each(sq, "s2")
    s.wait()
    inv = norm_scale(lambda c: hid[:, c].astype(F32))
    total = None
    for c in COLS:
        g = s.total(c)
        scaled = hid[:, c].astype(F32) * inv
        gs = g * scaled
        gains[0, :, c] = jnp.sum(gs.reshape(SLAB // 8, 8, 128), axis=0)
        e = gs * gain[0:1, c]
        total = e if total is None else total + e
    inner = jnp.sum(total, axis=1, keepdims=True) * (1.0 / D)
    for c in COLS:
        e = s.total(c) * gain[0:1, c]
        v = grad_after[:, c] + inv * (e - hid[:, c].astype(F32) * inv * inner)
        outs[:, c] = v.astype(BF)
    gains[1] = gain_two[...]
    mine = pl.ds(pl.multiple_of(p.gy * 128, 128), 128)
    gcp = []
    for _, _, _, dev in rows:
        at = pl.ds(pl.multiple_of(dev[1] * 128, 128), 128)
        gcp.append(w.send(gains.at[:, :, at], gcame.at[p.gy], dev))
    glocal = w.copy(gains.at[:, :, mine], gcame.at[p.gy])
    each(sq, "s3")
    o = Scatter(w, outs, hid_cols, rows)
    o.s1()
    each(big, "s5")
    each(so, "s5")
    each(sq, "s4")
    for cp in gcp:
        cp.wait_recv()
    glocal.wait()
    gsum[...] = jnp.sum(gcame[...], axis=0)
    lcp = [w.send(gsum, gcame2.at[p.gx], dev) for _, dev in lanes]
    llocal = w.copy(gsum, gcame2.at[p.gx])
    for cp in lcp:
        cp.wait_recv()
    llocal.wait()
    o_gain[...] = jnp.sum(gcame2[...], axis=0)
    each(sq, "s5")
    o.s2()
    w.drain()


def call_third(*args):
    scratch = [
        pltpu.SemaphoreType.DMA((116,)), pltpu.SemaphoreType.DMA((97,)),
        pltpu.VMEM((T, D), BF), pltpu.VMEM((T, D), BF),
        pltpu.VMEM((2, D, 256), BF), pltpu.VMEM((256, D), BF),
        pltpu.VMEM((4, HEAD, T), BF), pltpu.VMEM((2, 256, T), BF), pltpu.VMEM((T, 512), BF),
        pltpu.VMEM((HEAD, T), F32), pltpu.VMEM((HEAD, T), F32), pltpu.VMEM((3 * QB, QB), F32),
        pltpu.VMEM((T, 1), jnp.int32), pltpu.VMEM((1, T), jnp.int32),
        pltpu.VMEM((4, 2, SLAB, D), BF),
        *LineSum.SCRATCH,
        pltpu.VMEM((SLAB, D), BF),
        pltpu.VMEM((2, 8, D), F32),
        pltpu.VMEM((16, 2, 8, 128), F32),
        pltpu.VMEM((2, 8, 128), F32),
        pltpu.VMEM((8, 2, 8, 128), F32),
        pltpu.VMEM((4, 2, 384, 128), BF),
        pltpu.VMEM((4, 2, 128, 256), BF),
        pltpu.VMEM((2, 4, 2, 384, 128), BF),
        pltpu.VMEM((2, 4, 2, 128, 256), BF),
        pltpu.VMEM((2, 4, 2, 256, 512), BF),
        pltpu.VMEM((SLAB, D), BF), pltpu.VMEM((SLAB, D), F32),
        pltpu.VMEM((8, D), F32), pltpu.VMEM((8, D), F32),
        pltpu.VMEM((4, HEAD, T), BF), pltpu.VMEM((HEAD, T), BF), pltpu.VMEM((HEAD, T), BF),
        pltpu.VMEM((4, HEAD, T), BF), pltpu.VMEM((8, T), F32),
        pltpu.VMEM((32, T), F32), pltpu.VMEM((32, T), F32),
    ]
    scratch += WeightSum.scratch(128, 512) * 2
    scratch += WeightSum.scratch(192, 128) * 2 + WeightSum.scratch(64, 256) * 2
    return pl.pallas_call(
        third_kernel,
        out_shape=[
            jax.ShapeDtypeStruct((2 * T, 128), BF),
            jax.ShapeDtypeStruct((2, 8, 128), F32),
            jax.ShapeDtypeStruct((384, 128), F32),
            jax.ShapeDtypeStruct((128, 256), F32),
            jax.ShapeDtypeStruct((256, 512), F32),
        ],
        in_specs=[ANY] * 16 + [VM],
        out_specs=[ANY, VM, VM, VM, VM],
        scratch_shapes=scratch,
        compiler_params=pltpu.CompilerParams(
            collective_id=2, has_side_effects=True, vmem_limit_bytes=62 << 20
        ),
        name="third",
    )(*args)


def outputs_kernel(
    a_cols, a_hid, a_gains, a_qkv, a_o, a_gate, a_up, a_down,
    x_cols, x_hid, x_gain, x_q, x_k, x_v, x_o, x_gain2, x_gate, x_up, x_down,
    sem, cols, hid, gains, qkv,
):
    first = [
        pltpu.make_async_copy(a, b, sem.at[i])
        for i, (a, b) in enumerate(
            ((a_cols, cols), (a_hid, hid), (a_gains, gains), (a_qkv, qkv), (a_o, x_o), (a_gate, x_gate), (a_up, x_up), (a_down, x_down))
        )
    ]
    for cp in first:
        cp.start()
    first[0].wait()
    x_cols[...] = cols[...].astype(F32)
    first[1].wait()
    x_hid[...] = hid[...].astype(F32)
    first[2].wait()
    x_gain[...] = jnp.sum(gains[0], axis=0, keepdims=True)
    x_gain2[...] = jnp.sum(gains[1], axis=0, keepdims=True)
    first[3].wait()
    x_q[...] = qkv[:256]
    kv = qkv[256:].T
    x_k[:, :128] = kv[:32]
    x_k[:, 128:] = kv[64:96]
    x_v[:, :128] = kv[32:64]
    x_v[:, 128:] = kv[96:]
    for cp in first[4:]:
        cp.wait()


def call_outputs(*args):
    shapes = [
        (2 * T, 128), (2 * T, 128), (1, 128), (256, 128), (32, 256), (32, 256), (128, 256), (1, 128),
        (256, 512), (256, 512), (512, 256),
    ]
    return pl.pallas_call(
        outputs_kernel,
        out_shape=[jax.ShapeDtypeStruct(v, F32) for v in shapes],
        in_specs=[ANY] * 8,
        out_specs=[VM] * 11,
        scratch_shapes=[
            pltpu.SemaphoreType.DMA((8,)),
            pltpu.VMEM((2 * T, 128), BF), pltpu.VMEM((2 * T, 128), BF),
            pltpu.VMEM((2, 8, 128), F32), pltpu.VMEM((384, 128), F32),
        ],
        compiler_params=pltpu.CompilerParams(vmem_limit_bytes=62 << 20),
        name="outputs",
    )(*args)


def per_device(
    hidden, attn_gain, wq, wk, wv, wo, ffn_gain, gate, up, down, segments, cotangent,
):
    freq = (ROPE_BASE ** (-np.arange(0, HEAD, 2, dtype=np.float32) / HEAD)).astype(np.float32)[:, None]
    (
        cot, gg, uu, dd, w2, o2, n1, hid_slab, qt, kt, vt, ht, lse, after, n2, act, gain, cos, sin
    ) = call_first(
        hidden, cotangent, gate, up, down, wo, wq, wk.T, wv.T, attn_gain[None], ffn_gain[None], segments, freq
    )
    grad_attn, grad_after, gain_two, out_cols, o_down, o_gate, g_up = call_second(
        n2.reshape(T, D), cot, gg.reshape(2, D, 512), uu.reshape(2, D, 512),
        dd.reshape(2, 8, 512, 256), after, gain, act,
    )
    hid_cols, o_gain, o_qkv, o_o, o_up = call_third(
        grad_attn.reshape(T, D), hid_slab, grad_after, gain, gain_two, w2, o2, n1,
        qt, kt, vt, ht, lse, cos, sin, g_up.reshape(2, 4, 2, 256, 512), segments,
    )
    res = call_outputs(out_cols, hid_cols, o_gain, o_qkv, o_o, o_gate, o_up, o_down)
    return (
        res[0], res[1], res[2].reshape(128), res[3], res[4].T, res[5].T, res[6], res[7].reshape(128), *res[8:],
    )


def solution(mesh):
    wide, cols, tall = P("gx", "gy"), P("gy"), P("gy", "gx")
    return jax.shard_map(
        per_device,
        mesh=mesh,
        in_specs=(wide, cols, wide, wide, wide, tall, cols, wide, wide, tall, P("gx", None), wide),
        out_specs=(wide, wide, cols, wide, wide, wide, tall, cols, wide, wide, tall),
        check_vma=False,
    )
```

```python
import functools

import jax
import jax.numpy as jnp
import numpy as np
from jax import lax
from jax.experimental import pallas as pl
from jax.experimental.pallas import tpu as pltpu
from jax.sharding import PartitionSpec as P

HEAD = 64
EPS = 1e-06
ROPE_BASE = 10000000.0
ATTN_SCALE = 1.0 / 64.0
RES = 0.22
T = 1024
D = 2048
SLAB = 128
QB = 256
BF = jnp.bfloat16
F32 = jnp.float32
MESH = pl.DeviceIdType.MESH
ANY = pl.BlockSpec(memory_space=pl.ANY)
VM = pl.BlockSpec(memory_space=pltpu.VMEM)


class Place:
    def __init__(self):
        gx = lax.axis_index("gx")
        gy = lax.axis_index("gy")
        self.gx, self.gy = gx, gy
        self.x, self.yl = gx // 2, lax.rem(gx, 2)
        self.yh, self.z, self.c = gy // 8, lax.rem(gy // 2, 4), lax.rem(gy, 2)
        self.y = self.yh * 2 + self.yl
        self.r = self.z * 2 + self.c

    def at(self, x=0, y=0, z=0, c=0):
        xx = lax.rem(self.x + x + 4, 4)
        yy = lax.rem(self.y + y + 4, 4)
        zz = lax.rem(self.z + z + 4, 4)
        cc = lax.rem(self.c + c, 2)
        return (xx * 2 + lax.rem(yy, 2), (yy // 2) * 8 + zz * 2 + cc)

    def step(self, axis, k):
        return self.at(**{axis: k})

    def pos(self, axis, k):
        return lax.rem(getattr(self, axis) + k + 4, 4)


class Wire:
    def __init__(self, place, send, recv):
        self.place, self.send_sem, self.recv_sem = place, send, recv
        self.starts, self.lands = 0, 0
        self.sent = []

    def send(self, src, dst, to):
        i, j = self.starts, self.lands
        self.starts, self.lands = i + 1, j + 1
        cp = pltpu.make_async_remote_copy(
            src_ref=src,
            dst_ref=dst,
            send_sem=self.send_sem.at[i],
            recv_sem=self.recv_sem.at[j],
            device_id=to,
            device_id_type=MESH,
        )
        cp.start()
        self.sent.append(cp)
        return cp

    def copy(self, src, dst):
        i = self.starts
        self.starts += 1
        cp = pltpu.make_async_copy(src, dst, self.send_sem.at[i])
        cp.start()
        return cp

    def drain(self):
        for cp in self.sent:
            cp.wait_send()
        self.sent = []


def say_hello(peers):
    for peer in peers:
        pl.semaphore_signal(pltpu.get_barrier_semaphore(), inc=1, device_id=peer, device_id_type=MESH)


def hear_all(peers):
    pl.semaphore_wait(pltpu.get_barrier_semaphore(), len(peers))


def ring_peers(p):
    return [p.at(x=1), p.at(x=-1), p.at(y=1), p.at(y=-1)]


def row_peers(p):
    out = []
    for y in (0, 2):
        for z in range(4):
            for c in range(2):
                if (y, z, c) != (0, 0, 0):
                    out.append((y, z, c, p.at(y=y, z=z, c=c)))
    return out


def line_peers(p):
    return [p.at(c=1), p.at(z=1), p.at(z=-1)]


class WeightGather:
    def __init__(self, wire, src, dst, start, rows, order, stage=None):
        self.w, self.src, self.dst, self.stage = wire, src, dst, stage
        self.r0, self.n, self.order = start, rows, order
        self.a1, self.a2 = ("x", "y") if order == 0 else ("y", "x")

    def one(self, k, half=None):
        p = self.w.place
        x, y = (p.pos("x", k), p.y) if self.a1 == "x" else (p.x, p.pos("y", k))
        return self.dst.at[y // 2, x, lax.rem(y, 2), self.span(half)]

    def four(self, k, half=None):
        p = self.w.place
        if self.a2 == "y":
            y = p.pos("y", k)
            return self.dst.at[y // 2, :, lax.rem(y, 2), self.span(half)]
        return self.dst.at[:, p.pos("x", k), :, self.span(half)]

    def span(self, half):
        if half is None:
            return pl.ds(self.r0, self.n)
        return pl.ds(self.r0 + half * (self.n // 2), self.n // 2)

    def s1(self):
        w, p = self.w, self.w.place
        own = self.src.at[pl.ds(self.r0, self.n)]
        if self.stage is None:
            self.local = w.copy(own, self.one(0))
        else:
            self.local = w.copy(own, self.stage.at[pl.ds(self.r0, self.n)])
        self.up = w.send(own, self.one(0), p.step(self.a1, 1))
        self.down = w.send(own, self.one(0), p.step(self.a1, -1))

    def s2(self):
        w, p = self.w, self.w.place
        if self.stage is not None:
            self.local.wait()
            self.local = w.copy(self.stage.at[pl.ds(self.r0, self.n)], self.one(0))
        self.up.wait_recv()
        self.up2 = w.send(self.one(-1, 0), self.one(-1, 0), p.step(self.a1, 1))
        self.down.wait_recv()
        self.down2 = w.send(self.one(1, 1), self.one(1, 1), p.step(self.a1, -1))

    def s3(self):
        w, p = self.w, self.w.place
        self.local.wait()
        self.up2.wait_recv()
        self.down2.wait_recv()
        self.up3 = w.send(self.four(0), self.four(0), p.step(self.a2, 1))
        self.down3 = w.send(self.four(0), self.four(0), p.step(self.a2, -1))

    def s4(self):
        w, p = self.w, self.w.place
        self.up3.wait_recv()
        self.up4 = w.send(self.four(-1, 0), self.four(-1, 0), p.step(self.a2, 1))
        self.down3.wait_recv()
        self.down4 = w.send(self.four(1, 1), self.four(1, 1), p.step(self.a2, -1))

    def s5(self):
        self.up4.wait_recv()
        self.down4.wait_recv()


class RowGather:
    def __init__(self, wire, src, dst, stage=None):
        self.w, self.src, self.dst, self.stage = wire, src, dst, stage

    def block(self, yh, k, c=None):
        p = self.w.place
        c = p.c if c is None else c
        gy = yh * 8 + p.pos("z", k) * 2 + c
        return self.dst.at[:, pl.ds(pl.multiple_of(gy * 128, 128), 128)]

    def out(self, src, yh, k):
        b = self.block(yh, k)
        self.cores.append(self.w.send(src, b, self.w.place.at(c=1)))

    def s0(self):
        w, p = self.w, self.w.place
        self.cores = []
        mine = self.src.at[pl.ds(pl.multiple_of(p.yh * T, T), T)]
        other = self.src.at[pl.ds(pl.multiple_of((1 - p.yh) * T, T), T)]
        own = self.block(p.yh, 0)
        self.local = w.copy(mine, own if self.stage is None else self.stage)
        self.swap = w.send(other, own, p.at(y=2))

    def s1(self):
        w, p = self.w, self.w.place
        mine = self.src.at[pl.ds(pl.multiple_of(p.yh * T, T), T)]
        own = self.block(p.yh, 0)
        self.up0 = w.send(mine, own, p.at(z=1))
        self.down0 = w.send(mine, own, p.at(z=-1))
        self.out(mine, p.yh, 0)

    def s2(self):
        w, p = self.w, self.w.place
        if self.stage is not None:
            self.local.wait()
            self.local = w.copy(self.stage, self.block(p.yh, 0))
        self.swap.wait_recv()
        b = self.block(1 - p.yh, 0)
        self.up1 = w.send(b, b, p.at(z=1))
        self.down1 = w.send(b, b, p.at(z=-1))
        self.out(b, 1 - p.yh, 0)

    def s3(self):
        w, p = self.w, self.w.place
        self.up0.wait_recv()
        b = self.block(p.yh, -1)
        self.up2 = w.send(b, b, p.at(z=1))
        self.out(b, p.yh, -1)
        self.down0.wait_recv()
        self.out(self.block(p.yh, 1), p.yh, 1)
        self.down1.wait_recv()
        b = self.block(1 - p.yh, 1)
        self.down2 = w.send(b, b, p.at(z=-1))
        self.out(b, 1 - p.yh, 1)
        self.up1.wait_recv()
        self.out(self.block(1 - p.yh, -1), 1 - p.yh, -1)

    def s4(self):
        p = self.w.place
        self.up2.wait_recv()
        self.out(self.block(p.yh, 2), p.yh, 2)
        self.down2.wait_recv()
        self.out(self.block(1 - p.yh, 2), 1 - p.yh, 2)

    def s5(self):
        self.local.wait()
        for cp in self.cores:
            cp.wait_recv()


def add_rows(dst, srcs, rows):
    step = max(16, min(rows, 32768 // dst.shape[-1]))
    while rows % step:
        step //= 2

    def body(i, carry):
        at = pl.ds(pl.multiple_of(i * step, step), step)
        total = srcs[0][at].astype(F32)
        for v in srcs[1:]:
            total = total + v[at].astype(F32)
        dst[at] = total.astype(dst.dtype)
        return carry

    lax.fori_loop(0, rows // step, body, 0)


class LineSum:
    SCRATCH = [
        pltpu.VMEM((4, SLAB, D), BF),
        pltpu.VMEM((2, SLAB // 2, D), BF),
        pltpu.VMEM((2, SLAB, D), BF),
    ]
    ORDER = (2, 1, -1, 0)

    def __init__(self, wire, part, got, far, near):
        self.w, self.part, self.got = wire, part, got
        self.far, self.near = far, near
        self.core = {}
        self.last = []

    def mine(self, k, half=None):
        p = self.w.place
        if half is None:
            return self.part.at[p.pos("z", k), p.c]
        return self.part.at[p.pos("z", k), p.c, pl.ds(half * (SLAB // 2), SLAB // 2)]

    def push(self, k):
        w, p = self.w, self.w.place
        z = p.pos("z", k)
        self.core[k] = w.send(self.part.at[z, 1 - p.c], self.got.at[z], p.at(c=1))

    def merge(self, k):
        z = self.w.place.pos("z", k)
        self.core[k].wait_recv()
        add_rows(self.mine(k), [self.mine(k), self.got.at[z]], SLAB)

    def send_far(self):
        w, p = self.w, self.w.place
        self.up = w.send(self.mine(2, 0), self.far.at[0], p.at(z=1))
        self.down = w.send(self.mine(2, 1), self.far.at[1], p.at(z=-1))

    def near_first(self, i):
        self.near_half(1 if i == 0 else -1, i, 1 - i)

    def near_second(self, i):
        k, far = (1, self.up) if i == 0 else (-1, self.down)
        far.wait_recv()
        add_rows(self.mine(k, i), [self.mine(k, i), self.far.at[i]], SLAB // 2)
        self.near_half(k, i, i)

    def near_half(self, k, i, h):
        at = pl.ds(h * (SLAB // 2), SLAB // 2)
        self.last.append(self.w.send(self.mine(k, h), self.near.at[i, at], self.w.place.at(z=k)))

    def after_block(self, t):
        self.push(self.ORDER[t])
        if t == 1:
            self.merge(2)
            self.send_far()
        if t == 2:
            self.merge(1)
            self.near_first(0)
        if t == 3:
            self.merge(-1)
            self.near_first(1)
            self.merge(0)

    def finish(self):
        self.near_second(0)
        self.near_second(1)

    def wait(self):
        for cp in self.last:
            cp.wait_recv()

    def total(self, at):
        p = self.w.place
        return (
            self.part[p.z, p.c, :, at].astype(F32)
            + self.near[0, :, at].astype(F32)
            + self.near[1, :, at].astype(F32)
        )


class LineGather:
    def __init__(self, wire, src, dst):
        self.w, self.src, self.dst = wire, src, dst

    def slot(self, k, half=None):
        p = self.w.place
        if half is None:
            return self.dst.at[p.pos("z", k), p.c]
        return self.dst.at[p.pos("z", k), p.c, pl.ds(half * (SLAB // 2), SLAB // 2)]

    def s1(self):
        w, p = self.w, self.w.place
        self.up = w.send(self.src, self.slot(0), p.at(z=1))
        self.down = w.send(self.src, self.slot(0), p.at(z=-1))
        self.cores = [w.send(self.src, self.slot(0), p.at(c=1))]
        self.local = w.copy(self.src, self.slot(0))

    def s2(self):
        w, p = self.w, self.w.place
        self.up.wait_recv()
        self.up2 = w.send(self.slot(-1, 0), self.slot(-1, 0), p.at(z=1))
        self.cores.append(w.send(self.slot(-1), self.slot(-1), p.at(c=1)))
        self.down.wait_recv()
        self.down2 = w.send(self.slot(1, 1), self.slot(1, 1), p.at(z=-1))
        self.cores.append(w.send(self.slot(1), self.slot(1), p.at(c=1)))

    def s3(self):
        w, p = self.w, self.w.place
        self.up2.wait_recv()
        self.cores.append(w.send(self.slot(2, 0), self.slot(2, 0), p.at(c=1)))
        self.down2.wait_recv()
        self.cores.append(w.send(self.slot(2, 1), self.slot(2, 1), p.at(c=1)))

    def s4(self):
        self.local.wait()
        for cp in self.cores:
            cp.wait_recv()


class Scatter:
    def __init__(self, wire, src, dst, rows):
        self.w, self.src, self.dst, self.rows = wire, src, dst, rows

    def s1(self):
        w, p = self.w, self.w.place
        mine = self.dst.at[pl.ds(pl.multiple_of(p.yh * T + p.r * SLAB, SLAB), SLAB)]
        self.copies = []
        for y, z, c, dev in self.rows:
            at = pl.ds(pl.multiple_of(dev[1] * 128, 128), 128)
            self.copies.append(w.send(self.src.at[:, at], mine, dev))
        at = pl.ds(pl.multiple_of(p.gy * 128, 128), 128)
        self.local = w.copy(self.src.at[:, at], mine)

    def s2(self):
        self.local.wait()
        for cp in self.copies:
            cp.wait_recv()


def each_rows(rows, step, f):
    def body(i, carry):
        f(pl.ds(pl.multiple_of(i * step, step), step))
        return carry

    lax.fori_loop(0, rows // step, body, 0)


COLS = [slice(j * 128, (j + 1) * 128) for j in range(16)]


def contract(a, b, da, db):
    return lax.dot_general(a, b, (((da,), (db,)), ((), ())), preferred_element_type=F32)


def rows_of(i, n):
    return pl.ds(pl.multiple_of(i * n, n), n)


def row_mean(parts):
    total = parts[0]
    for v in parts[1:]:
        total = total + v
    return jnp.sum(total, axis=1, keepdims=True) * (1.0 / D)


def norm_scale(load):
    squares = []
    total = None
    for at in COLS:
        v = load(at)
        total = v * v if total is None else total + v * v
    return lax.rsqrt(jnp.sum(total, axis=1, keepdims=True) * (1.0 / D) + EPS)


def unpack(packed, wide, out_rows, j):
    for g in range(8):
        src = packed.at[g // 2, g % 2]
        wide[g * 256 : (g + 1) * 256, :128] = src[:256]
        kv = src[256:384]
        wide[g * 256 : g * 256 + 128, 128:192] = kv[:, :64]
        wide[g * 256 + 128 : (g + 1) * 256, 128:192] = kv[:, 64:]
        out_rows[rows_of(j, 128), g * 256 : g * 256 + 128] = src[384:512]
        out_rows[rows_of(j, 128), g * 256 + 128 : (g + 1) * 256] = src[512:]


def key_window(i):
    return pl.multiple_of(jnp.maximum(i - 2, 0) * QB, QB)


def pick_segment(p, segs, seg_row, seg_col):
    row = jnp.where(p.yh == 0, segs[0:1], segs[1:2])
    seg_row[...] = row
    wide = jnp.broadcast_to(row.astype(F32), (128, T)).T
    seg_col[...] = wide[:, 0:1].astype(jnp.int32)


def bias_tile(seg_col, seg_row, lo, n, i):
    first = i * QB
    same = seg_col[pl.ds(lo, n)] == seg_row[:, pl.ds(first, QB)]
    rows = lo + lax.broadcasted_iota(jnp.int32, (n, QB), 0)
    cols = first + lax.broadcasted_iota(jnp.int32, (n, QB), 1)
    return jnp.where(same & (rows <= cols), 0.0, -1e30)


def first_kernel(
    hidden, cot, gate, up, down, wo, wq, wkt, wvt, gain_a, gain_b, segs, freq,
    c_out, g_out, u_out, d_out, w2_out, o2_out, n1_out, slab_out, qt_out, kt_out, vt_out, ht_out,
    lse_out, after_out, n2_out, act_out, gain_out, cos_out, sin_out,
    send, recv, h, n1, q_tmp, q_got, w2, o2, qt, kt, vt, ht, part, got, far, near,
    after, normed, gain, seg_col, seg_row, cos, sin, bias, lse, v_cot, v_gate, v_up, v_down,
    dw, cv, act, v_q, gains,
):
    p = Place()
    w = Wire(p, send, recv)
    rows = row_peers(p)
    peers = ring_peers(p) + [dev for _, _, _, dev in rows]
    say_hello(peers)
    v_q[:256] = wq[...]
    kv = [wkt[:, :128], wvt[:, :128], wkt[:, 128:], wvt[:, 128:]]
    v_q[256:384] = jnp.concatenate(kv, axis=0).astype(F32).T.astype(BF)
    v_q[384:512] = wo[:, :128]
    v_q[512:] = wo[:, 128:]
    gains[...] = jnp.zeros_like(gains)
    gains[0:1] = gain_a[...]
    gains[1:2] = gain_b[...]
    pick_segment(p, segs, seg_row, seg_col)
    earlier = jnp.zeros((8, T), F32)
    for b in range(8):
        less = seg_col[b * 128 : (b + 1) * 128] < seg_row[...]
        earlier = earlier + jnp.sum(jnp.where(less, 1.0, 0.0).reshape(16, 8, T), axis=0)
    starts = jnp.sum(earlier, axis=0, keepdims=True)
    places = lax.broadcasted_iota(jnp.int32, (1, T), 1).astype(F32) - starts
    turned = freq[...] * places
    cos[...] = jnp.cos(turned)
    sin[...] = jnp.sin(turned)

    hear_all(peers)
    hg = RowGather(w, hidden, h)
    cg = RowGather(w, cot, c_out, v_cot)
    aq = [WeightGather(w, v_q, q_tmp, 320 * i, 320, i) for i in range(2)]
    gu = [WeightGather(w, gate, g_out, 0, 256, 0, v_gate), WeightGather(w, up, u_out, 0, 256, 1, v_up)]
    dn = [WeightGather(w, down, d_out, 256 * i, 256, i, v_down) for i in range(2)]

    def each(group, stage):
        for b in group:
            getattr(b, stage)()

    each(aq, "s1")
    hg.s0()
    hg.s1()
    own = pl.ds(pl.multiple_of(p.gy * 128, 128), 128)
    glocal = w.copy(gains, gain.at[:, own])
    gcopies = [w.send(gains, gain.at[:, own], dev) for _, _, _, dev in rows]

    each(aq, "s2")
    each(aq, "s3")
    hg.s2()
    each(dn, "s1")
    cg.s0()
    each(aq, "s4")
    hg.s3()
    each(aq, "s5")
    q_swap = w.send(q_tmp.at[1 - p.c], q_got, p.at(c=1))
    unpack(q_tmp.at[p.c], w2.at[p.c], o2, p.c)
    each(dn, "s2")
    hg.s4()
    cg.s1()
    each(gu, "s1")
    q_swap.wait_recv()
    unpack(q_got, w2.at[1 - p.c], o2, 1 - p.c)
    hg.s5()
    cg.s2()
    glocal.wait()
    for cp in gcopies:
        cp.wait_recv()

    def project(i, carry):
        at = rows_of(i, QB)
        inv = norm_scale(lambda c: h[at, c].astype(F32))
        for c in COLS:
            n1[at, c] = (h[at, c].astype(F32) * inv * gain[0:1, c]).astype(BF)
        ct, st = cos[:, at], sin[:, at]
        keys = []
        for j in range(2):
            lin = contract(n1[at], w2[j, :, :192], 1, 0)
            qj = lin[:, :128].T
            kv = lin[:, 128:].T
            for hh in range(2):
                a, b = qj[hh * 64 : hh * 64 + 32], qj[hh * 64 + 32 : hh * 64 + 64]
                qt[2 * j + hh, 0:32, at] = (a * ct - b * st).astype(BF) * ATTN_SCALE
                qt[2 * j + hh, 32:64, at] = (b * ct + a * st).astype(BF) * ATTN_SCALE
            keys.append(kv[:32])
            vt[j * 32 : (j + 1) * 32, at] = kv[32:].astype(BF)
        a, b = keys
        kt[0:32, at] = (a * ct - b * st).astype(BF)
        kt[32:64, at] = (b * ct + a * st).astype(BF)
        return carry

    lax.fori_loop(0, 4, project, 0)
    exports = [
        w.copy(w2, w2_out), w.copy(o2, o2_out),
        w.copy(n1, n1_out),
        w.copy(h.at[pl.ds(pl.multiple_of(p.r * SLAB, SLAB), SLAB)], slab_out),
        w.copy(qt, qt_out), w.copy(kt, kt_out), w.copy(vt, vt_out),
    ]
    each(dn, "s3")
    gain_out[...] = gain[...]
    cos_out[...] = cos[...]
    sin_out[...] = sin[...]
    s = LineSum(w, part, got, far, near)

    def attend(t):
        i = p.pos("z", LineSum.ORDER[t])
        lo = key_window(i)
        at = rows_of(i, QB)
        keys = pl.ds(lo, 3 * QB)
        bias[...] = bias_tile(seg_col, seg_row, lo, 3 * QB, pl.multiple_of(i, 1))

        def head(n, carry):
            sc = contract(kt[:, keys], qt[n, :, at], 0, 0) + bias[...]
            top = jnp.max(sc, axis=0, keepdims=True)
            e = jnp.exp(sc - top)
            total = jnp.sum(e, axis=0, keepdims=True)
            o = contract(vt[:, keys], e.astype(BF), 1, 0) * (1.0 / total)
            ht[n, :, at] = o.astype(BF)
            lse[pl.ds(n, 1), at] = top + jnp.log(total)
            return carry

        lax.fori_loop(0, 4, head, 0)

    def out_project(t):
        i = p.pos("z", LineSum.ORDER[t])
        block = ht[:, :, rows_of(i, QB)].reshape(256, QB)
        for b in range(4):
            cols = slice(b * 512, (b + 1) * 512)
            o = contract(block, o2[:, cols], 0, 0).astype(BF)
            part[i, 0, :, cols] = o[:SLAB]
            part[i, 1, :, cols] = o[SLAB:]
        s.after_block(t)

    attend(0)
    out_project(0)
    each(gu, "s2")
    attend(1)
    out_project(1)
    cg.s3()
    attend(2)
    out_project(2)
    attend(3)
    out_project(3)
    exports += [w.copy(ht, ht_out), w.copy(lse, lse_out)]
    s.finish()
    each(dn, "s4")
    each(gu, "s3")
    cg.s4()
    s.wait()
    slab = pl.ds(pl.multiple_of(p.r * SLAB, SLAB), SLAB)
    for c in COLS:
        after[:, c] = h[slab, c].astype(F32) + RES * s.total(c)
    inv = norm_scale(lambda c: after[:, c])
    for c in COLS:
        normed[:, c] = (after[:, c] * inv * gain[1:2, c]).astype(BF)
    g = LineGather(w, normed, n2_out)
    g.s1()
    exports.append(w.copy(after, after_out))
    each(dn, "s5")
    loads = [
        w.copy(d_out.at[j, g // 2, g % 2], dw.at[j, :, pl.ds(g * 256, 256)]) for j in range(2) for g in range(8)
    ]
    cg.s5()
    loads.append(w.copy(c_out, cv))
    for cp in loads:
        cp.wait()

    def act_grad(i, carry):
        at = rows_of(i, 512)
        for j in range(2):
            act[j, at] = (RES * contract(cv[at], dw[j], 1, 1)).astype(BF)
        return carry

    lax.fori_loop(0, 2, act_grad, 0)
    exports.append(w.copy(act, act_out))
    g.s2()
    each(gu, "s4")
    g.s3()
    w.drain()
    each(gu, "s5")
    g.s4()
    for cp in exports:
        cp.wait()
    w.drain()


def call_first(*args):
    shapes = [
        ((T, D), BF),
        ((2, 4, 2, 256, 512), BF), ((2, 4, 2, 256, 512), BF), ((2, 4, 2, 512, 256), BF),
        ((2, D, 256), BF), ((256, D), BF),
        ((T, D), BF), ((SLAB, D), BF),
        ((4, HEAD, T), BF), ((HEAD, T), BF), ((HEAD, T), BF), ((4, HEAD, T), BF),
        ((8, T), F32), ((SLAB, D), F32), ((4, 2, SLAB, D), BF), ((2, T, 512), BF),
        ((8, D), F32), ((32, T), F32), ((32, T), F32),
    ]
    out_specs = [ANY] * 16 + [VM] * 3
    scratch = [
        pltpu.SemaphoreType.DMA((156,)), pltpu.SemaphoreType.DMA((113,)),
        pltpu.VMEM((T, D), BF), pltpu.VMEM((T, D), BF),
        pltpu.VMEM((2, 4, 2, 640, 128), BF), pltpu.VMEM((4, 2, 640, 128), BF),
        pltpu.VMEM((2, D, 256), BF), pltpu.VMEM((256, D), BF),
        pltpu.VMEM((4, HEAD, T), BF), pltpu.VMEM((HEAD, T), BF), pltpu.VMEM((HEAD, T), BF),
        pltpu.VMEM((4, HEAD, T), BF), pltpu.VMEM((4, 2, SLAB, D), BF),
        *LineSum.SCRATCH,
        pltpu.VMEM((SLAB, D), F32), pltpu.VMEM((SLAB, D), BF),
        pltpu.VMEM((8, D), F32), pltpu.VMEM((T, 1), jnp.int32), pltpu.VMEM((1, T), jnp.int32),
        pltpu.VMEM((32, T), F32), pltpu.VMEM((32, T), F32), pltpu.VMEM((3 * QB, QB), F32),
        pltpu.VMEM((8, T), F32),
        pltpu.VMEM((T, 128), BF), pltpu.VMEM((256, 512), BF), pltpu.VMEM((256, 512), BF),
        pltpu.VMEM((512, 256), BF),
        pltpu.VMEM((2, 512, D), BF), pltpu.VMEM((T, D), BF), pltpu.VMEM((2, T, 512), BF),
        pltpu.VMEM((640, 128), BF), pltpu.VMEM((8, 128), F32),
    ]
    return pl.pallas_call(
        first_kernel,
        out_shape=[jax.ShapeDtypeStruct(s, d) for s, d in shapes],
        in_specs=[ANY] * 5 + [VM] * 8,
        out_specs=out_specs,
        scratch_shapes=scratch,
        compiler_params=pltpu.CompilerParams(
            collective_id=0, has_side_effects=True, vmem_limit_bytes=62 << 20
        ),
        name="first",
    )(*args)


class WeightSum:
    @staticmethod
    def scratch(rows, cols):
        h = rows // 2
        return [
            pltpu.VMEM((2, 4, h, cols), BF),
            pltpu.VMEM((2, 4, rows, cols), BF),
            pltpu.VMEM((2, h, cols), BF),
            pltpu.VMEM((2, rows, cols), BF),
        ]

    def __init__(self, wire, part, out, start, rows, order, far, came, far2, came2):
        self.w, self.part, self.out = wire, part, out
        self.r0, self.n = start, rows
        self.a1, self.a2 = ("y", "x") if order == 0 else ("x", "y")
        self.far, self.came, self.far2, self.came2 = far, came, far2, came2

    def span(self, half):
        if half is None:
            return pl.ds(self.r0, self.n)
        return pl.ds(self.r0 + half * (self.n // 2), self.n // 2)

    def src(self, k, j, half=None):
        p = self.w.place
        if self.a1 == "y":
            y = p.pos("y", k)
            return self.part.at[y // 2, j, lax.rem(y, 2), self.span(half)]
        return self.part.at[j // 2, p.pos("x", k), lax.rem(j, 2), self.span(half)]

    def four(self, k, half=None, part=None):
        p = self.w.place
        part = self.part if part is None else part
        if self.a1 == "y":
            y = p.pos("y", k)
            return part.at[y // 2, :, lax.rem(y, 2), self.span(half)]
        return part.at[:, p.pos("x", k), :, self.span(half)]

    def land(self, ref, i):
        if self.a1 == "y":
            return ref.at[i]
        return ref.reshape(2, 2, 2, *ref.shape[2:]).at[i]

    def s1(self, part=None):
        w, p = self.w, self.w.place
        self.up = w.send(self.four(2, 0, part), self.land(self.far, 0), p.step(self.a1, 1))
        self.down = w.send(self.four(2, 1, part), self.land(self.far, 1), p.step(self.a1, -1))

    def s2(self):
        w, p = self.w, self.w.place
        h = self.n // 2
        self.up.wait_recv()
        for j in range(4):
            a = self.src(1, j, 0)
            add_rows(a, [a, self.far.at[0, j]], h)
        self.up2 = w.send(self.four(1), self.land(self.came, 0), p.step(self.a1, 1))
        self.down.wait_recv()
        for j in range(4):
            a = self.src(-1, j, 1)
            add_rows(a, [a, self.far.at[1, j]], h)
        self.down2 = w.send(self.four(-1), self.land(self.came, 1), p.step(self.a1, -1))

    def s3(self):
        w, p = self.w, self.w.place
        self.up2.wait_recv()
        self.down2.wait_recv()
        for k in (2, 1, -1, 0):
            j = p.pos(self.a2, k)
            a = self.src(0, j)
            add_rows(a, [a, self.came.at[0, j], self.came.at[1, j]], self.n)
            if k == 2:
                self.up3 = w.send(self.src(0, j, 0), self.far2.at[0], p.step(self.a2, 1))
                self.down3 = w.send(self.src(0, j, 1), self.far2.at[1], p.step(self.a2, -1))

    def s4(self):
        w, p = self.w, self.w.place
        h = self.n // 2
        self.up3.wait_recv()
        j = p.pos(self.a2, 1)
        a = self.src(0, j, 0)
        add_rows(a, [a, self.far2.at[0]], h)
        self.up4 = w.send(self.src(0, j), self.came2.at[0], p.step(self.a2, 1))
        self.down3.wait_recv()
        j = p.pos(self.a2, -1)
        a = self.src(0, j, 1)
        add_rows(a, [a, self.far2.at[1]], h)
        self.down4 = w.send(self.src(0, j), self.came2.at[1], p.step(self.a2, -1))

    def s5(self):
        self.up4.wait_recv()
        self.down4.wait_recv()
        j = self.w.place.pos(self.a2, 0)
        add_rows(
            self.out.at[pl.ds(self.r0, self.n)],
            [self.src(0, j), self.came2.at[0], self.came2.at[1]],
            self.n,
        )


def second_kernel(
    n2_in, cot_in, g_in, u_in, d_in, after_in, gain_in, act_in,
    attn_out, grad_after_out, gain_part, outs_out, o_down, o_gate, gu_out,
    send, recv, n2, pg, gw, uw, dw, ggp, ha, gup, gd, pf, attn, outs, after, gain, slab, v_down, v_gate, *sc,
):
    p = Place()
    w = Wire(p, send, recv)
    peers = ring_peers(p)
    say_hello(peers + line_peers(p))
    cot = pg.reshape(T, D)
    loads = []
    for j in range(2):
        part = [w.copy(g_in.at[j], gw.at[j]), w.copy(u_in.at[j], uw.at[j]), w.copy(act_in.at[j], ggp.at[j])]
        part += [w.copy(n2_in, n2)] if j == 0 else []
        loads.append(part)
    l_d = [w.copy(d_in.at[j, g], dw.at[j, :, pl.ds(g * 256, 256)]) for j in range(2) for g in range(8)]
    l_c = w.copy(cot_in, cot)
    l_s = [
        w.copy(after_in, after), w.copy(gain_in, gain),
    ]
    hear_all(peers + line_peers(p))
    f = LineSum(w, pf, *sc[0:3])
    s = LineSum(w, pg, *sc[3:6])
    down = [WeightSum(w, gd, v_down, 256 * i, 256, i, *sc[6 + 4 * i : 10 + 4 * i]) for i in range(2)]
    gparts = gw.reshape(2, 4, 2, 256, 512)
    gates = [WeightSum(w, gparts, v_gate, 128 * i, 128, i, *sc[14 + 4 * i : 18 + 4 * i]) for i in range(2)]

    def each(group, stage):
        for b in group:
            getattr(b, stage)()

    for t, k in enumerate(LineSum.ORDER):
        i = p.pos("z", k)
        at = rows_of(i, QB)

        def units(j, carry):
            gate = contract(n2[at], gw[j], 1, 0)
            upp = contract(n2[at], uw[j], 1, 0)
            ga = ggp[j, at].astype(F32)
            sig = 1.0 / (1.0 + jnp.exp(-gate))
            silu = gate * sig
            ha[j, at] = (silu * upp).astype(BF)
            ggp[j, at] = (ga * upp * sig * (1.0 + gate * (1.0 - sig))).astype(BF)
            gup[j, at] = (ga * silu).astype(BF)
            return carry

        if t == 0:
            for j in range(2):
                for cp in loads[j]:
                    cp.wait()
                units(j, 0)
            for cp in l_d:
                cp.wait()
        else:
            lax.fori_loop(0, 2, units, 0)
        for b in range(4):
            cols = slice(b * 512, (b + 1) * 512)
            o = (contract(ha[0, at], dw[0, :, cols], 1, 0) + contract(ha[1, at], dw[1, :, cols], 1, 0)).astype(BF)
            pf[i, 0, :, cols] = o[:SLAB]
            pf[i, 1, :, cols] = o[SLAB:]
        f.after_block(t)

    def down_grad(g, carry):
        at = rows_of(g, 512)
        for j in range(2):
            v = (RES * contract(ha[j], cot[:, at], 0, 0)).astype(BF)
            gd[j, g, 0] = v[:, :256]
            gd[j, g, 1] = v[:, 256:]
        return carry

    l_c.wait()
    lax.fori_loop(0, 4, down_grad, 0)
    slab[...] = cot[rows_of(p.r, SLAB)]
    f.finish()
    each(down, "s1")
    for t, k in enumerate(LineSum.ORDER):
        i = p.pos("z", k)
        at = rows_of(i, QB)
        for b in range(4):
            cols = slice(b * 512, (b + 1) * 512)
            o = contract(ggp[0, at], gw[0, cols], 1, 1) + contract(gup[0, at], uw[0, cols], 1, 1)
            o = o + contract(ggp[1, at], gw[1, cols], 1, 1) + contract(gup[1, at], uw[1, cols], 1, 1)
            o = o.astype(BF)
            pg[i, 0, :, cols] = o[:SLAB]
            pg[i, 1, :, cols] = o[SLAB:]
        s.after_block(t)
        if t == 1:
            each(down, "s2")

    def gate_grad(g, carry):
        at = rows_of(g, 512)
        for j in range(2):
            gw[j, at] = contract(n2[:, at], ggp[j], 0, 0).astype(BF)
        return carry

    def up_grad(g, carry):
        at = rows_of(g, 512)
        for j in range(2):
            uw[j, at] = contract(n2[:, at], gup[j], 0, 0).astype(BF)
        return carry

    lax.fori_loop(0, 1, gate_grad, 0)
    s.finish()
    lax.fori_loop(1, 4, gate_grad, 0)
    each(gates, "s1")
    lax.fori_loop(0, 2, up_grad, 0)
    each(down, "s3")
    for cp in l_s:
        cp.wait()
    f.wait()
    for c in COLS:
        outs[:, c] = (after[:, c] + RES * f.total(c)).astype(BF)
    s.wait()
    inv = norm_scale(lambda c: after[:, c])
    total = None
    for c in COLS:
        g = s.total(c)
        scaled = after[:, c] * inv
        gs = g * scaled
        gain_part[:, c] = jnp.sum(gs.reshape(SLAB // 8, 8, 128), axis=0)
        e = gs * gain[1:2, c]
        total = e if total is None else total + e
    inner = jnp.sum(total, axis=1, keepdims=True) * (1.0 / D)
    for c in COLS:
        e = s.total(c) * gain[1:2, c]
        v = slab[:, c].astype(F32) + inv * (e - after[:, c] * inv * inner)
        after[:, c] = v
        attn[:, c] = (RES * v).astype(BF)
    a = LineGather(w, attn, attn_out)
    a.s1()
    each(gates, "s2")
    lax.fori_loop(2, 4, up_grad, 0)
    e_u = w.copy(uw, gu_out)
    each(down, "s4")
    a.s2()
    each(gates, "s3")
    each(down, "s5")
    e_out = [w.copy(after, grad_after_out), w.copy(v_down, o_down), w.copy(outs, outs_out)]
    a.s3()
    each(gates, "s4")
    a.s4()
    w.drain()
    each(gates, "s5")
    e_out.append(w.copy(v_gate, o_gate))
    e_u.wait()
    for cp in e_out:
        cp.wait()
    w.drain()


def call_second(*args):
    scratch = [
        pltpu.SemaphoreType.DMA((93,)), pltpu.SemaphoreType.DMA((61,)),
        pltpu.VMEM((T, D), BF), pltpu.VMEM((4, 2, SLAB, D), BF),
        pltpu.VMEM((2, D, 512), BF), pltpu.VMEM((2, D, 512), BF), pltpu.VMEM((2, 512, D), BF),
        pltpu.VMEM((2, T, 512), BF), pltpu.VMEM((2, T, 512), BF), pltpu.VMEM((2, T, 512), BF),
        pltpu.VMEM((2, 4, 2, 512, 256), BF),
        pltpu.VMEM((4, 2, SLAB, D), BF),
        pltpu.VMEM((SLAB, D), BF), pltpu.VMEM((SLAB, D), BF), pltpu.VMEM((SLAB, D), F32),
        pltpu.VMEM((8, D), F32), pltpu.VMEM((SLAB, D), BF),
        pltpu.VMEM((512, 256), F32), pltpu.VMEM((256, 512), F32),
    ]
    scratch += LineSum.SCRATCH * 2
    scratch += WeightSum.scratch(256, 256) * 2 + WeightSum.scratch(128, 512) * 2
    return pl.pallas_call(
        second_kernel,
        out_shape=[
            jax.ShapeDtypeStruct((4, 2, SLAB, D), BF),
            jax.ShapeDtypeStruct((SLAB, D), F32),
            jax.ShapeDtypeStruct((8, D), F32),
            jax.ShapeDtypeStruct((SLAB, D), BF),
            jax.ShapeDtypeStruct((512, 256), F32),
            jax.ShapeDtypeStruct((256, 512), F32),
            jax.ShapeDtypeStruct((2, D, 512), BF),
        ],
        in_specs=[ANY] * 8,
        out_specs=[ANY, ANY, VM, ANY, ANY, ANY, ANY],
        scratch_shapes=scratch,
        compiler_params=pltpu.CompilerParams(
            collective_id=1, has_side_effects=True, vmem_limit_bytes=62 << 20
        ),
        name="second",
    )(*args)


def key_range(i):
    return max(0, (i - 2) * QB), (i + 1) * QB


def third_kernel(
    ga_in, hid_in, grad_after_in, gain_in, gain_two_in, w2_in, o_in, n1_in, qt_in, kt_in, vt_in, ht_in,
    lse_in, cos_in, sin_in, gu_in, outs_in, segs,
    out_cols, hid_cols, o_gain, o_q, o_o, o_up,
    send, recv, ga, n1, w2, o2, ght, gt, gn, gk, gv, bias, seg_col, seg_row,
    part, got, far, near, outs, gains, gcame, gsum, gcame2, tq, to, rq, ro, gu,
    hid, grad_after, gain, gain_two, qt, kt, vt, ht, lse, cos, sin, *sc,
):
    p = Place()
    w = Wire(p, send, recv)
    rows = row_peers(p)
    lanes = [(k, (lax.rem(p.gx + k, 8), p.gy)) for k in range(1, 8)]
    peers = [dev for _, _, _, dev in rows] + [dev for _, dev in lanes] + [p.at(y=1), p.at(y=-1)]
    say_hello(peers)
    l_ga = [w.copy(ga_in, ga), w.copy(o_in, o2), w.copy(ht_in, ht)]
    l_qk = [w.copy(a, b) for a, b in ((qt_in, qt), (kt_in, kt), (vt_in, vt), (lse_in, lse), (cos_in, cos), (sin_in, sin))]
    hear_all(peers)
    big = [WeightSum(w, gu, o_up, 128 * i, 128, i, *sc[4 * i : 4 * i + 4]) for i in range(2)]
    sq = [WeightSum(w, rq, o_q, 192 * i, 192, i, *sc[8 + 4 * i : 12 + 4 * i]) for i in range(2)]
    so = [WeightSum(w, ro, o_o, 64 * i, 64, i, *sc[16 + 4 * i : 20 + 4 * i]) for i in range(2)]

    def each(group, stage):
        for b in group:
            getattr(b, stage)()

    for b in big:
        b.s1(gu_in)
    l_big = [w.copy(gu_in, gu)]
    l_n1 = w.copy(n1_in, n1)
    l_w2 = [w.copy(w2_in, w2)]
    l_s = [w.copy(a, b) for a, b in ((hid_in, hid), (grad_after_in, grad_after), (gain_in, gain), (gain_two_in, gain_two))]
    pick_segment(p, segs, seg_row, seg_col)
    gk[...] = jnp.zeros_like(gk)
    gv[...] = jnp.zeros_like(gv)
    gt[:, 192:] = jnp.zeros((2, 64, T), BF)
    for cp in l_ga:
        cp.wait()

    def heads_grad(i, carry):
        at = rows_of(i, QB)
        ght[:, :, at] = contract(o2[...], ga[at], 1, 1).astype(BF).reshape(4, HEAD, QB)
        return carry

    lax.fori_loop(0, 4, heads_grad, 0)

    def out_grad(dst, j):
        hj = ht[pl.ds(j * 2, 2)].reshape(128, T)
        for g in range(8):
            dst[g // 2, g % 2] = contract(hj, ga[:, g * 256 : (g + 1) * 256], 1, 0).astype(BF)

    out_grad(to, 1 - p.c)
    swap_o = w.send(to, ro.at[p.c], p.at(c=1))
    out_grad(ro.at[p.c], p.c)
    for cp in l_qk:
        cp.wait()
    for i in range(4):
        lo, hi = key_range(i)
        at = slice(i * QB, (i + 1) * QB)
        bias[: hi - lo] = bias_tile(seg_col, seg_row, lo, hi - lo, i)

        def head(n, carry):
            q = qt[n, :, at]
            g = ght[n, :, at]
            sc_ = contract(kt[:, lo:hi], q, 0, 0) + bias[: hi - lo]
            pr = jnp.exp(sc_ - lse[pl.ds(n, 1), at])
            gp = contract(vt[:, lo:hi], g, 0, 0)
            inner = jnp.sum(ht[n, :, at].astype(F32) * g.astype(F32), axis=0, keepdims=True)
            gs = (pr * (gp - inner)).astype(BF)
            gq = contract(kt[:, lo:hi], gs, 1, 0) * ATTN_SCALE
            a, b = gq[:32], gq[32:]
            first = pl.multiple_of(lax.rem(n, 2) * 64, 64)
            gt[n // 2, pl.ds(first, 32), at] = (a * cos[:, at] + b * sin[:, at]).astype(BF)
            gt[n // 2, pl.ds(first + 32, 32), at] = (b * cos[:, at] - a * sin[:, at]).astype(BF)
            gk[:, lo:hi] += contract(q, gs, 1, 1)
            gv[:, lo:hi] += contract(g, pr.astype(BF), 1, 1)
            return carry

        lax.fori_loop(0, 4, head, 0)
        if i == 0:
            swap_o.wait_recv()
            each(so, "s1")
            x = Scatter(w, outs_in, out_cols, rows)
            x.s1()
        if i == 1:
            for cp in l_big:
                cp.wait()
            each(big, "s2")
        if i == 2:
            each(so, "s2")
    a, b = gk[:32], gk[32:]
    gt[0, 128:160] = (a * cos[...] + b * sin[...]).astype(BF)
    gt[1, 128:160] = (b * cos[...] - a * sin[...]).astype(BF)
    gt[0, 160:192] = gv[:32].astype(BF)
    gt[1, 160:192] = gv[32:].astype(BF)
    other = 1 - p.c
    for i in range(4):
        gn[i * QB : (i + 1) * QB, :256] = gt[other, :, i * QB : (i + 1) * QB].T
        gn[i * QB : (i + 1) * QB, 256:] = gt[p.c, :, i * QB : (i + 1) * QB].T
    for cp in l_w2:
        cp.wait()
    s = LineSum(w, part, got, far, near)
    for t, k in enumerate(LineSum.ORDER):
        i = p.pos("z", k)
        at = rows_of(i, QB)
        for b in range(4):
            cols = slice(b * 512, (b + 1) * 512)
            o = contract(gn[at, :192], w2[other, cols, :192], 1, 1) + contract(gn[at, 256:448], w2[p.c, cols, :192], 1, 1)
            o = o.astype(BF)
            part[i, 0, :, cols] = o[:SLAB]
            part[i, 1, :, cols] = o[SLAB:]
        s.after_block(t)
    l_n1.wait()

    def in_grad(g, carry):
        v = contract(n1[:, rows_of(g, 512)], gn[...], 0, 0).astype(BF)
        for half in range(2):
            for dst, first in ((tq, 0), (rq.at[p.c], 256)):
                u = v[half * 256 : half * 256 + 256, first : first + 256]
                dst[g, half, :256] = u[:, :128]
                dst[g, half, 256:, :64] = u[:128, 128:192]
                dst[g, half, 256:, 64:] = u[128:, 128:192]
        return carry

    lax.fori_loop(0, 3, in_grad, 0)
    s.finish()
    lax.fori_loop(3, 4, in_grad, 0)
    swap_q = w.send(tq, rq.at[p.c], p.at(c=1))
    each(so, "s3")
    each(big, "s3")
    swap_q.wait_recv()
    each(sq, "s1")
    each(so, "s4")
    each(big, "s4")
    for cp in l_s:
        cp.wait()
    each(sq, "s2")
    s.wait()
    inv = norm_scale(lambda c: hid[:, c].astype(F32))
    total = None
    for c in COLS:
        g = s.total(c)
        scaled = hid[:, c].astype(F32) * inv
        gs = g * scaled
        gains[0, :, c] = jnp.sum(gs.reshape(SLAB // 8, 8, 128), axis=0)
        e = gs * gain[0:1, c]
        total = e if total is None else total + e
    inner = jnp.sum(total, axis=1, keepdims=True) * (1.0 / D)
    for c in COLS:
        e = s.total(c) * gain[0:1, c]
        v = grad_after[:, c] + inv * (e - hid[:, c].astype(F32) * inv * inner)
        outs[:, c] = v.astype(BF)
    gains[1] = gain_two[...]
    mine = pl.ds(pl.multiple_of(p.gy * 128, 128), 128)
    gcp = []
    for _, _, _, dev in rows:
        at = pl.ds(pl.multiple_of(dev[1] * 128, 128), 128)
        gcp.append(w.send(gains.at[:, :, at], gcame.at[p.gy], dev))
    glocal = w.copy(gains.at[:, :, mine], gcame.at[p.gy])
    each(sq, "s3")
    o = Scatter(w, outs, hid_cols, rows)
    o.s1()
    each(big, "s5")
    each(so, "s5")
    for cp in gcp:
        cp.wait_recv()
    glocal.wait()
    gsum[...] = jnp.sum(gcame[...], axis=0)
    lcp = [w.send(gsum, gcame2.at[p.gx], dev) for _, dev in lanes]
    llocal = w.copy(gsum, gcame2.at[p.gx])
    each(sq, "s4")
    for cp in lcp:
        cp.wait_recv()
    llocal.wait()
    o_gain[...] = jnp.sum(gcame2[...], axis=0)
    x.s2()
    o.s2()
    w.drain()
    each(sq, "s5")
    w.drain()


def call_third(*args):
    scratch = [
        pltpu.SemaphoreType.DMA((132,)), pltpu.SemaphoreType.DMA((112,)),
        pltpu.VMEM((T, D), BF), pltpu.VMEM((T, D), BF),
        pltpu.VMEM((2, D, 256), BF), pltpu.VMEM((256, D), BF),
        pltpu.VMEM((4, HEAD, T), BF), pltpu.VMEM((2, 256, T), BF), pltpu.VMEM((T, 512), BF),
        pltpu.VMEM((HEAD, T), F32), pltpu.VMEM((HEAD, T), F32), pltpu.VMEM((3 * QB, QB), F32),
        pltpu.VMEM((T, 1), jnp.int32), pltpu.VMEM((1, T), jnp.int32),
        pltpu.VMEM((4, 2, SLAB, D), BF),
        *LineSum.SCRATCH,
        pltpu.VMEM((SLAB, D), BF),
        pltpu.VMEM((2, 8, D), F32),
        pltpu.VMEM((16, 2, 8, 128), F32),
        pltpu.VMEM((2, 8, 128), F32),
        pltpu.VMEM((8, 2, 8, 128), F32),
        pltpu.VMEM((4, 2, 384, 128), BF),
        pltpu.VMEM((4, 2, 128, 256), BF),
        pltpu.VMEM((2, 4, 2, 384, 128), BF),
        pltpu.VMEM((2, 4, 2, 128, 256), BF),
        pltpu.VMEM((2, 4, 2, 256, 512), BF),
        pltpu.VMEM((SLAB, D), BF), pltpu.VMEM((SLAB, D), F32),
        pltpu.VMEM((8, D), F32), pltpu.VMEM((8, D), F32),
        pltpu.VMEM((4, HEAD, T), BF), pltpu.VMEM((HEAD, T), BF), pltpu.VMEM((HEAD, T), BF),
        pltpu.VMEM((4, HEAD, T), BF), pltpu.VMEM((8, T), F32),
        pltpu.VMEM((32, T), F32), pltpu.VMEM((32, T), F32),
    ]
    scratch += WeightSum.scratch(128, 512) * 2
    scratch += WeightSum.scratch(192, 128) * 2 + WeightSum.scratch(64, 256) * 2
    return pl.pallas_call(
        third_kernel,
        out_shape=[
            jax.ShapeDtypeStruct((2 * T, 128), BF),
            jax.ShapeDtypeStruct((2 * T, 128), BF),
            jax.ShapeDtypeStruct((2, 8, 128), F32),
            jax.ShapeDtypeStruct((384, 128), F32),
            jax.ShapeDtypeStruct((128, 256), F32),
            jax.ShapeDtypeStruct((256, 512), F32),
        ],
        in_specs=[ANY] * 17 + [VM],
        out_specs=[ANY, ANY, VM, VM, VM, VM],
        scratch_shapes=scratch,
        compiler_params=pltpu.CompilerParams(
            collective_id=2, has_side_effects=True, vmem_limit_bytes=62 << 20
        ),
        name="third",
    )(*args)


def outputs_kernel(
    a_cols, a_hid, a_gains, a_qkv, a_o, a_gate, a_up, a_down,
    x_cols, x_hid, x_gain, x_q, x_k, x_v, x_o, x_gain2, x_gate, x_up, x_down,
    sem, cols, hid, gains, qkv,
):
    first = [
        pltpu.make_async_copy(a, b, sem.at[i])
        for i, (a, b) in enumerate(
            ((a_cols, cols), (a_hid, hid), (a_gains, gains), (a_qkv, qkv), (a_o, x_o), (a_gate, x_gate), (a_up, x_up), (a_down, x_down))
        )
    ]
    for cp in first:
        cp.start()
    first[0].wait()
    x_cols[...] = cols[...].astype(F32)
    first[1].wait()
    x_hid[...] = hid[...].astype(F32)
    first[2].wait()
    x_gain[...] = jnp.sum(gains[0], axis=0, keepdims=True)
    x_gain2[...] = jnp.sum(gains[1], axis=0, keepdims=True)
    first[3].wait()
    x_q[...] = qkv[:256]
    kv = qkv[256:].T
    x_k[:, :128] = kv[:32]
    x_k[:, 128:] = kv[64:96]
    x_v[:, :128] = kv[32:64]
    x_v[:, 128:] = kv[96:]
    for cp in first[4:]:
        cp.wait()


def call_outputs(*args):
    shapes = [
        (2 * T, 128), (2 * T, 128), (1, 128), (256, 128), (32, 256), (32, 256), (128, 256), (1, 128),
        (256, 512), (256, 512), (512, 256),
    ]
    return pl.pallas_call(
        outputs_kernel,
        out_shape=[jax.ShapeDtypeStruct(v, F32) for v in shapes],
        in_specs=[ANY] * 8,
        out_specs=[VM] * 11,
        scratch_shapes=[
            pltpu.SemaphoreType.DMA((8,)),
            pltpu.VMEM((2 * T, 128), BF), pltpu.VMEM((2 * T, 128), BF),
            pltpu.VMEM((2, 8, 128), F32), pltpu.VMEM((384, 128), F32),
        ],
        compiler_params=pltpu.CompilerParams(vmem_limit_bytes=62 << 20),
        name="outputs",
    )(*args)


def per_device(
    hidden, attn_gain, wq, wk, wv, wo, ffn_gain, gate, up, down, segments, cotangent,
):
    freq = (ROPE_BASE ** (-np.arange(0, HEAD, 2, dtype=np.float32) / HEAD)).astype(np.float32)[:, None]
    (
        cot, gg, uu, dd, w2, o2, n1, hid_slab, qt, kt, vt, ht, lse, after, n2, act, gain, cos, sin
    ) = call_first(
        hidden, cotangent, gate, up, down, wo, wq, wk.T, wv.T, attn_gain[None], ffn_gain[None], segments, freq
    )
    grad_attn, grad_after, gain_two, outs, o_down, o_gate, g_up = call_second(
        n2.reshape(T, D), cot, gg.reshape(2, D, 512), uu.reshape(2, D, 512),
        dd.reshape(2, 8, 512, 256), after, gain, act,
    )
    out_cols, hid_cols, o_gain, o_qkv, o_o, o_up = call_third(
        grad_attn.reshape(T, D), hid_slab, grad_after, gain, gain_two, w2, o2, n1,
        qt, kt, vt, ht, lse, cos, sin, g_up.reshape(2, 4, 2, 256, 512), outs, segments,
    )
    res = call_outputs(out_cols, hid_cols, o_gain, o_qkv, o_o, o_gate, o_up, o_down)
    return (
        res[0], res[1], res[2].reshape(128), res[3], res[4].T, res[5].T, res[6], res[7].reshape(128), *res[8:],
    )


def solution(mesh):
    wide, cols, tall = P("gx", "gy"), P("gy"), P("gy", "gx")
    return jax.shard_map(
        per_device,
        mesh=mesh,
        in_specs=(wide, cols, wide, wide, wide, tall, cols, wide, wide, tall, P("gx", None), wide),
        out_specs=(wide, wide, cols, wide, wide, wide, tall, cols, wide, wide, tall),
        check_vma=False,
    )
```

```python
import functools

import jax
import jax.numpy as jnp
import numpy as np
from jax import lax
from jax.experimental import pallas as pl
from jax.experimental.pallas import tpu as pltpu
from jax.sharding import PartitionSpec as P

HEAD = 64
EPS = 1e-06
ROPE_BASE = 10000000.0
ATTN_SCALE = 1.0 / 64.0
RES = 0.22
T = 1024
D = 2048
SLAB = 128
QB = 256
BF = jnp.bfloat16
F32 = jnp.float32
MESH = pl.DeviceIdType.MESH
ANY = pl.BlockSpec(memory_space=pl.ANY)
VM = pl.BlockSpec(memory_space=pltpu.VMEM)


class Place:
    def __init__(self):
        gx = lax.axis_index("gx")
        gy = lax.axis_index("gy")
        self.gx, self.gy = gx, gy
        self.x, self.yl = gx // 2, lax.rem(gx, 2)
        self.yh, self.z, self.c = gy // 8, lax.rem(gy // 2, 4), lax.rem(gy, 2)
        self.y = self.yh * 2 + self.yl
        self.r = self.z * 2 + self.c

    def at(self, x=0, y=0, z=0, c=0):
        xx = lax.rem(self.x + x + 4, 4)
        yy = lax.rem(self.y + y + 4, 4)
        zz = lax.rem(self.z + z + 4, 4)
        cc = lax.rem(self.c + c, 2)
        return (xx * 2 + lax.rem(yy, 2), (yy // 2) * 8 + zz * 2 + cc)

    def step(self, axis, k):
        return self.at(**{axis: k})

    def pos(self, axis, k):
        return lax.rem(getattr(self, axis) + k + 4, 4)


class Wire:
    def __init__(self, place, send, recv):
        self.place, self.send_sem, self.recv_sem = place, send, recv
        self.starts, self.lands = 0, 0
        self.sent = []

    def send(self, src, dst, to):
        i, j = self.starts, self.lands
        self.starts, self.lands = i + 1, j + 1
        cp = pltpu.make_async_remote_copy(
            src_ref=src,
            dst_ref=dst,
            send_sem=self.send_sem.at[i],
            recv_sem=self.recv_sem.at[j],
            device_id=to,
            device_id_type=MESH,
        )
        cp.start()
        self.sent.append(cp)
        return cp

    def copy(self, src, dst):
        i = self.starts
        self.starts += 1
        cp = pltpu.make_async_copy(src, dst, self.send_sem.at[i])
        cp.start()
        return cp

    def drain(self):
        for cp in self.sent:
            cp.wait_send()
        self.sent = []


def say_hello(peers):
    for peer in peers:
        pl.semaphore_signal(pltpu.get_barrier_semaphore(), inc=1, device_id=peer, device_id_type=MESH)


def hear_all(peers):
    pl.semaphore_wait(pltpu.get_barrier_semaphore(), len(peers))


def ring_peers(p):
    return [p.at(x=1), p.at(x=-1), p.at(y=1), p.at(y=-1)]


def row_peers(p):
    out = []
    for y in (0, 2):
        for z in range(4):
            for c in range(2):
                if (y, z, c) != (0, 0, 0):
                    out.append((y, z, c, p.at(y=y, z=z, c=c)))
    return out


def line_peers(p):
    return [p.at(c=1), p.at(z=1), p.at(z=-1)]


class WeightGather:
    def __init__(self, wire, src, dst, start, rows, order, stage=None):
        self.w, self.src, self.dst, self.stage = wire, src, dst, stage
        self.r0, self.n, self.order = start, rows, order
        self.a1, self.a2 = ("x", "y") if order == 0 else ("y", "x")

    def one(self, k, half=None):
        p = self.w.place
        x, y = (p.pos("x", k), p.y) if self.a1 == "x" else (p.x, p.pos("y", k))
        return self.dst.at[y // 2, x, lax.rem(y, 2), self.span(half)]

    def four(self, k, half=None):
        p = self.w.place
        if self.a2 == "y":
            y = p.pos("y", k)
            return self.dst.at[y // 2, :, lax.rem(y, 2), self.span(half)]
        return self.dst.at[:, p.pos("x", k), :, self.span(half)]

    def span(self, half):
        if half is None:
            return pl.ds(self.r0, self.n)
        return pl.ds(self.r0 + half * (self.n // 2), self.n // 2)

    def s1(self):
        w, p = self.w, self.w.place
        own = self.src.at[pl.ds(self.r0, self.n)]
        if self.stage is None:
            self.local = w.copy(own, self.one(0))
        else:
            self.local = w.copy(own, self.stage.at[pl.ds(self.r0, self.n)])
        self.up = w.send(own, self.one(0), p.step(self.a1, 1))
        self.down = w.send(own, self.one(0), p.step(self.a1, -1))

    def s2(self):
        w, p = self.w, self.w.place
        if self.stage is not None:
            self.local.wait()
            self.local = w.copy(self.stage.at[pl.ds(self.r0, self.n)], self.one(0))
        self.up.wait_recv()
        self.up2 = w.send(self.one(-1, 0), self.one(-1, 0), p.step(self.a1, 1))
        self.down.wait_recv()
        self.down2 = w.send(self.one(1, 1), self.one(1, 1), p.step(self.a1, -1))

    def s3(self):
        w, p = self.w, self.w.place
        self.local.wait()
        self.up2.wait_recv()
        self.down2.wait_recv()
        self.up3 = w.send(self.four(0), self.four(0), p.step(self.a2, 1))
        self.down3 = w.send(self.four(0), self.four(0), p.step(self.a2, -1))

    def s4(self):
        w, p = self.w, self.w.place
        self.up3.wait_recv()
        self.up4 = w.send(self.four(-1, 0), self.four(-1, 0), p.step(self.a2, 1))
        self.down3.wait_recv()
        self.down4 = w.send(self.four(1, 1), self.four(1, 1), p.step(self.a2, -1))

    def s5(self):
        self.up4.wait_recv()
        self.down4.wait_recv()


class RowGather:
    def __init__(self, wire, src, dst, stage=None):
        self.w, self.src, self.dst, self.stage = wire, src, dst, stage

    def block(self, yh, k, c=None):
        p = self.w.place
        c = p.c if c is None else c
        gy = yh * 8 + p.pos("z", k) * 2 + c
        return self.dst.at[:, pl.ds(pl.multiple_of(gy * 128, 128), 128)]

    def out(self, src, yh, k):
        b = self.block(yh, k)
        self.cores.append(self.w.send(src, b, self.w.place.at(c=1)))

    def s0(self):
        w, p = self.w, self.w.place
        self.cores = []
        mine = self.src.at[pl.ds(pl.multiple_of(p.yh * T, T), T)]
        other = self.src.at[pl.ds(pl.multiple_of((1 - p.yh) * T, T), T)]
        own = self.block(p.yh, 0)
        self.local = w.copy(mine, own if self.stage is None else self.stage)
        self.swap = w.send(other, own, p.at(y=2))

    def s1(self):
        w, p = self.w, self.w.place
        mine = self.src.at[pl.ds(pl.multiple_of(p.yh * T, T), T)]
        own = self.block(p.yh, 0)
        self.up0 = w.send(mine, own, p.at(z=1))
        self.down0 = w.send(mine, own, p.at(z=-1))
        self.out(mine, p.yh, 0)

    def s2(self):
        w, p = self.w, self.w.place
        if self.stage is not None:
            self.local.wait()
            self.local = w.copy(self.stage, self.block(p.yh, 0))
        self.swap.wait_recv()
        b = self.block(1 - p.yh, 0)
        self.up1 = w.send(b, b, p.at(z=1))
        self.down1 = w.send(b, b, p.at(z=-1))
        self.out(b, 1 - p.yh, 0)

    def s3(self):
        w, p = self.w, self.w.place
        self.up0.wait_recv()
        b = self.block(p.yh, -1)
        self.up2 = w.send(b, b, p.at(z=1))
        self.out(b, p.yh, -1)
        self.down0.wait_recv()
        self.out(self.block(p.yh, 1), p.yh, 1)
        self.down1.wait_recv()
        b = self.block(1 - p.yh, 1)
        self.down2 = w.send(b, b, p.at(z=-1))
        self.out(b, 1 - p.yh, 1)
        self.up1.wait_recv()
        self.out(self.block(1 - p.yh, -1), 1 - p.yh, -1)

    def s4(self):
        p = self.w.place
        self.up2.wait_recv()
        self.out(self.block(p.yh, 2), p.yh, 2)
        self.down2.wait_recv()
        self.out(self.block(1 - p.yh, 2), 1 - p.yh, 2)

    def s5(self):
        self.local.wait()
        for cp in self.cores:
            cp.wait_recv()


def add_rows(dst, srcs, rows):
    step = max(16, min(rows, 32768 // dst.shape[-1]))
    while rows % step:
        step //= 2

    def body(i, carry):
        at = pl.ds(pl.multiple_of(i * step, step), step)
        total = srcs[0][at].astype(F32)
        for v in srcs[1:]:
            total = total + v[at].astype(F32)
        dst[at] = total.astype(dst.dtype)
        return carry

    lax.fori_loop(0, rows // step, body, 0)


class LineSum:
    SCRATCH = [
        pltpu.VMEM((4, SLAB, D), BF),
        pltpu.VMEM((2, SLAB // 2, D), BF),
        pltpu.VMEM((2, SLAB, D), BF),
    ]
    ORDER = (2, 1, -1, 0)

    def __init__(self, wire, part, got, far, near):
        self.w, self.part, self.got = wire, part, got
        self.far, self.near = far, near
        self.core = {}
        self.last = []

    def mine(self, k, half=None):
        p = self.w.place
        if half is None:
            return self.part.at[p.pos("z", k), p.c]
        return self.part.at[p.pos("z", k), p.c, pl.ds(half * (SLAB // 2), SLAB // 2)]

    def push(self, k):
        w, p = self.w, self.w.place
        z = p.pos("z", k)
        self.core[k] = w.send(self.part.at[z, 1 - p.c], self.got.at[z], p.at(c=1))

    def merge(self, k):
        z = self.w.place.pos("z", k)
        self.core[k].wait_recv()
        add_rows(self.mine(k), [self.mine(k), self.got.at[z]], SLAB)

    def send_far(self):
        w, p = self.w, self.w.place
        self.up = w.send(self.mine(2, 0), self.far.at[0], p.at(z=1))
        self.down = w.send(self.mine(2, 1), self.far.at[1], p.at(z=-1))

    def near_first(self, i):
        self.near_half(1 if i == 0 else -1, i, 1 - i)

    def near_second(self, i):
        k, far = (1, self.up) if i == 0 else (-1, self.down)
        far.wait_recv()
        add_rows(self.mine(k, i), [self.mine(k, i), self.far.at[i]], SLAB // 2)
        self.near_half(k, i, i)

    def near_half(self, k, i, h):
        at = pl.ds(h * (SLAB // 2), SLAB // 2)
        self.last.append(self.w.send(self.mine(k, h), self.near.at[i, at], self.w.place.at(z=k)))

    def after_block(self, t):
        self.push(self.ORDER[t])
        if t == 1:
            self.merge(2)
            self.send_far()
        if t == 2:
            self.merge(1)
            self.near_first(0)
        if t == 3:
            self.merge(-1)
            self.near_first(1)
            self.merge(0)

    def finish(self):
        self.near_second(0)
        self.near_second(1)

    def wait(self):
        for cp in self.last:
            cp.wait_recv()

    def total(self, at):
        p = self.w.place
        return (
            self.part[p.z, p.c, :, at].astype(F32)
            + self.near[0, :, at].astype(F32)
            + self.near[1, :, at].astype(F32)
        )


class LineGather:
    def __init__(self, wire, src, dst):
        self.w, self.src, self.dst = wire, src, dst

    def slot(self, k, half=None):
        p = self.w.place
        if half is None:
            return self.dst.at[p.pos("z", k), p.c]
        return self.dst.at[p.pos("z", k), p.c, pl.ds(half * (SLAB // 2), SLAB // 2)]

    def s1(self):
        w, p = self.w, self.w.place
        self.up = w.send(self.src, self.slot(0), p.at(z=1))
        self.down = w.send(self.src, self.slot(0), p.at(z=-1))
        self.cores = [w.send(self.src, self.slot(0), p.at(c=1))]
        self.local = w.copy(self.src, self.slot(0))

    def s2(self):
        w, p = self.w, self.w.place
        self.up.wait_recv()
        self.up2 = w.send(self.slot(-1, 0), self.slot(-1, 0), p.at(z=1))
        self.cores.append(w.send(self.slot(-1), self.slot(-1), p.at(c=1)))
        self.down.wait_recv()
        self.down2 = w.send(self.slot(1, 1), self.slot(1, 1), p.at(z=-1))
        self.cores.append(w.send(self.slot(1), self.slot(1), p.at(c=1)))

    def s3(self):
        w, p = self.w, self.w.place
        self.up2.wait_recv()
        self.cores.append(w.send(self.slot(2, 0), self.slot(2, 0), p.at(c=1)))
        self.down2.wait_recv()
        self.cores.append(w.send(self.slot(2, 1), self.slot(2, 1), p.at(c=1)))

    def s4(self):
        self.local.wait()
        for cp in self.cores:
            cp.wait_recv()


class Scatter:
    def __init__(self, wire, src, dst, rows):
        self.w, self.src, self.dst, self.rows = wire, src, dst, rows

    def s1(self):
        w, p = self.w, self.w.place
        mine = self.dst.at[pl.ds(pl.multiple_of(p.yh * T + p.r * SLAB, SLAB), SLAB)]
        self.copies = []
        for y, z, c, dev in self.rows:
            at = pl.ds(pl.multiple_of(dev[1] * 128, 128), 128)
            self.copies.append(w.send(self.src.at[:, at], mine, dev))
        at = pl.ds(pl.multiple_of(p.gy * 128, 128), 128)
        self.local = w.copy(self.src.at[:, at], mine)

    def s2(self):
        self.local.wait()
        for cp in self.copies:
            cp.wait_recv()


def each_rows(rows, step, f):
    def body(i, carry):
        f(pl.ds(pl.multiple_of(i * step, step), step))
        return carry

    lax.fori_loop(0, rows // step, body, 0)


COLS = [slice(j * 128, (j + 1) * 128) for j in range(16)]


def contract(a, b, da, db):
    return lax.dot_general(a, b, (((da,), (db,)), ((), ())), preferred_element_type=F32)


def rows_of(i, n):
    return pl.ds(pl.multiple_of(i * n, n), n)


def row_mean(parts):
    total = parts[0]
    for v in parts[1:]:
        total = total + v
    return jnp.sum(total, axis=1, keepdims=True) * (1.0 / D)


def norm_scale(load):
    squares = []
    total = None
    for at in COLS:
        v = load(at)
        total = v * v if total is None else total + v * v
    return lax.rsqrt(jnp.sum(total, axis=1, keepdims=True) * (1.0 / D) + EPS)


def unpack(packed, wide, out_rows, j):
    for g in range(8):
        src = packed.at[g // 2, g % 2]
        wide[g * 256 : (g + 1) * 256, :128] = src[:256]
        kv = src[256:384]
        wide[g * 256 : g * 256 + 128, 128:192] = kv[:, :64]
        wide[g * 256 + 128 : (g + 1) * 256, 128:192] = kv[:, 64:]
        out_rows[rows_of(j, 128), g * 256 : g * 256 + 128] = src[384:512]
        out_rows[rows_of(j, 128), g * 256 + 128 : (g + 1) * 256] = src[512:]


def key_window(i):
    return pl.multiple_of(jnp.maximum(i - 2, 0) * QB, QB)


def pick_segment(p, segs, seg_row, seg_col):
    row = jnp.where(p.yh == 0, segs[0:1], segs[1:2])
    seg_row[...] = row
    wide = jnp.broadcast_to(row.astype(F32), (128, T)).T
    seg_col[...] = wide[:, 0:1].astype(jnp.int32)


def bias_tile(seg_col, seg_row, lo, n, i):
    first = i * QB
    same = seg_col[pl.ds(lo, n)] == seg_row[:, pl.ds(first, QB)]
    rows = lo + lax.broadcasted_iota(jnp.int32, (n, QB), 0)
    cols = first + lax.broadcasted_iota(jnp.int32, (n, QB), 1)
    return jnp.where(same & (rows <= cols), 0.0, -1e30)


def first_kernel(
    hidden, cot, gate, up, down, wo, wq, wkt, wvt, gain_a, gain_b, segs, freq,
    c_out, g_out, u_out, d_out, w2_out, o2_out, n1_out, slab_out, qt_out, kt_out, vt_out, ht_out,
    lse_out, after_out, n2_out, act_out, gain_out, cos_out, sin_out,
    send, recv, h, n1, q_tmp, q_got, w2, o2, qt, kt, vt, ht, part, got, far, near,
    after, normed, gain, seg_col, seg_row, cos, sin, bias, lse, v_cot, v_gate, v_up, v_down,
    dw, cv, act, v_q, gains,
):
    p = Place()
    w = Wire(p, send, recv)
    rows = row_peers(p)
    peers = ring_peers(p) + [dev for _, _, _, dev in rows]
    say_hello(peers)
    v_q[:256] = wq[...]
    kv = [wkt[:, :128], wvt[:, :128], wkt[:, 128:], wvt[:, 128:]]
    v_q[256:384] = jnp.concatenate(kv, axis=0).astype(F32).T.astype(BF)
    v_q[384:512] = wo[:, :128]
    v_q[512:] = wo[:, 128:]
    gains[...] = jnp.zeros_like(gains)
    gains[0:1] = gain_a[...]
    gains[1:2] = gain_b[...]
    pick_segment(p, segs, seg_row, seg_col)
    earlier = jnp.zeros((8, T), F32)
    for b in range(8):
        less = seg_col[b * 128 : (b + 1) * 128] < seg_row[...]
        earlier = earlier + jnp.sum(jnp.where(less, 1.0, 0.0).reshape(16, 8, T), axis=0)
    starts = jnp.sum(earlier, axis=0, keepdims=True)
    places = lax.broadcasted_iota(jnp.int32, (1, T), 1).astype(F32) - starts
    turned = freq[...] * places
    cos[...] = jnp.cos(turned)
    sin[...] = jnp.sin(turned)

    hear_all(peers)
    hg = RowGather(w, hidden, h)
    cg = RowGather(w, cot, c_out, v_cot)
    aq = [WeightGather(w, v_q, q_tmp, 320 * i, 320, i) for i in range(2)]
    gu = [WeightGather(w, gate, g_out, 0, 256, 0, v_gate), WeightGather(w, up, u_out, 0, 256, 1, v_up)]
    dn = [WeightGather(w, down, d_out, 256 * i, 256, i, v_down) for i in range(2)]

    def each(group, stage):
        for b in group:
            getattr(b, stage)()

    each(aq, "s1")
    hg.s0()
    hg.s1()
    own = pl.ds(pl.multiple_of(p.gy * 128, 128), 128)
    glocal = w.copy(gains, gain.at[:, own])
    gcopies = [w.send(gains, gain.at[:, own], dev) for _, _, _, dev in rows]

    each(aq, "s2")
    each(aq, "s3")
    hg.s2()
    each(dn, "s1")
    cg.s0()
    each(aq, "s4")
    hg.s3()
    each(dn, "s2")
    each(gu, "s1")
    each(aq, "s5")
    q_swap = w.send(q_tmp.at[1 - p.c], q_got, p.at(c=1))
    unpack(q_tmp.at[p.c], w2.at[p.c], o2, p.c)
    hg.s4()
    cg.s1()
    q_swap.wait_recv()
    unpack(q_got, w2.at[1 - p.c], o2, 1 - p.c)
    hg.s5()
    cg.s2()
    each(dn, "s3")
    glocal.wait()
    for cp in gcopies:
        cp.wait_recv()

    def project(i, carry):
        at = rows_of(i, QB)
        inv = norm_scale(lambda c: h[at, c].astype(F32))
        for c in COLS:
            n1[at, c] = (h[at, c].astype(F32) * inv * gain[0:1, c]).astype(BF)
        ct, st = cos[:, at], sin[:, at]
        keys = []
        for j in range(2):
            lin = contract(n1[at], w2[j, :, :192], 1, 0)
            qj = lin[:, :128].T
            kv = lin[:, 128:].T
            for hh in range(2):
                a, b = qj[hh * 64 : hh * 64 + 32], qj[hh * 64 + 32 : hh * 64 + 64]
                qt[2 * j + hh, 0:32, at] = (a * ct - b * st).astype(BF) * ATTN_SCALE
                qt[2 * j + hh, 32:64, at] = (b * ct + a * st).astype(BF) * ATTN_SCALE
            keys.append(kv[:32])
            vt[j * 32 : (j + 1) * 32, at] = kv[32:].astype(BF)
        a, b = keys
        kt[0:32, at] = (a * ct - b * st).astype(BF)
        kt[32:64, at] = (b * ct + a * st).astype(BF)
        return carry

    lax.fori_loop(0, 4, project, 0)
    exports = [
        w.copy(w2, w2_out), w.copy(o2, o2_out),
        w.copy(n1, n1_out),
        w.copy(h.at[pl.ds(pl.multiple_of(p.r * SLAB, SLAB), SLAB)], slab_out),
        w.copy(qt, qt_out), w.copy(kt, kt_out), w.copy(vt, vt_out),
    ]
    each(gu, "s2")
    gain_out[...] = gain[...]
    cos_out[...] = cos[...]
    sin_out[...] = sin[...]
    s = LineSum(w, part, got, far, near)

    def attend(t):
        i = p.pos("z", LineSum.ORDER[t])
        lo = key_window(i)
        at = rows_of(i, QB)
        keys = pl.ds(lo, 3 * QB)
        bias[...] = bias_tile(seg_col, seg_row, lo, 3 * QB, pl.multiple_of(i, 1))

        def head(n, carry):
            sc = contract(kt[:, keys], qt[n, :, at], 0, 0) + bias[...]
            top = jnp.max(sc, axis=0, keepdims=True)
            e = jnp.exp(sc - top)
            total = jnp.sum(e, axis=0, keepdims=True)
            o = contract(vt[:, keys], e.astype(BF), 1, 0) * (1.0 / total)
            ht[n, :, at] = o.astype(BF)
            lse[pl.ds(n, 1), at] = top + jnp.log(total)
            return carry

        lax.fori_loop(0, 4, head, 0)

    def out_project(t):
        i = p.pos("z", LineSum.ORDER[t])
        block = ht[:, :, rows_of(i, QB)].reshape(256, QB)
        for b in range(4):
            cols = slice(b * 512, (b + 1) * 512)
            o = contract(block, o2[:, cols], 0, 0).astype(BF)
            part[i, 0, :, cols] = o[:SLAB]
            part[i, 1, :, cols] = o[SLAB:]
        s.after_block(t)

    attend(0)
    out_project(0)
    attend(1)
    out_project(1)
    cg.s3()
    attend(2)
    out_project(2)
    each(dn, "s4")
    each(gu, "s3")
    attend(3)
    out_project(3)
    exports += [w.copy(ht, ht_out), w.copy(lse, lse_out)]
    s.finish()
    cg.s4()
    s.wait()
    slab = pl.ds(pl.multiple_of(p.r * SLAB, SLAB), SLAB)
    for c in COLS:
        after[:, c] = h[slab, c].astype(F32) + RES * s.total(c)
    inv = norm_scale(lambda c: after[:, c])
    for c in COLS:
        normed[:, c] = (after[:, c] * inv * gain[1:2, c]).astype(BF)
    g = LineGather(w, normed, n2_out)
    g.s1()
    exports.append(w.copy(after, after_out))
    each(dn, "s5")
    loads = [
        w.copy(d_out.at[j, g // 2, g % 2], dw.at[j, :, pl.ds(g * 256, 256)]) for j in range(2) for g in range(8)
    ]
    cg.s5()
    loads.append(w.copy(c_out, cv))
    for cp in loads:
        cp.wait()

    def act_grad(i, carry):
        at = rows_of(i, 512)
        for j in range(2):
            act[j, at] = (RES * contract(cv[at], dw[j], 1, 1)).astype(BF)
        return carry

    lax.fori_loop(0, 2, act_grad, 0)
    exports.append(w.copy(act, act_out))
    each(gu, "s4")
    g.s2()
    g.s3()
    w.drain()
    each(gu, "s5")
    g.s4()
    for cp in exports:
        cp.wait()
    w.drain()


def call_first(*args):
    shapes = [
        ((T, D), BF),
        ((2, 4, 2, 256, 512), BF), ((2, 4, 2, 256, 512), BF), ((2, 4, 2, 512, 256), BF),
        ((2, D, 256), BF), ((256, D), BF),
        ((T, D), BF), ((SLAB, D), BF),
        ((4, HEAD, T), BF), ((HEAD, T), BF), ((HEAD, T), BF), ((4, HEAD, T), BF),
        ((8, T), F32), ((SLAB, D), F32), ((4, 2, SLAB, D), BF), ((2, T, 512), BF),
        ((8, D), F32), ((32, T), F32), ((32, T), F32),
    ]
    out_specs = [ANY] * 16 + [VM] * 3
    scratch = [
        pltpu.SemaphoreType.DMA((156,)), pltpu.SemaphoreType.DMA((113,)),
        pltpu.VMEM((T, D), BF), pltpu.VMEM((T, D), BF),
        pltpu.VMEM((2, 4, 2, 640, 128), BF), pltpu.VMEM((4, 2, 640, 128), BF),
        pltpu.VMEM((2, D, 256), BF), pltpu.VMEM((256, D), BF),
        pltpu.VMEM((4, HEAD, T), BF), pltpu.VMEM((HEAD, T), BF), pltpu.VMEM((HEAD, T), BF),
        pltpu.VMEM((4, HEAD, T), BF), pltpu.VMEM((4, 2, SLAB, D), BF),
        *LineSum.SCRATCH,
        pltpu.VMEM((SLAB, D), F32), pltpu.VMEM((SLAB, D), BF),
        pltpu.VMEM((8, D), F32), pltpu.VMEM((T, 1), jnp.int32), pltpu.VMEM((1, T), jnp.int32),
        pltpu.VMEM((32, T), F32), pltpu.VMEM((32, T), F32), pltpu.VMEM((3 * QB, QB), F32),
        pltpu.VMEM((8, T), F32),
        pltpu.VMEM((T, 128), BF), pltpu.VMEM((256, 512), BF), pltpu.VMEM((256, 512), BF),
        pltpu.VMEM((512, 256), BF),
        pltpu.VMEM((2, 512, D), BF), pltpu.VMEM((T, D), BF), pltpu.VMEM((2, T, 512), BF),
        pltpu.VMEM((640, 128), BF), pltpu.VMEM((8, 128), F32),
    ]
    return pl.pallas_call(
        first_kernel,
        out_shape=[jax.ShapeDtypeStruct(s, d) for s, d in shapes],
        in_specs=[ANY] * 5 + [VM] * 8,
        out_specs=out_specs,
        scratch_shapes=scratch,
        compiler_params=pltpu.CompilerParams(
            collective_id=0, has_side_effects=True, vmem_limit_bytes=62 << 20
        ),
        name="first",
    )(*args)


class WeightSum:
    @staticmethod
    def scratch(rows, cols):
        h = rows // 2
        return [
            pltpu.VMEM((2, 4, h, cols), BF),
            pltpu.VMEM((2, 4, rows, cols), BF),
            pltpu.VMEM((2, h, cols), BF),
            pltpu.VMEM((2, rows, cols), BF),
        ]

    def __init__(self, wire, part, out, start, rows, order, far, came, far2, came2):
        self.w, self.part, self.out = wire, part, out
        self.r0, self.n = start, rows
        self.a1, self.a2 = ("y", "x") if order == 0 else ("x", "y")
        self.far, self.came, self.far2, self.came2 = far, came, far2, came2

    def span(self, half):
        if half is None:
            return pl.ds(self.r0, self.n)
        return pl.ds(self.r0 + half * (self.n // 2), self.n // 2)

    def src(self, k, j, half=None):
        p = self.w.place
        if self.a1 == "y":
            y = p.pos("y", k)
            return self.part.at[y // 2, j, lax.rem(y, 2), self.span(half)]
        return self.part.at[j // 2, p.pos("x", k), lax.rem(j, 2), self.span(half)]

    def four(self, k, half=None, part=None):
        p = self.w.place
        part = self.part if part is None else part
        if self.a1 == "y":
            y = p.pos("y", k)
            return part.at[y // 2, :, lax.rem(y, 2), self.span(half)]
        return part.at[:, p.pos("x", k), :, self.span(half)]

    def land(self, ref, i):
        if self.a1 == "y":
            return ref.at[i]
        return ref.reshape(2, 2, 2, *ref.shape[2:]).at[i]

    def s1(self, part=None):
        w, p = self.w, self.w.place
        self.up = w.send(self.four(2, 0, part), self.land(self.far, 0), p.step(self.a1, 1))
        self.down = w.send(self.four(2, 1, part), self.land(self.far, 1), p.step(self.a1, -1))

    def s2(self):
        w, p = self.w, self.w.place
        h = self.n // 2
        self.up.wait_recv()
        for j in range(4):
            a = self.src(1, j, 0)
            add_rows(a, [a, self.far.at[0, j]], h)
        self.up2 = w.send(self.four(1), self.land(self.came, 0), p.step(self.a1, 1))
        self.down.wait_recv()
        for j in range(4):
            a = self.src(-1, j, 1)
            add_rows(a, [a, self.far.at[1, j]], h)
        self.down2 = w.send(self.four(-1), self.land(self.came, 1), p.step(self.a1, -1))

    def s3(self):
        w, p = self.w, self.w.place
        self.up2.wait_recv()
        self.down2.wait_recv()
        for k in (2, 1, -1, 0):
            j = p.pos(self.a2, k)
            a = self.src(0, j)
            add_rows(a, [a, self.came.at[0, j], self.came.at[1, j]], self.n)
            if k == 2:
                self.up3 = w.send(self.src(0, j, 0), self.far2.at[0], p.step(self.a2, 1))
                self.down3 = w.send(self.src(0, j, 1), self.far2.at[1], p.step(self.a2, -1))

    def s4(self):
        w, p = self.w, self.w.place
        h = self.n // 2
        self.up3.wait_recv()
        j = p.pos(self.a2, 1)
        a = self.src(0, j, 0)
        add_rows(a, [a, self.far2.at[0]], h)
        self.up4 = w.send(self.src(0, j), self.came2.at[0], p.step(self.a2, 1))
        self.down3.wait_recv()
        j = p.pos(self.a2, -1)
        a = self.src(0, j, 1)
        add_rows(a, [a, self.far2.at[1]], h)
        self.down4 = w.send(self.src(0, j), self.came2.at[1], p.step(self.a2, -1))

    def s5(self):
        self.up4.wait_recv()
        self.down4.wait_recv()
        j = self.w.place.pos(self.a2, 0)
        add_rows(
            self.out.at[pl.ds(self.r0, self.n)],
            [self.src(0, j), self.came2.at[0], self.came2.at[1]],
            self.n,
        )


def second_kernel(
    n2_in, cot_in, g_in, u_in, d_in, after_in, gain_in, act_in,
    attn_out, grad_after_out, gain_part, outs_out, o_down, o_gate, gu_out,
    send, recv, n2, pg, gw, uw, dw, ggp, ha, gup, gd, pf, attn, outs, after, gain, slab, v_down, v_gate, *sc,
):
    p = Place()
    w = Wire(p, send, recv)
    peers = ring_peers(p)
    say_hello(peers + line_peers(p))
    cot = pg.reshape(T, D)
    loads = []
    for j in range(2):
        part = [w.copy(g_in.at[j], gw.at[j]), w.copy(u_in.at[j], uw.at[j]), w.copy(act_in.at[j], ggp.at[j])]
        part += [w.copy(n2_in, n2)] if j == 0 else []
        loads.append(part)
    l_d = [w.copy(d_in.at[j, g], dw.at[j, :, pl.ds(g * 256, 256)]) for j in range(2) for g in range(8)]
    l_c = w.copy(cot_in, cot)
    l_s = [
        w.copy(after_in, after), w.copy(gain_in, gain),
    ]
    hear_all(peers + line_peers(p))
    f = LineSum(w, pf, *sc[0:3])
    s = LineSum(w, pg, *sc[3:6])
    down = [WeightSum(w, gd, v_down, 256 * i, 256, i, *sc[6 + 4 * i : 10 + 4 * i]) for i in range(2)]
    gparts = gw.reshape(2, 4, 2, 256, 512)
    gates = [WeightSum(w, gparts, v_gate, 128 * i, 128, i, *sc[14 + 4 * i : 18 + 4 * i]) for i in range(2)]

    def each(group, stage):
        for b in group:
            getattr(b, stage)()

    for t, k in enumerate(LineSum.ORDER):
        i = p.pos("z", k)
        at = rows_of(i, QB)

        def units(j, carry):
            gate = contract(n2[at], gw[j], 1, 0)
            upp = contract(n2[at], uw[j], 1, 0)
            ga = ggp[j, at].astype(F32)
            sig = 1.0 / (1.0 + jnp.exp(-gate))
            silu = gate * sig
            ha[j, at] = (silu * upp).astype(BF)
            ggp[j, at] = (ga * upp * sig * (1.0 + gate * (1.0 - sig))).astype(BF)
            gup[j, at] = (ga * silu).astype(BF)
            return carry

        if t == 0:
            for j in range(2):
                for cp in loads[j]:
                    cp.wait()
                units(j, 0)
            for cp in l_d:
                cp.wait()
        else:
            lax.fori_loop(0, 2, units, 0)
        for b in range(4):
            cols = slice(b * 512, (b + 1) * 512)
            o = (contract(ha[0, at], dw[0, :, cols], 1, 0) + contract(ha[1, at], dw[1, :, cols], 1, 0)).astype(BF)
            pf[i, 0, :, cols] = o[:SLAB]
            pf[i, 1, :, cols] = o[SLAB:]
        f.after_block(t)

    def down_grad(g, carry):
        at = rows_of(g, 512)
        for j in range(2):
            v = (RES * contract(ha[j], cot[:, at], 0, 0)).astype(BF)
            gd[j, g, 0] = v[:, :256]
            gd[j, g, 1] = v[:, 256:]
        return carry

    l_c.wait()
    lax.fori_loop(0, 4, down_grad, 0)
    slab[...] = cot[rows_of(p.r, SLAB)]
    f.finish()
    each(down, "s1")
    for t, k in enumerate(LineSum.ORDER):
        i = p.pos("z", k)
        at = rows_of(i, QB)
        for b in range(4):
            cols = slice(b * 512, (b + 1) * 512)
            o = contract(ggp[0, at], gw[0, cols], 1, 1) + contract(gup[0, at], uw[0, cols], 1, 1)
            o = o + contract(ggp[1, at], gw[1, cols], 1, 1) + contract(gup[1, at], uw[1, cols], 1, 1)
            o = o.astype(BF)
            pg[i, 0, :, cols] = o[:SLAB]
            pg[i, 1, :, cols] = o[SLAB:]
        s.after_block(t)
        if t == 1:
            each(down, "s2")

    def gate_grad(g, carry):
        at = rows_of(g, 512)
        for j in range(2):
            gw[j, at] = contract(n2[:, at], ggp[j], 0, 0).astype(BF)
        return carry

    def up_grad(g, carry):
        at = rows_of(g, 512)
        for j in range(2):
            uw[j, at] = contract(n2[:, at], gup[j], 0, 0).astype(BF)
        return carry

    lax.fori_loop(0, 1, gate_grad, 0)
    s.finish()
    lax.fori_loop(1, 4, gate_grad, 0)
    each(gates, "s1")
    lax.fori_loop(0, 2, up_grad, 0)
    each(down, "s3")
    for cp in l_s:
        cp.wait()
    f.wait()
    for c in COLS:
        outs[:, c] = (after[:, c] + RES * f.total(c)).astype(BF)
    s.wait()
    inv = norm_scale(lambda c: after[:, c])
    total = None
    for c in COLS:
        g = s.total(c)
        scaled = after[:, c] * inv
        gs = g * scaled
        gain_part[:, c] = jnp.sum(gs.reshape(SLAB // 8, 8, 128), axis=0)
        e = gs * gain[1:2, c]
        total = e if total is None else total + e
    inner = jnp.sum(total, axis=1, keepdims=True) * (1.0 / D)
    for c in COLS:
        e = s.total(c) * gain[1:2, c]
        v = slab[:, c].astype(F32) + inv * (e - after[:, c] * inv * inner)
        after[:, c] = v
        attn[:, c] = (RES * v).astype(BF)
    a = LineGather(w, attn, attn_out)
    a.s1()
    each(gates, "s2")
    lax.fori_loop(2, 4, up_grad, 0)
    e_u = w.copy(uw, gu_out)
    each(down, "s4")
    a.s2()
    each(gates, "s3")
    each(down, "s5")
    e_out = [w.copy(after, grad_after_out), w.copy(v_down, o_down), w.copy(outs, outs_out)]
    a.s3()
    each(gates, "s4")
    a.s4()
    w.drain()
    each(gates, "s5")
    e_out.append(w.copy(v_gate, o_gate))
    e_u.wait()
    for cp in e_out:
        cp.wait()
    w.drain()


def call_second(*args):
    scratch = [
        pltpu.SemaphoreType.DMA((93,)), pltpu.SemaphoreType.DMA((61,)),
        pltpu.VMEM((T, D), BF), pltpu.VMEM((4, 2, SLAB, D), BF),
        pltpu.VMEM((2, D, 512), BF), pltpu.VMEM((2, D, 512), BF), pltpu.VMEM((2, 512, D), BF),
        pltpu.VMEM((2, T, 512), BF), pltpu.VMEM((2, T, 512), BF), pltpu.VMEM((2, T, 512), BF),
        pltpu.VMEM((2, 4, 2, 512, 256), BF),
        pltpu.VMEM((4, 2, SLAB, D), BF),
        pltpu.VMEM((SLAB, D), BF), pltpu.VMEM((SLAB, D), BF), pltpu.VMEM((SLAB, D), F32),
        pltpu.VMEM((8, D), F32), pltpu.VMEM((SLAB, D), BF),
        pltpu.VMEM((512, 256), F32), pltpu.VMEM((256, 512), F32),
    ]
    scratch += LineSum.SCRATCH * 2
    scratch += WeightSum.scratch(256, 256) * 2 + WeightSum.scratch(128, 512) * 2
    return pl.pallas_call(
        second_kernel,
        out_shape=[
            jax.ShapeDtypeStruct((4, 2, SLAB, D), BF),
            jax.ShapeDtypeStruct((SLAB, D), F32),
            jax.ShapeDtypeStruct((8, D), F32),
            jax.ShapeDtypeStruct((SLAB, D), BF),
            jax.ShapeDtypeStruct((512, 256), F32),
            jax.ShapeDtypeStruct((256, 512), F32),
            jax.ShapeDtypeStruct((2, D, 512), BF),
        ],
        in_specs=[ANY] * 8,
        out_specs=[ANY, ANY, VM, ANY, ANY, ANY, ANY],
        scratch_shapes=scratch,
        compiler_params=pltpu.CompilerParams(
            collective_id=1, has_side_effects=True, vmem_limit_bytes=62 << 20
        ),
        name="second",
    )(*args)


def key_range(i):
    return max(0, (i - 2) * QB), (i + 1) * QB


def third_kernel(
    ga_in, hid_in, grad_after_in, gain_in, gain_two_in, w2_in, o_in, n1_in, qt_in, kt_in, vt_in, ht_in,
    lse_in, cos_in, sin_in, gu_in, outs_in, segs,
    out_cols, hid_cols, o_gain, o_q, o_o, o_up,
    send, recv, ga, n1, w2, o2, ght, gt, gn, gk, gv, bias, seg_col, seg_row,
    part, got, far, near, outs, gains, gcame, gsum, gcame2, tq, to, rq, ro, gu,
    hid, grad_after, gain, gain_two, qt, kt, vt, ht, lse, cos, sin, *sc,
):
    p = Place()
    w = Wire(p, send, recv)
    rows = row_peers(p)
    lanes = [(k, (lax.rem(p.gx + k, 8), p.gy)) for k in range(1, 8)]
    peers = [dev for _, _, _, dev in rows] + [dev for _, dev in lanes] + [p.at(y=1), p.at(y=-1)]
    say_hello(peers)
    l_ga = [w.copy(ga_in, ga), w.copy(o_in, o2), w.copy(ht_in, ht)]
    l_qk = [w.copy(a, b) for a, b in ((qt_in, qt), (kt_in, kt), (vt_in, vt), (lse_in, lse), (cos_in, cos), (sin_in, sin))]
    hear_all(peers)
    big = [WeightSum(w, gu, o_up, 128 * i, 128, i, *sc[4 * i : 4 * i + 4]) for i in range(2)]
    sq = [WeightSum(w, rq, o_q, 192 * i, 192, i, *sc[8 + 4 * i : 12 + 4 * i]) for i in range(2)]
    so = [WeightSum(w, ro, o_o, 64 * i, 64, i, *sc[16 + 4 * i : 20 + 4 * i]) for i in range(2)]

    def each(group, stage):
        for b in group:
            getattr(b, stage)()

    for b in big:
        b.s1(gu_in)
    l_big = [w.copy(gu_in, gu)]
    l_n1 = w.copy(n1_in, n1)
    l_w2 = [w.copy(w2_in, w2)]
    l_s = [w.copy(a, b) for a, b in ((hid_in, hid), (grad_after_in, grad_after), (gain_in, gain), (gain_two_in, gain_two))]
    pick_segment(p, segs, seg_row, seg_col)
    gk[...] = jnp.zeros_like(gk)
    gv[...] = jnp.zeros_like(gv)
    gt[:, 192:] = jnp.zeros((2, 64, T), BF)
    for cp in l_ga:
        cp.wait()

    def heads_grad(i, carry):
        at = rows_of(i, QB)
        ght[:, :, at] = contract(o2[...], ga[at], 1, 1).astype(BF).reshape(4, HEAD, QB)
        return carry

    lax.fori_loop(0, 4, heads_grad, 0)

    def out_grad(dst, j):
        hj = ht[pl.ds(j * 2, 2)].reshape(128, T)
        for g in range(8):
            dst[g // 2, g % 2] = contract(hj, ga[:, g * 256 : (g + 1) * 256], 1, 0).astype(BF)

    out_grad(to, 1 - p.c)
    swap_o = w.send(to, ro.at[p.c], p.at(c=1))
    out_grad(ro.at[p.c], p.c)
    for cp in l_qk:
        cp.wait()
    for i in range(4):
        lo, hi = key_range(i)
        at = slice(i * QB, (i + 1) * QB)
        bias[: hi - lo] = bias_tile(seg_col, seg_row, lo, hi - lo, i)

        def head(n, carry):
            q = qt[n, :, at]
            g = ght[n, :, at]
            sc_ = contract(kt[:, lo:hi], q, 0, 0) + bias[: hi - lo]
            pr = jnp.exp(sc_ - lse[pl.ds(n, 1), at])
            gp = contract(vt[:, lo:hi], g, 0, 0)
            inner = jnp.sum(ht[n, :, at].astype(F32) * g.astype(F32), axis=0, keepdims=True)
            gs = (pr * (gp - inner)).astype(BF)
            gq = contract(kt[:, lo:hi], gs, 1, 0) * ATTN_SCALE
            a, b = gq[:32], gq[32:]
            first = pl.multiple_of(lax.rem(n, 2) * 64, 64)
            gt[n // 2, pl.ds(first, 32), at] = (a * cos[:, at] + b * sin[:, at]).astype(BF)
            gt[n // 2, pl.ds(first + 32, 32), at] = (b * cos[:, at] - a * sin[:, at]).astype(BF)
            gk[:, lo:hi] += contract(q, gs, 1, 1)
            gv[:, lo:hi] += contract(g, pr.astype(BF), 1, 1)
            return carry

        lax.fori_loop(0, 4, head, 0)
        if i == 0:
            swap_o.wait_recv()
            each(so, "s1")
            x = Scatter(w, outs_in, out_cols, rows)
            x.s1()
        if i == 1:
            for cp in l_big:
                cp.wait()
            each(big, "s2")
        if i == 2:
            each(so, "s2")
    a, b = gk[:32], gk[32:]
    gt[0, 128:160] = (a * cos[...] + b * sin[...]).astype(BF)
    gt[1, 128:160] = (b * cos[...] - a * sin[...]).astype(BF)
    gt[0, 160:192] = gv[:32].astype(BF)
    gt[1, 160:192] = gv[32:].astype(BF)
    other = 1 - p.c
    for i in range(4):
        gn[i * QB : (i + 1) * QB, :256] = gt[other, :, i * QB : (i + 1) * QB].T
        gn[i * QB : (i + 1) * QB, 256:] = gt[p.c, :, i * QB : (i + 1) * QB].T
    for cp in l_w2:
        cp.wait()
    s = LineSum(w, part, got, far, near)
    for t, k in enumerate(LineSum.ORDER):
        i = p.pos("z", k)
        at = rows_of(i, QB)
        for b in range(4):
            cols = slice(b * 512, (b + 1) * 512)
            o = contract(gn[at, :192], w2[other, cols, :192], 1, 1) + contract(gn[at, 256:448], w2[p.c, cols, :192], 1, 1)
            o = o.astype(BF)
            part[i, 0, :, cols] = o[:SLAB]
            part[i, 1, :, cols] = o[SLAB:]
        s.after_block(t)
    l_n1.wait()

    def in_grad(g, carry):
        v = contract(n1[:, rows_of(g, 512)], gn[...], 0, 0).astype(BF)
        for half in range(2):
            for dst, first in ((tq, 0), (rq.at[p.c], 256)):
                u = v[half * 256 : half * 256 + 256, first : first + 256]
                dst[g, half, :256] = u[:, :128]
                dst[g, half, 256:, :64] = u[:128, 128:192]
                dst[g, half, 256:, 64:] = u[128:, 128:192]
        return carry

    lax.fori_loop(0, 3, in_grad, 0)
    s.finish()
    lax.fori_loop(3, 4, in_grad, 0)
    swap_q = w.send(tq, rq.at[p.c], p.at(c=1))
    each(so, "s3")
    each(big, "s3")
    swap_q.wait_recv()
    each(sq, "s1")
    each(so, "s4")
    each(big, "s4")
    for cp in l_s:
        cp.wait()
    each(sq, "s2")
    s.wait()
    inv = norm_scale(lambda c: hid[:, c].astype(F32))
    total = None
    for c in COLS:
        g = s.total(c)
        scaled = hid[:, c].astype(F32) * inv
        gs = g * scaled
        gains[0, :, c] = jnp.sum(gs.reshape(SLAB // 8, 8, 128), axis=0)
        e = gs * gain[0:1, c]
        total = e if total is None else total + e
    inner = jnp.sum(total, axis=1, keepdims=True) * (1.0 / D)
    for c in COLS:
        e = s.total(c) * gain[0:1, c]
        v = grad_after[:, c] + inv * (e - hid[:, c].astype(F32) * inv * inner)
        outs[:, c] = v.astype(BF)
    gains[1] = gain_two[...]
    mine = pl.ds(pl.multiple_of(p.gy * 128, 128), 128)
    gcp = []
    for _, _, _, dev in rows:
        at = pl.ds(pl.multiple_of(dev[1] * 128, 128), 128)
        gcp.append(w.send(gains.at[:, :, at], gcame.at[p.gy], dev))
    glocal = w.copy(gains.at[:, :, mine], gcame.at[p.gy])
    each(sq, "s3")
    o = Scatter(w, outs, hid_cols, rows)
    o.s1()
    each(big, "s5")
    each(so, "s5")
    for cp in gcp:
        cp.wait_recv()
    glocal.wait()
    gsum[...] = jnp.sum(gcame[...], axis=0)
    lcp = [w.send(gsum, gcame2.at[p.gx], dev) for _, dev in lanes]
    llocal = w.copy(gsum, gcame2.at[p.gx])
    each(sq, "s4")
    for cp in lcp:
        cp.wait_recv()
    llocal.wait()
    o_gain[...] = jnp.sum(gcame2[...], axis=0)
    x.s2()
    o.s2()
    w.drain()
    each(sq, "s5")
    w.drain()


def call_third(*args):
    scratch = [
        pltpu.SemaphoreType.DMA((132,)), pltpu.SemaphoreType.DMA((112,)),
        pltpu.VMEM((T, D), BF), pltpu.VMEM((T, D), BF),
        pltpu.VMEM((2, D, 256), BF), pltpu.VMEM((256, D), BF),
        pltpu.VMEM((4, HEAD, T), BF), pltpu.VMEM((2, 256, T), BF), pltpu.VMEM((T, 512), BF),
        pltpu.VMEM((HEAD, T), F32), pltpu.VMEM((HEAD, T), F32), pltpu.VMEM((3 * QB, QB), F32),
        pltpu.VMEM((T, 1), jnp.int32), pltpu.VMEM((1, T), jnp.int32),
        pltpu.VMEM((4, 2, SLAB, D), BF),
        *LineSum.SCRATCH,
        pltpu.VMEM((SLAB, D), BF),
        pltpu.VMEM((2, 8, D), F32),
        pltpu.VMEM((16, 2, 8, 128), F32),
        pltpu.VMEM((2, 8, 128), F32),
        pltpu.VMEM((8, 2, 8, 128), F32),
        pltpu.VMEM((4, 2, 384, 128), BF),
        pltpu.VMEM((4, 2, 128, 256), BF),
        pltpu.VMEM((2, 4, 2, 384, 128), BF),
        pltpu.VMEM((2, 4, 2, 128, 256), BF),
        pltpu.VMEM((2, 4, 2, 256, 512), BF),
        pltpu.VMEM((SLAB, D), BF), pltpu.VMEM((SLAB, D), F32),
        pltpu.VMEM((8, D), F32), pltpu.VMEM((8, D), F32),
        pltpu.VMEM((4, HEAD, T), BF), pltpu.VMEM((HEAD, T), BF), pltpu.VMEM((HEAD, T), BF),
        pltpu.VMEM((4, HEAD, T), BF), pltpu.VMEM((8, T), F32),
        pltpu.VMEM((32, T), F32), pltpu.VMEM((32, T), F32),
    ]
    scratch += WeightSum.scratch(128, 512) * 2
    scratch += WeightSum.scratch(192, 128) * 2 + WeightSum.scratch(64, 256) * 2
    return pl.pallas_call(
        third_kernel,
        out_shape=[
            jax.ShapeDtypeStruct((2 * T, 128), BF),
            jax.ShapeDtypeStruct((2 * T, 128), BF),
            jax.ShapeDtypeStruct((2, 8, 128), F32),
            jax.ShapeDtypeStruct((384, 128), F32),
            jax.ShapeDtypeStruct((128, 256), F32),
            jax.ShapeDtypeStruct((256, 512), F32),
        ],
        in_specs=[ANY] * 17 + [VM],
        out_specs=[ANY, ANY, VM, VM, VM, VM],
        scratch_shapes=scratch,
        compiler_params=pltpu.CompilerParams(
            collective_id=2, has_side_effects=True, vmem_limit_bytes=62 << 20
        ),
        name="third",
    )(*args)


def outputs_kernel(
    a_cols, a_hid, a_gains, a_qkv, a_o, a_gate, a_up, a_down,
    x_cols, x_hid, x_gain, x_q, x_k, x_v, x_o, x_gain2, x_gate, x_up, x_down,
    sem, cols, hid, gains, qkv,
):
    first = [
        pltpu.make_async_copy(a, b, sem.at[i])
        for i, (a, b) in enumerate(
            ((a_cols, cols), (a_hid, hid), (a_gains, gains), (a_qkv, qkv), (a_o, x_o), (a_gate, x_gate), (a_up, x_up), (a_down, x_down))
        )
    ]
    for cp in first:
        cp.start()
    first[0].wait()
    x_cols[...] = cols[...].astype(F32)
    first[1].wait()
    x_hid[...] = hid[...].astype(F32)
    first[2].wait()
    x_gain[...] = jnp.sum(gains[0], axis=0, keepdims=True)
    x_gain2[...] = jnp.sum(gains[1], axis=0, keepdims=True)
    first[3].wait()
    x_q[...] = qkv[:256]
    kv = qkv[256:].T
    x_k[:, :128] = kv[:32]
    x_k[:, 128:] = kv[64:96]
    x_v[:, :128] = kv[32:64]
    x_v[:, 128:] = kv[96:]
    for cp in first[4:]:
        cp.wait()


def call_outputs(*args):
    shapes = [
        (2 * T, 128), (2 * T, 128), (1, 128), (256, 128), (32, 256), (32, 256), (128, 256), (1, 128),
        (256, 512), (256, 512), (512, 256),
    ]
    return pl.pallas_call(
        outputs_kernel,
        out_shape=[jax.ShapeDtypeStruct(v, F32) for v in shapes],
        in_specs=[ANY] * 8,
        out_specs=[VM] * 11,
        scratch_shapes=[
            pltpu.SemaphoreType.DMA((8,)),
            pltpu.VMEM((2 * T, 128), BF), pltpu.VMEM((2 * T, 128), BF),
            pltpu.VMEM((2, 8, 128), F32), pltpu.VMEM((384, 128), F32),
        ],
        compiler_params=pltpu.CompilerParams(vmem_limit_bytes=62 << 20),
        name="outputs",
    )(*args)


def per_device(
    hidden, attn_gain, wq, wk, wv, wo, ffn_gain, gate, up, down, segments, cotangent,
):
    freq = (ROPE_BASE ** (-np.arange(0, HEAD, 2, dtype=np.float32) / HEAD)).astype(np.float32)[:, None]
    (
        cot, gg, uu, dd, w2, o2, n1, hid_slab, qt, kt, vt, ht, lse, after, n2, act, gain, cos, sin
    ) = call_first(
        hidden, cotangent, gate, up, down, wo, wq, wk.T, wv.T, attn_gain[None], ffn_gain[None], segments, freq
    )
    grad_attn, grad_after, gain_two, outs, o_down, o_gate, g_up = call_second(
        n2.reshape(T, D), cot, gg.reshape(2, D, 512), uu.reshape(2, D, 512),
        dd.reshape(2, 8, 512, 256), after, gain, act,
    )
    out_cols, hid_cols, o_gain, o_qkv, o_o, o_up = call_third(
        grad_attn.reshape(T, D), hid_slab, grad_after, gain, gain_two, w2, o2, n1,
        qt, kt, vt, ht, lse, cos, sin, g_up.reshape(2, 4, 2, 256, 512), outs, segments,
    )
    res = call_outputs(out_cols, hid_cols, o_gain, o_qkv, o_o, o_gate, o_up, o_down)
    return (
        res[0], res[1], res[2].reshape(128), res[3], res[4].T, res[5].T, res[6], res[7].reshape(128), *res[8:],
    )


def solution(mesh):
    wide, cols, tall = P("gx", "gy"), P("gy"), P("gy", "gx")
    return jax.shard_map(
        per_device,
        mesh=mesh,
        in_specs=(wide, cols, wide, wide, wide, tall, cols, wide, wide, tall, P("gx", None), wide),
        out_specs=(wide, wide, cols, wide, wide, wide, tall, cols, wide, wide, tall),
        check_vma=False,
    )
```
